32 devices in a mesh: groups: 2 (over y), mem: 8 (over z, x), lat: 2 (over core).
Axes of the slice: x: 2, y: 2, z: 4, core: 2. Of those that a mesh axis runs over, the one named last changes fastest.
Arguments:
- state: bfloat16 [64, 8, 64, 512], P(('groups', 'mem'), None, 'lat'), parts along dimension 0, may hold values from -6 to 6
- counts: int32 [16], P(('groups', 'mem')), parts along dimension 0, may hold values from 1 to 4, 16 in all
- east_wind: float32 [128, 512], P(('groups', 'lat')), parts along dimension 0, may hold values from -0.48 to 0.48
- north_wind: float32 [128, 512], P(('groups', 'lat')), parts along dimension 0, may hold values from -0.48 to 0.48
- obs_cells: int32 [4, 32768], P(('groups', 'lat')), parts along dimension 0, may hold values from 0 to 16383
- obs_mask: int32 [4, 32768], P(('groups', 'lat')), parts along dimension 0, may hold values 0 or 1
- obs_values: float32 [4, 32768], P(('groups', 'lat')), parts along dimension 0, may hold values from -6 to 6
- obs_error: float32 [4, 32768], P(('groups', 'lat')), parts along dimension 0, may hold values from 0.2 to 2
- relax: float32 [8], replicated, may hold values from 0.3 to 0.9
Outputs:
- new_state: bfloat16 [64, 8, 64, 512], P(('groups', 'mem'), None, 'lat'), parts along dimension 0
- analysis_mean: bfloat16 [16, 64, 512], P('groups', 'lat'), parts along dimension 0
The draws below stay inside these ranges and needn't reach their ends.
There are 2 independent parts, one for each index of `groups`. The reference program is written for one: setup_inputs(seed, part) draws one part's arguments, and reference() takes and returns one part's arrays. A program takes and returns all parts, laid end to end along the dimension named above; an argument that names none is the same for every part. Nothing has to cross between parts.
Inputs may be any that keep to these rules, and one draw needn't show every extreme that they name: counts over the mem axis add up to 16, and some mem index holds 4 members.
All inputs are finite; a program needn't handle non-finite values. No bound on the sum of `counts` or of `obs_mask` on one device may be relied on, other than what follows from the above.
Results may differ from the reference program's by a relative error of at most 0.001.
The reference program's roundings to bfloat16 on the way (of `advected`) count: a program that leaves them out, or rounds other values in their place, can miss the bound.
Values may be sent and summed in bfloat16 or wider, within the bound.
A program may use at most 128 MiB of HBM per device.

```python
import math
import jax
import jax.numpy as jnp
import numpy as np
from jax import lax

FIELDS = 8
NLON = 512
ROWS = 32
STEPS = 4
SMOOTH = 16
OBS_BAND = 32768
SLOTS = 4
MEMBERS = 16
NLAT = 64
N_MEM = 8
N_LAT = 2


def plant(values, own_key, low, top_value):
    shape = values.shape
    spot = [jax.random.randint(jax.random.fold_in(own_key, axis), (), 0, shape[axis]) for axis in range(len(shape))]
    values = values.at[tuple(spot)].set(low)
    longest = shape.index(max(shape))
    spot[longest] = (spot[longest] + 1) % shape[longest]
    return values.at[tuple(spot)].set(top_value)


def block_levels(key, dims, pieces, low, top_value):
    gain = 1.0
    for position, shards_of in pieces:
        heights = jax.random.uniform(jax.random.fold_in(jax.random.fold_in(key, 6), position), (shards_of,), jnp.float32, low / len(pieces), top_value / len(pieces))
        gain = gain * jnp.repeat(jnp.exp(heights), dims[position] // shards_of).reshape((-1,) + (1,) * (len(dims) - 1 - position))
    return gain


def split_up(number_of, total, most, lean):
    weights = [(1 << 20) // math.isqrt(grade ** lean) + 1 for grade in range(2, number_of + 1)]
    rest, given = total - most - (number_of - 1), [1] * (number_of - 1)
    while rest > 0:
        free = [i for i in range(number_of - 1) if given[i] < most]
        mass, budget = sum([weights[i] for i in free]), rest
        for i in free:
            extra = min(most - given[i], max(1, budget * weights[i] // mass), rest)
            given[i] = given[i] + extra
            rest = rest - extra
    return np.array([most] + given)


def ragged(rng, count, total, bound, slope):
    if count == 2:
        one = jax.random.randint(rng, (), max(1, total - bound), min(bound, total - 1) + 1)
        return jnp.stack([one, total - one])
    tallies = jnp.asarray(split_up(count, total, bound, slope), jnp.int32)
    couples = (count - 1) // 2
    giver, taker = tallies[1:1 + 2 * couples:2], tallies[2:2 + 2 * couples:2]
    slack = jnp.minimum(giver - 1, bound - taker)
    shifted = jax.random.randint(jax.random.fold_in(rng, 1), (couples,), 0, 1 << 20) % (slack + 1)
    tallies = tallies.at[1:1 + 2 * couples:2].set(giver - shifted).at[2:2 + 2 * couples:2].set(taker + shifted)
    return tallies[jax.random.permutation(jax.random.fold_in(rng, 2), count)]


def noise(stream_key, shape, width, limit, pieces=(), held_as=jnp.bfloat16):
    gain = block_levels(stream_key, shape, pieces, -0.22, 0.18) if pieces else 1.0
    values = jax.random.normal(stream_key, shape, jnp.float32) * width * gain
    return jnp.minimum(jnp.maximum(values, -limit), limit).astype(held_as)


def setup_inputs(seed: int = 0, part: int = 0) -> dict:
    seeds = jax.random.split(jax.random.key(seed), 10)
    own_keys = jax.random.split(jax.random.fold_in(seeds[9], part), 10)
    return {
        "state": noise(own_keys[0], (N_MEM * SLOTS, FIELDS, NLAT, NLON), 1.0, 6.0, ((0, 8), (2, 2))),
        "counts": ragged(own_keys[1], N_MEM, MEMBERS, SLOTS, 2).astype(jnp.int32),
        "east_wind": jnp.clip(jax.random.uniform(own_keys[2], (NLAT, NLON), jnp.float32, -0.48, 0.48) * block_levels(own_keys[2], (NLAT, NLON), ((0, 2),), -0.4, 0.0), -0.48, 0.48),
        "north_wind": jnp.clip(jax.random.uniform(own_keys[3], (NLAT, NLON), jnp.float32, -0.48, 0.48) * block_levels(own_keys[3], (NLAT, NLON), ((0, 2),), -0.4, 0.0), -0.48, 0.48),
        "obs_cells": plant(jax.random.randint(own_keys[4], (N_LAT, OBS_BAND), 0, ROWS * NLON), jax.random.fold_in(own_keys[4], 1), 0, (ROWS * NLON) - 1).astype(jnp.int32),
        "obs_mask": plant((jax.random.randint(own_keys[5], (N_LAT, OBS_BAND), 0, 4) < 3).astype(jnp.int32), jax.random.fold_in(own_keys[5], 1), 0, 1),
        "obs_values": noise(own_keys[6], (N_LAT, OBS_BAND), 1.0, 6.0, ((0, 2),), jnp.float32),
        "obs_error": jnp.clip(jnp.exp(math.log(2.0) - 2.3025851 * jax.random.uniform(own_keys[7], (N_LAT, OBS_BAND), jnp.float32) ** block_levels(own_keys[7], (N_LAT, OBS_BAND), ((0, 2),), -0.2, 0.2)), 0.2, 2.0),
        "relax": jnp.clip(jax.random.uniform(seeds[8], (FIELDS,), jnp.float32, 0.3, 0.9), 0.3, 0.9),
    }


LOG_TWO_PI = 1.8378770664093453


def advance(field, east_wind, north_wind):
    centre = field[..., 1:-1, :]
    south_row = field[..., :-2, :]
    north_row = field[..., 2:, :]
    west_cell = jnp.roll(centre, 1, axis=-1)
    east_cell = jnp.roll(centre, -1, axis=-1)
    return (centre - jnp.maximum(east_wind, 0.0) * (centre - west_cell)
            - jnp.minimum(east_wind, 0.0) * (east_cell - centre)
            - jnp.maximum(north_wind, 0.0) * (centre - south_row)
            - jnp.minimum(north_wind, 0.0) * (north_row - centre))


def kernel_matrix(count, reach, periodic):
    index = jnp.arange(count, dtype=jnp.int32)
    offset = jnp.abs(index[:, None] - index[None, :])
    if periodic:
        offset = jnp.minimum(offset, count - offset)
    values = jnp.exp(-(2.0 * offset.astype(jnp.float32) / reach) ** 2)
    return jnp.where(offset <= reach, values, 0.0).astype(jnp.float32)


def band_grids(cells, mask, values, error, count):
    used = mask.astype(jnp.float32)
    inverse = used / (error * error)
    terms = jnp.stack([inverse, inverse * values,
                       inverse * values * values + used * (2.0 * jnp.log(error) + LOG_TWO_PI)])
    return jax.vmap(lambda column: jax.ops.segment_sum(column, cells, num_segments=count))(terms)


def reference(state, counts, east_wind, north_wind, obs_cells, obs_mask, obs_values, obs_error, relax):
    live = (jnp.arange(SLOTS, dtype=jnp.int32)[None, :] < counts[:, None]).reshape(-1)
    grids = jax.vmap(lambda a, b, c, d: band_grids(a, b, c, d, ROWS * NLON))(obs_cells, obs_mask, obs_values, obs_error)
    grids = grids.reshape(N_LAT, 3, ROWS, NLON).transpose(1, 0, 2, 3).reshape(3, NLAT, NLON)
    lat_kernel = kernel_matrix(NLAT, SMOOTH, False)
    lon_kernel = kernel_matrix(NLON, SMOOTH, True)

    def visit(carry, item):
        peak, total, weighted = carry
        member, alive = item
        field = member.astype(jnp.float32)
        for step in range(STEPS):
            padded = jnp.pad(field, ((0, 0), (1, 1), (0, 0)))
            field = advance(padded, east_wind, north_wind)
        advected = field.astype(jnp.bfloat16)
        value = advected[0].astype(jnp.float32)
        loglik = -0.5 * (grids[0] * value * value - 2.0 * grids[1] * value + grids[2])
        smoothed = jnp.dot(lat_kernel, loglik, precision=lax.Precision.HIGHEST, preferred_element_type=jnp.float32)
        scores = jnp.dot(smoothed, lon_kernel, precision=lax.Precision.HIGHEST, preferred_element_type=jnp.float32)
        new_peak = jnp.where(alive, jnp.maximum(peak, scores), peak)
        factor = jnp.exp(peak - new_peak)
        gains = jnp.where(alive, jnp.exp(scores - new_peak), 0.0)
        total = total * factor + gains
        weighted = weighted * factor[None] + gains[None] * advected.astype(jnp.float32)
        return (new_peak, total, weighted), advected

    start = (jnp.full((NLAT, NLON), -jnp.inf, jnp.float32), jnp.zeros((NLAT, NLON), jnp.float32),
             jnp.zeros((FIELDS, NLAT, NLON), jnp.float32))
    (peak, total, weighted), advected_all = lax.scan(visit, start, (state, live))
    merged = weighted / total[None]

    def relax_member(item):
        advected, alive = item
        values = advected.astype(jnp.float32)
        fresh = values + relax[:, None, None] * (merged - values)
        return jnp.where(alive, fresh, 0.0).astype(jnp.bfloat16)

    new_state = lax.map(relax_member, (advected_all, live))
    return new_state, merged.astype(jnp.bfloat16)
```

```python
import functools

import jax
import jax.numpy as jnp
from jax import lax
from jax.experimental import pallas as pl
from jax.experimental.pallas import tpu as pltpu
from jax.sharding import PartitionSpec as P

STEPS = 4
SMOOTH = 16
LOG_TWO_PI = 1.8378770664093453
MESH = pl.DeviceIdType.MESH
TILE_ROWS = 16
TILE_COLS = 128
OBS_BLOCK = 2048


def pieces(values):
    high = values.astype(jnp.bfloat16).astype(jnp.float32)
    rest = values - high
    mid = rest.astype(jnp.bfloat16).astype(jnp.float32)
    return high, mid, rest - mid


def partial_grids(rows, width, cells, mask, values, error):
    count = cells.shape[1]
    used = mask.astype(jnp.float32)
    inverse = used / (error * error)
    terms = (
        inverse,
        inverse * values,
        inverse * values * values + used * (2.0 * jnp.log(error) + LOG_TWO_PI),
    )
    row = cells // width
    column = cells - row * width
    row_hit = lax.broadcasted_iota(jnp.int32, (rows, count), 0) == row
    column_hit = jnp.where(
        lax.broadcasted_iota(jnp.int32, (width, count), 0) == column, 1.0, 0.0
    ).astype(jnp.bfloat16)
    left = jnp.concatenate(
        [
            jnp.where(row_hit, piece, 0.0).astype(jnp.bfloat16)
            for term in terms
            for piece in pieces(term)
        ],
        axis=0,
    )
    return lax.dot_general(
        left, column_hit, (((1,), (1,)), ((), ())), preferred_element_type=jnp.float32
    )


def kernel_values(offset):
    values = jnp.exp(-((2.0 * offset.astype(jnp.float32) / SMOOTH) ** 2))
    return jnp.where(jnp.abs(offset) <= SMOOTH, values, 0.0)


def cycle_kernel(
    n,
    state_ref,
    counts_ref,
    east_ref,
    north_ref,
    cells_ref,
    mask_ref,
    values_ref,
    error_ref,
    relax_ref,
    out_ref,
    mean_ref,
    cells,
    mask,
    values,
    error,
    state,
    counted,
    obs_send,
    obs_recv,
    grids,
    halo,
    wind_in,
    wind_halo,
    winds,
    advected,
    lon_kernel,
    loglik,
    loglik_halo,
    scores,
    send,
    recv,
    pair,
    merged,
    halo_sems,
    send_sems,
    recv_sems,
    back_send,
    back_recv,
    relay_send,
    local_sems,
    obs_sems,
    obs_arrived,
    grid_sems,
    grid_arrived,
):
    slots, fields, rows, width = state_ref.shape
    across = width // TILE_COLS
    owners = (rows // TILE_ROWS) * across
    me = lax.axis_index("mem")
    band = lax.axis_index("lat")
    other = 1 - band

    share = cells.shape[1]
    mine = pl.ds(pl.multiple_of(me * share, 128), share)
    loads = [
        pltpu.make_async_copy(source, target, local_sems.at[k])
        for k, (source, target) in enumerate(
            (
                (cells_ref.at[:, mine], cells),
                (mask_ref.at[:, mine], mask),
                (values_ref.at[:, mine], values),
                (error_ref.at[:, mine], error),
                (state_ref, state),
            )
        )
    ]
    for load in loads:
        load.start()

    barrier = pltpu.get_barrier_semaphore()

    def greet(d, carry):
        pl.semaphore_signal(
            barrier, inc=1, device_id={"mem": lax.rem(me + d, n)}, device_id_type=MESH
        )
        return carry

    pl.semaphore_signal(barrier, inc=1, device_id={"lat": other}, device_id_type=MESH)
    lax.fori_loop(1, n, greet, 0)

    wind_in[0] = east_ref[...]
    wind_in[1] = north_ref[...]
    i0 = lax.broadcasted_iota(jnp.int32, (width, width), 0)
    i1 = lax.broadcasted_iota(jnp.int32, (width, width), 1)
    apart = jnp.abs(i0 - i1)
    lon_kernel[...] = kernel_values(jnp.minimum(apart, width - apart))

    pl.semaphore_wait(barrier, n)

    def to_other(source, target, slot):
        copy = pltpu.make_async_remote_copy(
            src_ref=source,
            dst_ref=target,
            send_sem=halo_sems.at[0, slot],
            recv_sem=halo_sems.at[1, slot],
            device_id={"lat": other},
            device_id_type=MESH,
        )
        copy.start()
        return copy

    edge16 = pl.ds(pl.multiple_of(other * (rows - 16), 16), 16)
    edge8 = pl.ds(pl.multiple_of(other * (rows - 8), 8), 8)
    copy_winds = to_other(wind_in.at[:, edge8, :], wind_halo, 0)
    copy_state = to_other(state_ref.at[:, :, edge16, :], halo, 1)

    def tile(t):
        down = t // across
        return (
            pl.ds(pl.multiple_of(down * TILE_ROWS, TILE_ROWS), TILE_ROWS),
            pl.ds(pl.multiple_of((t - down * across) * TILE_COLS, TILE_COLS), TILE_COLS),
        )

    for load in loads[:4]:
        load.wait()
    block = min(share, OBS_BLOCK)
    for start in range(0, share, block):
        part = partial_grids(
            rows, width, *(ref[:, start : start + block] for ref in (cells, mask, values, error))
        )
        for term in range(3):
            base = 3 * term * rows
            terms = (
                part[base : base + rows]
                + part[base + rows : base + 2 * rows]
                + part[base + 2 * rows : base + 3 * rows]
            )
            if start == 0:
                counted[term] = terms
            else:
                counted[term] += terms

    def obs_out(t):
        return pltpu.make_async_remote_copy(
            src_ref=obs_send.at[t],
            dst_ref=obs_recv.at[me],
            send_sem=obs_sems.at[t],
            recv_sem=obs_arrived.at[me],
            device_id={"mem": t},
            device_id_type=MESH,
        )

    def give(j, carry):
        t = lax.rem(me + 1 + j, owners)
        down, along = tile(t)
        for term in range(3):
            obs_send[t, term] = counted[term, down, along]

        @pl.when(t != me)
        def _():
            obs_out(t).start()

        return carry

    lax.fori_loop(0, owners, give, 0)

    def grid_out(d):
        return pltpu.make_async_remote_copy(
            src_ref=grids.at[me],
            dst_ref=grids.at[me],
            send_sem=grid_sems.at[d],
            recv_sem=grid_arrived.at[me],
            device_id={"mem": lax.rem(me + d, n)},
            device_id_type=MESH,
        )

    near = lax.broadcasted_iota(jnp.int32, (8, width), 0)
    keep = jnp.where(band == 0, near, 7 - near) < STEPS

    copy_winds.wait()
    for kind in range(2):
        own = wind_in[kind]
        far = jnp.where(keep, wind_halo[kind], 0.0)
        whole = jnp.concatenate([own, far], axis=0)
        winds[2 * kind] = jnp.abs(whole)
        winds[2 * kind + 1] = whole
    loads[4].wait()
    copy_state.wait()

    def move(index, carry):
        kind = index // slots
        slot = lax.rem(index, slots)
        own = state[slot, kind].astype(jnp.float32)
        far = halo[slot, kind].astype(jnp.float32)
        far = jnp.where(band == 0, far[:8], far[8:])
        far = jnp.where(keep, far, 0.0)
        x = jnp.concatenate([own, far], axis=0)
        for _ in range(STEPS):
            west = pltpu.roll(x, 1, 1)
            east = pltpu.roll(x, width - 1, 1)
            south = pltpu.roll(x, 1, 0)
            north = pltpu.roll(x, rows + 7, 0)
            x = (
                x
                - winds[0] * (x - jnp.where(winds[1] > 0.0, west, east))
                - winds[2] * (x - jnp.where(winds[3] > 0.0, south, north))
            )
        advected[slot, kind] = x[:rows].astype(jnp.bfloat16)
        return carry

    total = slots * fields
    early, late = 3 * total // 8, 6 * total // 8
    lax.fori_loop(0, early, move, 0)

    @pl.when(me < owners)
    def _():
        def arrive(d, carry):
            source = lax.rem(me + n - d, n)
            pltpu.make_async_remote_copy(
                src_ref=obs_send.at[0],
                dst_ref=obs_recv.at[source],
                send_sem=obs_sems.at[0],
                recv_sem=obs_arrived.at[source],
                device_id={"mem": source},
                device_id_type=MESH,
            ).wait_recv()
            return carry

        lax.fori_loop(1, n, arrive, 0)
        obs_recv[me] = obs_send[me]
        grids[me] = lax.fori_loop(1, n, lambda d, sums: sums + obs_recv[d], obs_recv[0])

        def start(d, carry):
            grid_out(d).start()
            return carry

        lax.fori_loop(1, n, start, 0)

    lax.fori_loop(early, late, move, 0)

    def likely(t, carry):
        @pl.when(t != me)
        def _():
            pltpu.make_async_remote_copy(
                src_ref=grids.at[t],
                dst_ref=grids.at[t],
                send_sem=grid_sems.at[0],
                recv_sem=grid_arrived.at[t],
                device_id={"mem": t},
                device_id_type=MESH,
            ).wait_recv()

        down, along = tile(t)
        for slot in range(slots):
            value = advected[slot, 0, down, along].astype(jnp.float32)
            loglik[slot, down, along] = -0.5 * (
                grids[t, 0] * value * value - 2.0 * grids[t, 1] * value + grids[t, 2]
            )
        return carry

    lax.fori_loop(0, owners, likely, 0)
    copy_loglik = to_other(loglik.at[:, edge16, :], loglik_halo, 2)
    lax.fori_loop(late, total, move, 0)

    r0 = lax.broadcasted_iota(jnp.int32, (rows, rows), 0)
    r1 = lax.broadcasted_iota(jnp.int32, (rows, rows), 1)
    own_band = kernel_values(r0 - r1)
    h0 = lax.broadcasted_iota(jnp.int32, (rows, 16), 0)
    h1 = lax.broadcasted_iota(jnp.int32, (rows, 16), 1)
    far_band = kernel_values(jnp.where(band == 0, rows + h1 - h0, h0 + 16 - h1))
    dot = functools.partial(
        jnp.dot, precision=lax.Precision.HIGHEST, preferred_element_type=jnp.float32
    )
    copy_loglik.wait()
    smoothed = jnp.concatenate(
        [
            dot(own_band, loglik[slot]) + dot(far_band, loglik_halo[slot])
            for slot in range(slots)
        ],
        axis=0,
    )
    scores[...] = dot(smoothed, lon_kernel[...]).reshape(slots, rows, width)

    partner = me + 1 - 2 * lax.rem(me, 2)
    parity = lax.rem(me, 2)

    def outgoing(t):
        return pltpu.make_async_remote_copy(
            src_ref=send.at[t],
            dst_ref=recv.at[me // 2],
            send_sem=send_sems.at[t],
            recv_sem=recv_sems.at[me // 2],
            device_id={"mem": t},
            device_id_type=MESH,
        )

    def across_pair(t):
        return pltpu.make_async_remote_copy(
            src_ref=send.at[t],
            dst_ref=pair.at[t // 2],
            send_sem=send_sems.at[t],
            recv_sem=recv_sems.at[n // 2 + t // 2],
            device_id={"mem": partner},
            device_id_type=MESH,
        )

    def gather(t):
        down, along = tile(t)
        live = [
            jnp.where(slot < counts_ref[0], scores[slot, down, along], -jnp.inf)
            for slot in range(slots)
        ]
        peak = functools.reduce(jnp.maximum, live)
        gains = [jnp.exp(score - peak) for score in live]
        send[t, fields] = functools.reduce(jnp.add, gains)
        send[t, fields + 1] = peak
        for kind in range(fields):
            send[t, kind] = functools.reduce(
                jnp.add,
                [
                    gains[slot] * advected[slot, kind, down, along].astype(jnp.float32)
                    for slot in range(slots)
                ],
            )

    def give_pair(j, carry):
        t = lax.rem(partner + 4 + 2 * j, owners)
        gather(t)
        across_pair(t).start()
        return carry

    def give_owner(j, carry):
        t = lax.rem(me + 4 + 2 * j, owners)
        across_pair(t).wait_recv()
        low = send[t, fields + 1]
        high = pair[t // 2, fields + 1]
        peak = jnp.maximum(low, high)
        low = jnp.exp(low - peak)
        high = jnp.exp(high - peak)
        for kind in range(fields + 1):
            send[t, kind] = low * send[t, kind] + high * pair[t // 2, kind]
        send[t, fields + 1] = peak

        @pl.when(t != me)
        def _():
            outgoing(t).start()

        return carry

    def keep_own(j, carry):
        gather(2 * j + parity)
        return carry

    lax.fori_loop(0, owners // 2, give_pair, 0)
    lax.fori_loop(0, owners // 2, keep_own, 0)
    lax.fori_loop(0, owners // 2, give_owner, 0)

    def back(d):
        return pltpu.make_async_remote_copy(
            src_ref=merged.at[me],
            dst_ref=merged.at[me],
            send_sem=back_send.at[d],
            recv_sem=back_recv.at[me],
            device_id={"mem": lax.rem(me + 2 * d, n)},
            device_id_type=MESH,
        )

    def relay(t):
        return pltpu.make_async_remote_copy(
            src_ref=merged.at[t],
            dst_ref=merged.at[t],
            send_sem=relay_send.at[t],
            recv_sem=back_recv.at[t],
            device_id={"mem": partner},
            device_id_type=MESH,
        )

    @pl.when(me < owners)
    def _():
        def arrive(d, carry):
            source = lax.rem(me + 2 * d, n)
            pltpu.make_async_remote_copy(
                src_ref=send.at[0],
                dst_ref=recv.at[source // 2],
                send_sem=send_sems.at[0],
                recv_sem=recv_sems.at[source // 2],
                device_id={"mem": source},
                device_id_type=MESH,
            ).wait_recv()
            return carry

        lax.fori_loop(1, n // 2, arrive, 0)
        recv[me // 2] = send[me]
        peak = lax.fori_loop(
            1,
            n // 2,
            lambda d, top: jnp.maximum(top, recv[d, fields + 1]),
            recv[0, fields + 1],
        )

        def add(d, sums):
            factor = jnp.exp(recv[d, fields + 1] - peak)
            return tuple(sums[k] + factor * recv[d, k] for k in range(fields + 1))

        zero = jnp.zeros((TILE_ROWS, TILE_COLS), jnp.float32)
        sums = lax.fori_loop(0, n // 2, add, (zero,) * (fields + 1))
        for kind in range(fields):
            merged[me, kind] = sums[kind] / sums[fields]

        def start(d, carry):
            back(d).start()
            return carry

        lax.fori_loop(1, n // 2, start, 0)

    def landed(t):
        @pl.when(t != me)
        def _():
            relay(t).wait_recv()

    def pass_on(j, carry):
        t = lax.rem(me + owners - 2 * j, owners)
        landed(t)
        relay(t).start()
        finish(t)
        return carry

    def accept(j, carry):
        t = lax.rem(partner + owners - 2 * j, owners)
        landed(t)
        finish(t)
        return carry

    def finish(t):
        down, along = tile(t)
        for kind in range(fields):
            mean = merged[t, kind]
            mean_ref[kind, down, along] = mean.astype(jnp.bfloat16)
            for slot in range(slots):
                value = advected[slot, kind, down, along].astype(jnp.float32)
                fresh = value + relax_ref[kind] * (mean - value)
                out_ref[slot, kind, down, along] = jnp.where(
                    slot < counts_ref[0], fresh, 0.0
                ).astype(jnp.bfloat16)

    lax.fori_loop(0, owners // 2, pass_on, 0)
    lax.fori_loop(0, owners // 2, accept, 0)

    def sent(t, carry):
        @pl.when(t != me)
        def _():
            obs_out(t).wait_send()

        return carry

    lax.fori_loop(0, owners, sent, 0)

    def passed(j, carry):
        across_pair(2 * j + 1 - parity).wait_send()

        @pl.when(2 * j + parity != me)
        def _():
            outgoing(2 * j + parity).wait_send()

        relay(2 * j + parity).wait_send()
        return carry

    lax.fori_loop(0, owners // 2, passed, 0)

    @pl.when(me < owners)
    def _():
        def sent_back(d, carry):
            back(d).wait_send()
            return carry

        lax.fori_loop(1, n // 2, sent_back, 0)

        def sent_grids(d, carry):
            grid_out(d).wait_send()
            return carry

        lax.fori_loop(1, n, sent_grids, 0)


def cycle(n, state, counts, east_wind, north_wind, obs, relax):
    slots, fields, rows, width = state.shape
    owners = (rows // TILE_ROWS) * (width // TILE_COLS)
    share = obs[0].shape[1] // n
    tile = (TILE_ROWS, TILE_COLS)
    hbm = pl.BlockSpec(memory_space=pl.ANY)
    vmem = pl.BlockSpec(memory_space=pltpu.VMEM)
    smem = pl.BlockSpec(memory_space=pltpu.SMEM)
    f32, bf16 = jnp.float32, jnp.bfloat16
    return pl.pallas_call(
        functools.partial(cycle_kernel, n),
        out_shape=(
            pltpu.VMEM(state.shape, bf16),
            pltpu.VMEM((fields, rows, width), bf16),
        ),
        in_specs=[hbm, smem, vmem, vmem, hbm, hbm, hbm, hbm, smem],
        out_specs=(vmem, vmem),
        scratch_shapes=[
            pltpu.VMEM((1, share), jnp.int32),
            pltpu.VMEM((1, share), jnp.int32),
            pltpu.VMEM((1, share), f32),
            pltpu.VMEM((1, share), f32),
            pltpu.VMEM(state.shape, bf16),
            pltpu.VMEM((3, rows, width), f32),
            pltpu.VMEM((owners, 3) + tile, f32),
            pltpu.VMEM((n, 3) + tile, f32),
            pltpu.VMEM((owners, 3) + tile, f32),
            pltpu.VMEM((slots, fields, 16, width), bf16),
            pltpu.VMEM((2, rows, width), f32),
            pltpu.VMEM((2, 8, width), f32),
            pltpu.VMEM((4, rows + 8, width), f32),
            pltpu.VMEM((slots, fields, rows, width), bf16),
            pltpu.VMEM((width, width), f32),
            pltpu.VMEM((slots, rows, width), f32),
            pltpu.VMEM((slots, 16, width), f32),
            pltpu.VMEM((slots, rows, width), f32),
            pltpu.VMEM((owners, fields + 2, TILE_ROWS, TILE_COLS), f32),
            pltpu.VMEM((n // 2, fields + 2, TILE_ROWS, TILE_COLS), f32),
            pltpu.VMEM((owners // 2, fields + 2, TILE_ROWS, TILE_COLS), f32),
            pltpu.VMEM((owners, fields, TILE_ROWS, TILE_COLS), f32),
            pltpu.SemaphoreType.DMA((2, 3)),
            pltpu.SemaphoreType.DMA((owners,)),
            pltpu.SemaphoreType.DMA((n,)),
            pltpu.SemaphoreType.DMA((n,)),
            pltpu.SemaphoreType.DMA((owners,)),
            pltpu.SemaphoreType.DMA((owners,)),
            pltpu.SemaphoreType.DMA((5,)),
            pltpu.SemaphoreType.DMA((owners,)),
            pltpu.SemaphoreType.DMA((n,)),
            pltpu.SemaphoreType.DMA((n,)),
            pltpu.SemaphoreType.DMA((owners,)),
        ],
        compiler_params=pltpu.CompilerParams(
            collective_id=0, has_side_effects=True, vmem_limit_bytes=56 * 1024 * 1024
        ),
    )(state, counts, east_wind, north_wind, *obs, relax)


def write_kernel(fresh, mean, out, mean_out, sems):
    copies = [
        pltpu.make_async_copy(fresh, out, sems.at[0]),
        pltpu.make_async_copy(mean, mean_out, sems.at[1]),
    ]
    for copy in copies:
        copy.start()
    for copy in copies:
        copy.wait()


def write_out(fresh, mean):
    hbm = pl.BlockSpec(memory_space=pl.ANY)
    return pl.pallas_call(
        write_kernel,
        out_shape=(
            jax.ShapeDtypeStruct(fresh.shape, fresh.dtype),
            jax.ShapeDtypeStruct(mean.shape, mean.dtype),
        ),
        in_specs=[hbm, hbm],
        out_specs=(hbm, hbm),
        scratch_shapes=[pltpu.SemaphoreType.DMA((2,))],
    )(*(pltpu.with_memory_space_constraint(x, pltpu.VMEM) for x in (fresh, mean)))


def on_device(
    n, state, counts, east_wind, north_wind, obs_cells, obs_mask, obs_values, obs_error, relax
):
    obs = (obs_cells, obs_mask, obs_values, obs_error)
    fresh, mean = cycle(n, state, counts, east_wind, north_wind, obs, relax)
    return write_out(fresh, mean)


def solution(mesh):
    return jax.shard_map(
        functools.partial(on_device, mesh.shape["mem"]),
        mesh=mesh,
        in_specs=(
            P(("groups", "mem"), None, "lat", None),
            P(("groups", "mem")),
            P(("groups", "lat"), None),
            P(("groups", "lat"), None),
            P(("groups", "lat"), None),
            P(("groups", "lat"), None),
            P(("groups", "lat"), None),
            P(("groups", "lat"), None),
            P(),
        ),
        out_specs=(P(("groups", "mem"), None, "lat", None), P("groups", "lat", None)),
        check_vma=False,
    )
```

```python
import functools
import math

import jax
import jax.numpy as jnp
from jax import lax
from jax.experimental import pallas as pl
from jax.experimental.pallas import tpu as pltpu
from jax.sharding import PartitionSpec as P

STEPS = 4
SMOOTH = 16
LOG_TWO_PI = 1.8378770664093453
MESH = pl.DeviceIdType.MESH
TILE_ROWS = 16
TILE_COLS = 128
OBS_BLOCK = 2048
LEVELS = 32760.0
OCTAVE = 128.0
TINY = 1e-33


def pieces(values):
    high = values.astype(jnp.bfloat16).astype(jnp.float32)
    rest = values - high
    mid = rest.astype(jnp.bfloat16).astype(jnp.float32)
    return high, mid, rest - mid


def partial_grids(rows, width, cells, mask, values, error):
    count = cells.shape[1]
    used = mask.astype(jnp.float32)
    inverse = used / (error * error)
    terms = (
        inverse,
        inverse * values,
        inverse * values * values + used * (2.0 * jnp.log(error) + LOG_TWO_PI),
    )
    row = cells // width
    column = cells - row * width
    row_hit = lax.broadcasted_iota(jnp.int32, (rows, count), 0) == row
    column_hit = jnp.where(
        lax.broadcasted_iota(jnp.int32, (width, count), 0) == column, 1.0, 0.0
    ).astype(jnp.bfloat16)
    left = jnp.concatenate(
        [
            jnp.where(row_hit, piece, 0.0).astype(jnp.bfloat16)
            for term in terms
            for piece in pieces(term)
        ],
        axis=0,
    )
    return lax.dot_general(
        left, column_hit, (((1,), (1,)), ((), ())), preferred_element_type=jnp.float32
    )


def kernel_values(offset):
    values = jnp.exp(-((2.0 * offset.astype(jnp.float32) / SMOOTH) ** 2))
    return jnp.where(jnp.abs(offset) <= SMOOTH, values, 0.0)


def encode(means):
    top = functools.reduce(jnp.maximum, [jnp.abs(mean) for mean in means])
    code = jnp.ceil(jnp.log(jnp.maximum(top, TINY)) * (OCTAVE / math.log(2.0))) + 1.0
    levels = LEVELS * jnp.exp(code * (-math.log(2.0) / OCTAVE))
    whole = [jnp.floor(mean * levels + 0.5) for mean in means] + [code]
    return [value.astype(jnp.int32).astype(jnp.int16) for value in whole]


def integer(ref):
    return ref.astype(jnp.int32).astype(jnp.float32)


def scale_of(code):
    return jnp.exp(integer(code) * (math.log(2.0) / OCTAVE)) * (1.0 / LEVELS)


def cycle_kernel(
    n,
    state_ref,
    counts_ref,
    east_ref,
    north_ref,
    cells_ref,
    mask_ref,
    values_ref,
    error_ref,
    relax_ref,
    out_ref,
    mean_ref,
    cells,
    mask,
    values,
    error,
    state,
    counted,
    obs_send,
    obs_recv,
    grids,
    halo,
    wind_in,
    wind_halo,
    winds,
    advected,
    lon_kernel,
    loglik,
    loglik_halo,
    scores,
    held,
    send,
    send_log,
    recv,
    recv_log,
    merged,
    halo_sems,
    send_sems,
    recv_sems,
    send_log_sems,
    recv_log_sems,
    back_send,
    back_recv,
    relay_send,
    local_sems,
    obs_sems,
    obs_arrived,
    grid_sems,
    grid_arrived,
):
    slots, fields, rows, width = state_ref.shape
    across = width // TILE_COLS
    owners = (rows // TILE_ROWS) * across
    me = lax.axis_index("mem")
    band = lax.axis_index("lat")
    other = 1 - band

    share = cells.shape[1]
    mine = pl.ds(pl.multiple_of(me * share, 128), share)
    loads = [
        pltpu.make_async_copy(source, target, local_sems.at[k])
        for k, (source, target) in enumerate(
            (
                (cells_ref.at[:, mine], cells),
                (mask_ref.at[:, mine], mask),
                (values_ref.at[:, mine], values),
                (error_ref.at[:, mine], error),
                (state_ref, state),
            )
        )
    ]
    for load in loads:
        load.start()

    barrier = pltpu.get_barrier_semaphore()

    def greet(d, carry):
        pl.semaphore_signal(
            barrier, inc=1, device_id={"mem": lax.rem(me + d, n)}, device_id_type=MESH
        )
        return carry

    pl.semaphore_signal(barrier, inc=1, device_id={"lat": other}, device_id_type=MESH)
    lax.fori_loop(1, n, greet, 0)

    wind_in[0] = east_ref[...]
    wind_in[1] = north_ref[...]
    i0 = lax.broadcasted_iota(jnp.int32, (width, width), 0)
    i1 = lax.broadcasted_iota(jnp.int32, (width, width), 1)
    apart = jnp.abs(i0 - i1)
    lon_kernel[...] = kernel_values(jnp.minimum(apart, width - apart))

    pl.semaphore_wait(barrier, n)

    def to_other(source, target, slot):
        copy = pltpu.make_async_remote_copy(
            src_ref=source,
            dst_ref=target,
            send_sem=halo_sems.at[0, slot],
            recv_sem=halo_sems.at[1, slot],
            device_id={"lat": other},
            device_id_type=MESH,
        )
        copy.start()
        return copy

    edge16 = pl.ds(pl.multiple_of(other * (rows - 16), 16), 16)
    edge8 = pl.ds(pl.multiple_of(other * (rows - 8), 8), 8)
    copy_winds = to_other(wind_in.at[:, edge8, :], wind_halo, 0)
    copy_state = to_other(state_ref.at[:, :, edge16, :], halo, 1)

    def tile(t):
        down = t // across
        return (
            pl.ds(pl.multiple_of(down * TILE_ROWS, TILE_ROWS), TILE_ROWS),
            pl.ds(pl.multiple_of((t - down * across) * TILE_COLS, TILE_COLS), TILE_COLS),
        )

    for load in loads[:4]:
        load.wait()
    block = min(share, OBS_BLOCK)
    for start in range(0, share, block):
        part = partial_grids(
            rows, width, *(ref[:, start : start + block] for ref in (cells, mask, values, error))
        )
        for term in range(3):
            base = 3 * term * rows
            terms = (
                part[base : base + rows]
                + part[base + rows : base + 2 * rows]
                + part[base + 2 * rows : base + 3 * rows]
            )
            if start == 0:
                counted[term] = terms
            else:
                counted[term] += terms

    def obs_out(t):
        return pltpu.make_async_remote_copy(
            src_ref=obs_send.at[t],
            dst_ref=obs_recv.at[me],
            send_sem=obs_sems.at[t],
            recv_sem=obs_arrived.at[me],
            device_id={"mem": t},
            device_id_type=MESH,
        )

    def give(j, carry):
        t = lax.rem(me + 1 + j, owners)
        down, along = tile(t)
        for term in range(3):
            obs_send[t, term] = counted[term, down, along]

        @pl.when(t != me)
        def _():
            obs_out(t).start()

        return carry

    lax.fori_loop(0, owners, give, 0)

    def grid_out(d):
        return pltpu.make_async_remote_copy(
            src_ref=grids.at[me],
            dst_ref=grids.at[me],
            send_sem=grid_sems.at[d],
            recv_sem=grid_arrived.at[me],
            device_id={"mem": lax.rem(me + d, n)},
            device_id_type=MESH,
        )

    near = lax.broadcasted_iota(jnp.int32, (8, width), 0)
    keep = jnp.where(band == 0, near, 7 - near) < STEPS

    copy_winds.wait()
    for kind in range(2):
        own = wind_in[kind]
        far = jnp.where(keep, wind_halo[kind], 0.0)
        whole = jnp.concatenate([own, far], axis=0)
        winds[2 * kind] = jnp.abs(whole)
        winds[2 * kind + 1] = whole
    loads[4].wait()
    copy_state.wait()

    def move(index, carry):
        kind = index // slots
        slot = lax.rem(index, slots)
        own = state[slot, kind].astype(jnp.float32)
        far = halo[slot, kind].astype(jnp.float32)
        far = jnp.where(band == 0, far[:8], far[8:])
        far = jnp.where(keep, far, 0.0)
        x = jnp.concatenate([own, far], axis=0)
        for _ in range(STEPS):
            west = pltpu.roll(x, 1, 1)
            east = pltpu.roll(x, width - 1, 1)
            south = pltpu.roll(x, 1, 0)
            north = pltpu.roll(x, rows + 7, 0)
            x = (
                x
                - winds[0] * (x - jnp.where(winds[1] > 0.0, west, east))
                - winds[2] * (x - jnp.where(winds[3] > 0.0, south, north))
            )
        advected[slot, kind] = x[:rows].astype(jnp.bfloat16)
        return carry

    total = slots * fields
    early, late = 3 * total // 8, 6 * total // 8
    lax.fori_loop(0, early, move, 0)

    @pl.when(me < owners)
    def _():
        def arrive(d, carry):
            source = lax.rem(me + n - d, n)
            pltpu.make_async_remote_copy(
                src_ref=obs_send.at[0],
                dst_ref=obs_recv.at[source],
                send_sem=obs_sems.at[0],
                recv_sem=obs_arrived.at[source],
                device_id={"mem": source},
                device_id_type=MESH,
            ).wait_recv()
            return carry

        lax.fori_loop(1, n, arrive, 0)
        obs_recv[me] = obs_send[me]
        grids[me] = lax.fori_loop(1, n, lambda d, sums: sums + obs_recv[d], obs_recv[0])

        def start(d, carry):
            grid_out(d).start()
            return carry

        lax.fori_loop(1, n, start, 0)

    lax.fori_loop(early, late, move, 0)

    def likely(t, carry):
        @pl.when(t != me)
        def _():
            pltpu.make_async_remote_copy(
                src_ref=grids.at[t],
                dst_ref=grids.at[t],
                send_sem=grid_sems.at[0],
                recv_sem=grid_arrived.at[t],
                device_id={"mem": t},
                device_id_type=MESH,
            ).wait_recv()

        down, along = tile(t)
        for slot in range(slots):
            value = advected[slot, 0, down, along].astype(jnp.float32)
            loglik[slot, down, along] = -0.5 * (
                grids[t, 0] * value * value - 2.0 * grids[t, 1] * value + grids[t, 2]
            )
        return carry

    lax.fori_loop(0, owners, likely, 0)
    copy_loglik = to_other(loglik.at[:, edge16, :], loglik_halo, 2)
    lax.fori_loop(late, total, move, 0)

    r0 = lax.broadcasted_iota(jnp.int32, (rows, rows), 0)
    r1 = lax.broadcasted_iota(jnp.int32, (rows, rows), 1)
    own_band = kernel_values(r0 - r1)
    h0 = lax.broadcasted_iota(jnp.int32, (rows, 16), 0)
    h1 = lax.broadcasted_iota(jnp.int32, (rows, 16), 1)
    far_band = kernel_values(jnp.where(band == 0, rows + h1 - h0, h0 + 16 - h1))
    dot = functools.partial(
        jnp.dot, precision=lax.Precision.HIGHEST, preferred_element_type=jnp.float32
    )
    copy_loglik.wait()
    smoothed = jnp.concatenate(
        [
            dot(own_band, loglik[slot]) + dot(far_band, loglik_halo[slot])
            for slot in range(slots)
        ],
        axis=0,
    )
    scores[...] = dot(smoothed, lon_kernel[...]).reshape(slots, rows, width)

    partner = me + 1 - 2 * lax.rem(me, 2)
    parity = lax.rem(me, 2)

    half = n // 2

    def copies(t, slot, target):
        return [
            pltpu.make_async_remote_copy(
                src_ref=source.at[t],
                dst_ref=landing.at[slot],
                send_sem=sent_sems.at[t],
                recv_sem=landed_sems.at[slot],
                device_id={"mem": target},
                device_id_type=MESH,
            )
            for source, landing, sent_sems, landed_sems in (
                (send_log, recv_log, send_log_sems, recv_log_sems),
                (send, recv, send_sems, recv_sems),
            )
        ]

    def outgoing(t):
        return copies(t, me // 2, t)

    def across_pair(t):
        return copies(t, half + t // 2, partner)

    def start_all(made):
        for copy in made:
            copy.start()

    def gather(t):
        down, along = tile(t)
        live = [
            jnp.where(slot < counts_ref[0], scores[slot, down, along], -jnp.inf)
            for slot in range(slots)
        ]
        peak = functools.reduce(jnp.maximum, live)
        gains = [jnp.exp(score - peak) for score in live]
        weighted = [
            functools.reduce(
                jnp.add,
                [
                    gains[slot] * advected[slot, kind, down, along].astype(jnp.float32)
                    for slot in range(slots)
                ],
            )
            for kind in range(fields)
        ]
        return weighted, functools.reduce(jnp.add, gains), peak

    def put(t, weighted, total, peak):
        send_log[t] = peak + jnp.log(total)
        inverse = 1.0 / total
        for plane, value in enumerate(encode([value * inverse for value in weighted])):
            send[t, plane] = value

    def hold(t, weighted, total, peak):
        for plane, value in enumerate(weighted + [total, peak]):
            held[t // 2, plane] = value

    def give_pair(j, carry):
        t = lax.rem(partner + turn(j), owners)
        put(t, *gather(t))
        start_all(across_pair(t))
        return carry

    def turn(j):
        return lax.rem(owners + 4 - 2 * j, owners)

    def keep_own(j, carry):
        t = 2 * j + parity
        hold(t, *gather(t))
        return carry

    def merge(t, slot):
        low, high = held[t // 2, fields + 1], recv_log[slot]
        peak = jnp.maximum(low, high)
        low, high = jnp.exp(low - peak), jnp.exp(high - peak)
        scaled = high * scale_of(recv[slot, fields])
        weighted = [
            low * held[t // 2, kind] + scaled * integer(recv[slot, kind])
            for kind in range(fields)
        ]
        return weighted, low * held[t // 2, fields] + high, peak

    def give_owner(j, carry):
        t = lax.rem(me + turn(j), owners)
        for copy in across_pair(t):
            copy.wait_recv()
        sums = merge(t, half + t // 2)

        @pl.when(t != me)
        def _():
            put(t, *sums)
            start_all(outgoing(t))

        @pl.when(t == me)
        def _():
            hold(t, *sums)

        return carry

    lax.fori_loop(0, owners // 2, give_pair, 0)
    lax.fori_loop(0, owners // 2, keep_own, 0)
    lax.fori_loop(0, owners // 2, give_owner, 0)

    def back(d):
        return pltpu.make_async_remote_copy(
            src_ref=merged.at[me],
            dst_ref=merged.at[me],
            send_sem=back_send.at[d],
            recv_sem=back_recv.at[me],
            device_id={"mem": lax.rem(me + 2 * d, n)},
            device_id_type=MESH,
        )

    def relay(t):
        return pltpu.make_async_remote_copy(
            src_ref=merged.at[t],
            dst_ref=merged.at[t],
            send_sem=relay_send.at[t],
            recv_sem=back_recv.at[t],
            device_id={"mem": partner},
            device_id_type=MESH,
        )

    @pl.when(me < owners)
    def _():
        def arrive(d, carry):
            source = lax.rem(me + 2 * d, n)
            for copy in copies(0, source // 2, source):
                copy.wait_recv()
            return carry

        lax.fori_loop(1, half, arrive, 0)
        own = me // 2
        peak = lax.fori_loop(
            1,
            half,
            lambda d, top: jnp.maximum(top, recv_log[lax.rem(own + d, half)]),
            held[own, fields + 1],
        )

        def add(d, sums):
            slot = lax.rem(own + d, half)
            factor = jnp.exp(recv_log[slot] - peak)
            scaled = factor * scale_of(recv[slot, fields])
            return tuple(
                sums[kind] + scaled * integer(recv[slot, kind]) for kind in range(fields)
            ) + (sums[fields] + factor,)

        factor = jnp.exp(held[own, fields + 1] - peak)
        sums = lax.fori_loop(
            1, half, add, tuple(factor * held[own, plane] for plane in range(fields + 1))
        )
        inverse = 1.0 / sums[fields]
        for plane, value in enumerate(encode([sums[kind] * inverse for kind in range(fields)])):
            merged[me, plane] = value

        def start(d, carry):
            back(d).start()
            return carry

        lax.fori_loop(1, n // 2, start, 0)

    def landed(t):
        @pl.when(t != me)
        def _():
            relay(t).wait_recv()

    def pass_on(j, carry):
        t = lax.rem(me + owners - 2 * j, owners)
        landed(t)
        relay(t).start()
        finish(t)
        return carry

    def accept(j, carry):
        t = lax.rem(partner + owners - 2 * j, owners)
        landed(t)
        finish(t)
        return carry

    def finish(t):
        down, along = tile(t)
        scale = scale_of(merged[t, fields])
        for kind in range(fields):
            mean = scale * integer(merged[t, kind])
            mean_ref[kind, down, along] = mean.astype(jnp.bfloat16)
            for slot in range(slots):
                value = advected[slot, kind, down, along].astype(jnp.float32)
                fresh = value + relax_ref[kind] * (mean - value)
                out_ref[slot, kind, down, along] = jnp.where(
                    slot < counts_ref[0], fresh, 0.0
                ).astype(jnp.bfloat16)

    lax.fori_loop(0, owners // 2, pass_on, 0)
    lax.fori_loop(0, owners // 2, accept, 0)

    def sent(t, carry):
        @pl.when(t != me)
        def _():
            obs_out(t).wait_send()

        return carry

    lax.fori_loop(0, owners, sent, 0)

    def passed(j, carry):
        for copy in across_pair(2 * j + 1 - parity):
            copy.wait_send()

        @pl.when(2 * j + parity != me)
        def _():
            for copy in outgoing(2 * j + parity):
                copy.wait_send()

        relay(2 * j + parity).wait_send()
        return carry

    lax.fori_loop(0, owners // 2, passed, 0)

    @pl.when(me < owners)
    def _():
        def sent_back(d, carry):
            back(d).wait_send()
            return carry

        lax.fori_loop(1, n // 2, sent_back, 0)

        def sent_grids(d, carry):
            grid_out(d).wait_send()
            return carry

        lax.fori_loop(1, n, sent_grids, 0)


def cycle(n, state, counts, east_wind, north_wind, obs, relax):
    slots, fields, rows, width = state.shape
    owners = (rows // TILE_ROWS) * (width // TILE_COLS)
    share = obs[0].shape[1] // n
    tile = (TILE_ROWS, TILE_COLS)
    hbm = pl.BlockSpec(memory_space=pl.ANY)
    vmem = pl.BlockSpec(memory_space=pltpu.VMEM)
    smem = pl.BlockSpec(memory_space=pltpu.SMEM)
    f32, bf16 = jnp.float32, jnp.bfloat16
    return pl.pallas_call(
        functools.partial(cycle_kernel, n),
        out_shape=(
            pltpu.VMEM(state.shape, bf16),
            pltpu.VMEM((fields, rows, width), bf16),
        ),
        in_specs=[hbm, smem, vmem, vmem, hbm, hbm, hbm, hbm, smem],
        out_specs=(vmem, vmem),
        scratch_shapes=[
            pltpu.VMEM((1, share), jnp.int32),
            pltpu.VMEM((1, share), jnp.int32),
            pltpu.VMEM((1, share), f32),
            pltpu.VMEM((1, share), f32),
            pltpu.VMEM(state.shape, bf16),
            pltpu.VMEM((3, rows, width), f32),
            pltpu.VMEM((owners, 3) + tile, f32),
            pltpu.VMEM((n, 3) + tile, f32),
            pltpu.VMEM((owners, 3) + tile, f32),
            pltpu.VMEM((slots, fields, 16, width), bf16),
            pltpu.VMEM((2, rows, width), f32),
            pltpu.VMEM((2, 8, width), f32),
            pltpu.VMEM((4, rows + 8, width), f32),
            pltpu.VMEM((slots, fields, rows, width), bf16),
            pltpu.VMEM((width, width), f32),
            pltpu.VMEM((slots, rows, width), f32),
            pltpu.VMEM((slots, 16, width), f32),
            pltpu.VMEM((slots, rows, width), f32),
            pltpu.VMEM((owners // 2, fields + 2) + tile, f32),
            pltpu.VMEM((owners, fields + 1) + tile, jnp.int16),
            pltpu.VMEM((owners,) + tile, f32),
            pltpu.VMEM((n // 2 + owners // 2, fields + 1) + tile, jnp.int16),
            pltpu.VMEM((n // 2 + owners // 2,) + tile, f32),
            pltpu.VMEM((owners, fields + 1) + tile, jnp.int16),
            pltpu.SemaphoreType.DMA((2, 3)),
            pltpu.SemaphoreType.DMA((owners,)),
            pltpu.SemaphoreType.DMA((n // 2 + owners // 2,)),
            pltpu.SemaphoreType.DMA((owners,)),
            pltpu.SemaphoreType.DMA((n // 2 + owners // 2,)),
            pltpu.SemaphoreType.DMA((n,)),
            pltpu.SemaphoreType.DMA((owners,)),
            pltpu.SemaphoreType.DMA((owners,)),
            pltpu.SemaphoreType.DMA((5,)),
            pltpu.SemaphoreType.DMA((owners,)),
            pltpu.SemaphoreType.DMA((n,)),
            pltpu.SemaphoreType.DMA((n,)),
            pltpu.SemaphoreType.DMA((owners,)),
        ],
        compiler_params=pltpu.CompilerParams(
            collective_id=0, has_side_effects=True, vmem_limit_bytes=56 * 1024 * 1024
        ),
    )(state, counts, east_wind, north_wind, *obs, relax)


def write_kernel(fresh, mean, out, mean_out, sems):
    copies = [
        pltpu.make_async_copy(fresh, out, sems.at[0]),
        pltpu.make_async_copy(mean, mean_out, sems.at[1]),
    ]
    for copy in copies:
        copy.start()
    for copy in copies:
        copy.wait()


def write_out(fresh, mean):
    hbm = pl.BlockSpec(memory_space=pl.ANY)
    return pl.pallas_call(
        write_kernel,
        out_shape=(
            jax.ShapeDtypeStruct(fresh.shape, fresh.dtype),
            jax.ShapeDtypeStruct(mean.shape, mean.dtype),
        ),
        in_specs=[hbm, hbm],
        out_specs=(hbm, hbm),
        scratch_shapes=[pltpu.SemaphoreType.DMA((2,))],
    )(*(pltpu.with_memory_space_constraint(x, pltpu.VMEM) for x in (fresh, mean)))


def on_device(
    n, state, counts, east_wind, north_wind, obs_cells, obs_mask, obs_values, obs_error, relax
):
    obs = (obs_cells, obs_mask, obs_values, obs_error)
    fresh, mean = cycle(n, state, counts, east_wind, north_wind, obs, relax)
    return write_out(fresh, mean)


def solution(mesh):
    return jax.shard_map(
        functools.partial(on_device, mesh.shape["mem"]),
        mesh=mesh,
        in_specs=(
            P(("groups", "mem"), None, "lat", None),
            P(("groups", "mem")),
            P(("groups", "lat"), None),
            P(("groups", "lat"), None),
            P(("groups", "lat"), None),
            P(("groups", "lat"), None),
            P(("groups", "lat"), None),
            P(("groups", "lat"), None),
            P(),
        ),
        out_specs=(P(("groups", "mem"), None, "lat", None), P("groups", "lat", None)),
        check_vma=False,
    )
```

```python
import functools
import math

import jax
import jax.numpy as jnp
from jax import lax
from jax.experimental import pallas as pl
from jax.experimental.pallas import tpu as pltpu
from jax.sharding import PartitionSpec as P

STEPS = 4
SMOOTH = 16
LOG_TWO_PI = 1.8378770664093453
MESH = pl.DeviceIdType.MESH
TILE_ROWS = 16
TILE_COLS = 128
OBS_BLOCK = 2048
TOGETHER = 4
LEVELS = 32760.0
OCTAVE = 128.0
TINY = 1e-33


def pieces(values):
    high = values.astype(jnp.bfloat16).astype(jnp.float32)
    rest = values - high
    mid = rest.astype(jnp.bfloat16).astype(jnp.float32)
    return high, mid, rest - mid


def partial_grids(rows, width, cells, mask, values, error):
    count = cells.shape[1]
    used = mask.astype(jnp.float32)
    inverse = used / (error * error)
    terms = (
        inverse,
        inverse * values,
        inverse * values * values + used * (2.0 * jnp.log(error) + LOG_TWO_PI),
    )
    row = cells // width
    column = cells - row * width
    row_hit = lax.broadcasted_iota(jnp.int32, (rows, count), 0) == row
    column_hit = jnp.where(
        lax.broadcasted_iota(jnp.int32, (width, count), 0) == column, 1.0, 0.0
    ).astype(jnp.bfloat16)
    left = jnp.concatenate(
        [
            jnp.where(row_hit, piece, 0.0).astype(jnp.bfloat16)
            for term in terms
            for piece in pieces(term)
        ],
        axis=0,
    )
    return lax.dot_general(
        left, column_hit, (((1,), (1,)), ((), ())), preferred_element_type=jnp.float32
    )


def one_hot(hit):
    return jnp.where(hit, 1.0, 0.0).astype(jnp.bfloat16)


def permute(values, matrix):
    return jnp.dot(values, matrix, preferred_element_type=jnp.float32)


def kernel_values(offset):
    values = jnp.exp(-((2.0 * offset.astype(jnp.float32) / SMOOTH) ** 2))
    return jnp.where(jnp.abs(offset) <= SMOOTH, values, 0.0)


def encode(means):
    top = functools.reduce(jnp.maximum, [jnp.abs(mean) for mean in means])
    code = jnp.ceil(jnp.log(jnp.maximum(top, TINY)) * (OCTAVE / math.log(2.0))) + 1.0
    levels = LEVELS * jnp.exp(code * (-math.log(2.0) / OCTAVE))
    whole = [jnp.floor(mean * levels + 0.5) for mean in means] + [code]
    return [value.astype(jnp.int32).astype(jnp.int16) for value in whole]


def integer(ref):
    return ref.astype(jnp.int32).astype(jnp.float32)


def scale_of(code):
    return jnp.exp(integer(code) * (math.log(2.0) / OCTAVE)) * (1.0 / LEVELS)


def cycle_kernel(
    n,
    state_ref,
    counts_ref,
    east_ref,
    north_ref,
    cells_ref,
    mask_ref,
    values_ref,
    error_ref,
    relax_ref,
    out_ref,
    mean_ref,
    cells,
    mask,
    values,
    error,
    state,
    count,
    factors,
    counted,
    obs_send,
    obs_recv,
    grids,
    halo,
    wind_in,
    wind_halo,
    winds,
    spread_columns,
    gather_columns,
    lines,
    moved,
    advected,
    lon_kernel,
    loglik,
    loglik_halo,
    scores,
    held,
    send,
    send_log,
    recv,
    recv_log,
    merged,
    halo_sems,
    send_sems,
    recv_sems,
    send_log_sems,
    recv_log_sems,
    back_send,
    back_recv,
    relay_send,
    local_sems,
    obs_sems,
    obs_arrived,
    grid_sems,
    grid_arrived,
):
    slots, fields, rows, width = state_ref.shape
    across = width // TILE_COLS
    owners = (rows // TILE_ROWS) * across
    me = lax.axis_index("mem")
    band = lax.axis_index("lat")
    other = 1 - band

    share = cells.shape[1]
    mine = pl.ds(pl.multiple_of(me * share, 128), share)
    loads = [
        pltpu.make_async_copy(source, target, local_sems.at[k])
        for k, (source, target) in enumerate(
            (
                (cells_ref.at[:, mine], cells),
                (mask_ref.at[:, mine], mask),
                (values_ref.at[:, mine], values),
                (error_ref.at[:, mine], error),
                (state_ref, state),
                (east_ref, wind_in.at[0]),
                (north_ref, wind_in.at[1]),
                (counts_ref, count),
                (relax_ref, factors),
            )
        )
    ]
    for load in loads:
        load.start()

    barrier = pltpu.get_barrier_semaphore()

    def greet(d, carry):
        pl.semaphore_signal(
            barrier, inc=1, device_id={"mem": lax.rem(me + d, n)}, device_id_type=MESH
        )
        return carry

    pl.semaphore_signal(barrier, inc=1, device_id={"lat": other}, device_id_type=MESH)
    lax.fori_loop(1, n, greet, 0)

    i0 = lax.broadcasted_iota(jnp.int32, (width, width), 0)
    i1 = lax.broadcasted_iota(jnp.int32, (width, width), 1)
    spread_columns[...] = one_hot(i0 == across * lax.rem(i1, TILE_COLS) + i1 // TILE_COLS)
    gather_columns[...] = one_hot(i1 == across * lax.rem(i0, TILE_COLS) + i0 // TILE_COLS)
    apart = jnp.abs(i0 - i1)
    lon_kernel[...] = kernel_values(jnp.minimum(apart, width - apart))

    for load in loads[5:]:
        load.wait()
    pl.semaphore_wait(barrier, n)

    def to_other(source, target, slot):
        copy = pltpu.make_async_remote_copy(
            src_ref=source,
            dst_ref=target,
            send_sem=halo_sems.at[0, slot],
            recv_sem=halo_sems.at[1, slot],
            device_id={"lat": other},
            device_id_type=MESH,
        )
        copy.start()
        return copy

    edge16 = pl.ds(pl.multiple_of(other * (rows - 16), 16), 16)
    edge8 = pl.ds(pl.multiple_of(other * (rows - 8), 8), 8)
    copy_winds = to_other(wind_in.at[:, edge8, :], wind_halo, 0)
    copy_state = to_other(state_ref.at[:, :, edge16, :], halo, 1)

    def tile(t):
        down = t // across
        return (
            pl.ds(pl.multiple_of(down * TILE_ROWS, TILE_ROWS), TILE_ROWS),
            pl.ds(pl.multiple_of((t - down * across) * TILE_COLS, TILE_COLS), TILE_COLS),
        )

    for load in loads[:4]:
        load.wait()
    block = min(share, OBS_BLOCK)
    for start in range(0, share, block):
        part = partial_grids(
            rows, width, *(ref[:, start : start + block] for ref in (cells, mask, values, error))
        )
        for term in range(3):
            base = 3 * term * rows
            terms = (
                part[base : base + rows]
                + part[base + rows : base + 2 * rows]
                + part[base + 2 * rows : base + 3 * rows]
            )
            if start == 0:
                counted[term] = terms
            else:
                counted[term] += terms

    def obs_out(t):
        return pltpu.make_async_remote_copy(
            src_ref=obs_send.at[t],
            dst_ref=obs_recv.at[me],
            send_sem=obs_sems.at[t],
            recv_sem=obs_arrived.at[me],
            device_id={"mem": t},
            device_id_type=MESH,
        )

    def give(j, carry):
        t = lax.rem(me + 1 + j, owners)
        down, along = tile(t)
        for term in range(3):
            obs_send[t, term] = counted[term, down, along]

        @pl.when(t != me)
        def _():
            obs_out(t).start()

        return carry

    lax.fori_loop(0, owners, give, 0)

    def grid_out(d):
        return pltpu.make_async_remote_copy(
            src_ref=grids.at[me],
            dst_ref=grids.at[me],
            send_sem=grid_sems.at[d],
            recv_sem=grid_arrived.at[me],
            device_id={"mem": lax.rem(me + d, n)},
            device_id_type=MESH,
        )

    near = lax.broadcasted_iota(jnp.int32, (8, width), 0)
    keep = jnp.where(band == 0, near, 7 - near) < STEPS

    layers = (rows + 8) // 8

    def columns(c):
        return slice(c * TILE_COLS, (c + 1) * TILE_COLS)

    def spread(ref, c):
        return jnp.stack([ref[c, pl.ds(k, 8, stride=layers), :] for k in range(layers)])

    copy_winds.wait()
    split = []
    for kind in range(2):
        far = jnp.where(keep, wind_halo[kind], 0.0)
        split += pieces(jnp.concatenate([wind_in[kind], far], axis=0))
    split = permute(
        jnp.concatenate([piece.astype(jnp.bfloat16) for piece in split], axis=0),
        spread_columns[...],
    ).reshape(2, 3, rows + 8, width)
    for kind in range(2):
        whole = (split[kind, 0] + split[kind, 1]) + split[kind, 2]
        for c in range(across):
            lines[0, kind, c] = whole[:, columns(c)]
            wind = spread(lines.at[0, kind], c)
            winds[2 * kind, c] = jnp.abs(wind)
            winds[2 * kind + 1, c] = wind
    loads[4].wait()
    copy_state.wait()

    def lay_out(slot, carry):
        whole = permute(
            jnp.concatenate(
                [state[slot].reshape(fields * rows, width), halo[slot].reshape(fields * 16, width)],
                axis=0,
            ),
            spread_columns[...],
        )
        own = whole[: fields * rows].reshape(fields, rows, width)
        far = whole[fields * rows :].reshape(fields, 16, width)
        far = jnp.where(band == 0, far[:, :8], far[:, 8:])
        for c in range(across):
            lines[slot, :, c, :rows] = own[:, :, columns(c)]
            lines[slot, :, c, rows:] = jnp.where(keep[:, columns(c)], far[:, :, columns(c)], 0.0)
        return carry

    lax.fori_loop(0, slots, lay_out, 0)

    def step(x):
        west = [pltpu.roll(x[across - 1], 1, 2)] + x[:-1]
        east = x[1:] + [pltpu.roll(x[0], TILE_COLS - 1, 2)]
        south = [
            jnp.concatenate([pltpu.roll(v[layers - 1 :], 1, 1), v[: layers - 1]], axis=0) for v in x
        ]
        north = [jnp.concatenate([v[1:], pltpu.roll(v[:1], 7, 1)], axis=0) for v in x]
        return [
            x[c]
            - winds[0, c] * (x[c] - jnp.where(winds[1, c] > 0.0, west[c], east[c]))
            - winds[2, c] * (x[c] - jnp.where(winds[3, c] > 0.0, south[c], north[c]))
            for c in range(across)
        ]

    def move(index, carry):
        kind = index // (slots // TOGETHER)
        first = TOGETHER * lax.rem(index, slots // TOGETHER)
        fields_of = [lines.at[first + k, kind] for k in range(TOGETHER)]
        xs = [[spread(field, c) for c in range(across)] for field in fields_of]
        for _ in range(STEPS):
            xs = [step(x) for x in xs]
        for k, (field, x) in enumerate(zip(fields_of, xs)):
            for c in range(across):
                for layer in range(layers):
                    field[c, pl.ds(layer, 8, stride=layers), :] = x[c][layer]
                moved[kind, first + k, :, columns(c)] = field[c, :rows].astype(jnp.bfloat16)
        return carry

    def collect(first, last):
        whole = moved[first:last].reshape((last - first) * slots * rows, width)
        whole = permute(whole, gather_columns[...]).astype(jnp.bfloat16)
        advected[first:last] = whole.reshape(last - first, slots, rows, width)

    total = fields * (slots // TOGETHER)
    early, late = 3 * total // 8, 6 * total // 8
    lax.fori_loop(0, slots // TOGETHER, move, 0)
    collect(0, 1)
    lax.fori_loop(slots // TOGETHER, early, move, 0)

    @pl.when(me < owners)
    def _():
        def arrive(d, carry):
            source = lax.rem(me + n - d, n)
            pltpu.make_async_remote_copy(
                src_ref=obs_send.at[0],
                dst_ref=obs_recv.at[source],
                send_sem=obs_sems.at[0],
                recv_sem=obs_arrived.at[source],
                device_id={"mem": source},
                device_id_type=MESH,
            ).wait_recv()
            return carry

        lax.fori_loop(1, n, arrive, 0)
        obs_recv[me] = obs_send[me]
        grids[me] = lax.fori_loop(1, n, lambda d, sums: sums + obs_recv[d], obs_recv[0])

        def start(d, carry):
            grid_out(d).start()
            return carry

        lax.fori_loop(1, n, start, 0)

    lax.fori_loop(early, late, move, 0)

    def likely(t, carry):
        @pl.when(t != me)
        def _():
            pltpu.make_async_remote_copy(
                src_ref=grids.at[t],
                dst_ref=grids.at[t],
                send_sem=grid_sems.at[0],
                recv_sem=grid_arrived.at[t],
                device_id={"mem": t},
                device_id_type=MESH,
            ).wait_recv()

        down, along = tile(t)
        for slot in range(slots):
            value = advected[0, slot, down, along].astype(jnp.float32)
            loglik[slot, down, along] = -0.5 * (
                grids[t, 0] * value * value - 2.0 * grids[t, 1] * value + grids[t, 2]
            )
        return carry

    lax.fori_loop(0, owners, likely, 0)
    copy_loglik = to_other(loglik.at[:, edge16, :], loglik_halo, 2)
    lax.fori_loop(late, total, move, 0)
    collect(1, fields)

    r0 = lax.broadcasted_iota(jnp.int32, (rows, rows), 0)
    r1 = lax.broadcasted_iota(jnp.int32, (rows, rows), 1)
    own_band = kernel_values(r0 - r1)
    h0 = lax.broadcasted_iota(jnp.int32, (rows, 16), 0)
    h1 = lax.broadcasted_iota(jnp.int32, (rows, 16), 1)
    far_band = kernel_values(jnp.where(band == 0, rows + h1 - h0, h0 + 16 - h1))
    dot = functools.partial(
        jnp.dot, precision=lax.Precision.HIGHEST, preferred_element_type=jnp.float32
    )
    copy_loglik.wait()
    smoothed = jnp.concatenate(
        [
            dot(own_band, loglik[slot]) + dot(far_band, loglik_halo[slot])
            for slot in range(slots)
        ],
        axis=0,
    )
    scores[...] = dot(smoothed, lon_kernel[...]).reshape(slots, rows, width)

    partner = me + 1 - 2 * lax.rem(me, 2)
    parity = lax.rem(me, 2)

    half = n // 2

    def copies(t, slot, target):
        return [
            pltpu.make_async_remote_copy(
                src_ref=source.at[t],
                dst_ref=landing.at[slot],
                send_sem=sent_sems.at[t],
                recv_sem=landed_sems.at[slot],
                device_id={"mem": target},
                device_id_type=MESH,
            )
            for source, landing, sent_sems, landed_sems in (
                (send_log, recv_log, send_log_sems, recv_log_sems),
                (send, recv, send_sems, recv_sems),
            )
        ]

    def outgoing(t):
        return copies(t, me // 2, t)

    def across_pair(t):
        return copies(t, half + t // 2, partner)

    def start_all(made):
        for copy in made:
            copy.start()

    def gather(t):
        down, along = tile(t)
        live = [
            jnp.where(slot < count[0], scores[slot, down, along], -jnp.inf)
            for slot in range(slots)
        ]
        peak = functools.reduce(jnp.maximum, live)
        gains = [jnp.exp(score - peak) for score in live]
        weighted = [
            functools.reduce(
                jnp.add,
                [
                    gains[slot] * advected[kind, slot, down, along].astype(jnp.float32)
                    for slot in range(slots)
                ],
            )
            for kind in range(fields)
        ]
        return weighted, functools.reduce(jnp.add, gains), peak

    def put(t, weighted, total, peak):
        send_log[t] = peak + jnp.log(total)
        inverse = 1.0 / total
        for plane, value in enumerate(encode([value * inverse for value in weighted])):
            send[t, plane] = value

    def hold(t, weighted, total, peak):
        for plane, value in enumerate(weighted + [total, peak]):
            held[t // 2, plane] = value

    def turn(j):
        middle = owners // 2
        other_ones = 2 * j + 2 * jnp.where(2 * j >= middle, 1, 0)
        return jnp.where(j == 0, middle, jnp.where(j == middle - 1, 0, other_ones))

    def give_pair(j, carry):
        t = lax.rem(partner + turn(j), owners)
        put(t, *gather(t))
        start_all(across_pair(t))
        return carry

    def keep_own(j, carry):
        t = 2 * j + parity
        hold(t, *gather(t))
        return carry

    def merge(t, slot):
        low, high = held[t // 2, fields + 1], recv_log[slot]
        peak = jnp.maximum(low, high)
        low, high = jnp.exp(low - peak), jnp.exp(high - peak)
        scaled = high * scale_of(recv[slot, fields])
        weighted = [
            low * held[t // 2, kind] + scaled * integer(recv[slot, kind])
            for kind in range(fields)
        ]
        return weighted, low * held[t // 2, fields] + high, peak

    def give_owner(j, carry):
        t = lax.rem(me + turn(j), owners)
        for copy in across_pair(t):
            copy.wait_recv()
        sums = merge(t, half + t // 2)

        @pl.when(t != me)
        def _():
            put(t, *sums)
            start_all(outgoing(t))

        @pl.when(t == me)
        def _():
            hold(t, *sums)

        return carry

    lax.fori_loop(0, owners // 2, give_pair, 0)
    lax.fori_loop(0, owners // 2, keep_own, 0)
    lax.fori_loop(0, owners // 2, give_owner, 0)

    def back(d):
        return pltpu.make_async_remote_copy(
            src_ref=merged.at[me],
            dst_ref=merged.at[me],
            send_sem=back_send.at[d],
            recv_sem=back_recv.at[me],
            device_id={"mem": lax.rem(me + 2 * d, n)},
            device_id_type=MESH,
        )

    def relay(t):
        return pltpu.make_async_remote_copy(
            src_ref=merged.at[t],
            dst_ref=merged.at[t],
            send_sem=relay_send.at[t],
            recv_sem=back_recv.at[t],
            device_id={"mem": partner},
            device_id_type=MESH,
        )

    @pl.when(me < owners)
    def _():
        def arrive(d, carry):
            source = lax.rem(me + 2 * d, n)
            for copy in copies(0, source // 2, source):
                copy.wait_recv()
            return carry

        lax.fori_loop(1, half, arrive, 0)
        own = me // 2
        peak = lax.fori_loop(
            1,
            half,
            lambda d, top: jnp.maximum(top, recv_log[lax.rem(own + d, half)]),
            held[own, fields + 1],
        )

        def add(d, sums):
            slot = lax.rem(own + d, half)
            factor = jnp.exp(recv_log[slot] - peak)
            scaled = factor * scale_of(recv[slot, fields])
            return tuple(
                sums[kind] + scaled * integer(recv[slot, kind]) for kind in range(fields)
            ) + (sums[fields] + factor,)

        factor = jnp.exp(held[own, fields + 1] - peak)
        sums = lax.fori_loop(
            1, half, add, tuple(factor * held[own, plane] for plane in range(fields + 1))
        )
        inverse = 1.0 / sums[fields]
        for plane, value in enumerate(encode([sums[kind] * inverse for kind in range(fields)])):
            merged[me, plane] = value

        def start(d, carry):
            back(d).start()
            return carry

        lax.fori_loop(1, n // 2, start, 0)

    def landed(t):
        @pl.when(t != me)
        def _():
            relay(t).wait_recv()

    def pass_on(j, carry):
        t = lax.rem(me + owners - 2 * j, owners)
        landed(t)
        relay(t).start()
        finish(t)
        return carry

    def accept(j, carry):
        t = lax.rem(partner + owners - 2 * j, owners)
        landed(t)
        finish(t)
        return carry

    def finish(t):
        down, along = tile(t)
        scale = scale_of(merged[t, fields])
        for kind in range(fields):
            mean = scale * integer(merged[t, kind])
            mean_ref[kind, down, along] = mean.astype(jnp.bfloat16)
            for slot in range(slots):
                value = advected[kind, slot, down, along].astype(jnp.float32)
                fresh = value + factors[kind] * (mean - value)
                out_ref[slot, kind, down, along] = jnp.where(
                    slot < count[0], fresh, 0.0
                ).astype(jnp.bfloat16)

    lax.fori_loop(0, owners // 2, pass_on, 0)
    lax.fori_loop(0, owners // 2, accept, 0)

    def sent(t, carry):
        @pl.when(t != me)
        def _():
            obs_out(t).wait_send()

        return carry

    lax.fori_loop(0, owners, sent, 0)

    def passed(j, carry):
        for copy in across_pair(2 * j + 1 - parity):
            copy.wait_send()

        @pl.when(2 * j + parity != me)
        def _():
            for copy in outgoing(2 * j + parity):
                copy.wait_send()

        relay(2 * j + parity).wait_send()
        return carry

    lax.fori_loop(0, owners // 2, passed, 0)

    @pl.when(me < owners)
    def _():
        def sent_back(d, carry):
            back(d).wait_send()
            return carry

        lax.fori_loop(1, n // 2, sent_back, 0)

        def sent_grids(d, carry):
            grid_out(d).wait_send()
            return carry

        lax.fori_loop(1, n, sent_grids, 0)


def cycle(n, state, counts, east_wind, north_wind, obs, relax):
    slots, fields, rows, width = state.shape
    across = width // TILE_COLS
    owners = (rows // TILE_ROWS) * across
    share = obs[0].shape[1] // n
    tile = (TILE_ROWS, TILE_COLS)
    hbm = pl.BlockSpec(memory_space=pl.ANY)
    vmem = pl.BlockSpec(memory_space=pltpu.VMEM)
    f32, bf16 = jnp.float32, jnp.bfloat16
    return pl.pallas_call(
        functools.partial(cycle_kernel, n),
        out_shape=(
            pltpu.VMEM(state.shape, bf16),
            pltpu.VMEM((fields, rows, width), bf16),
        ),
        in_specs=[hbm] * 9,
        out_specs=(vmem, vmem),
        scratch_shapes=[
            pltpu.VMEM((1, share), jnp.int32),
            pltpu.VMEM((1, share), jnp.int32),
            pltpu.VMEM((1, share), f32),
            pltpu.VMEM((1, share), f32),
            pltpu.VMEM(state.shape, bf16),
            pltpu.SMEM(counts.shape, counts.dtype),
            pltpu.SMEM(relax.shape, relax.dtype),
            pltpu.VMEM((3, rows, width), f32),
            pltpu.VMEM((owners, 3) + tile, f32),
            pltpu.VMEM((n, 3) + tile, f32),
            pltpu.VMEM((owners, 3) + tile, f32),
            pltpu.VMEM((slots, fields, 16, width), bf16),
            pltpu.VMEM((2, rows, width), f32),
            pltpu.VMEM((2, 8, width), f32),
            pltpu.VMEM((4, across, (rows + 8) // 8, 8, TILE_COLS), f32),
            pltpu.VMEM((width, width), bf16),
            pltpu.VMEM((width, width), bf16),
            pltpu.VMEM((slots, fields, across, rows + 8, TILE_COLS), f32),
            pltpu.VMEM((fields, slots, rows, width), bf16),
            pltpu.VMEM((fields, slots, rows, width), bf16),
            pltpu.VMEM((width, width), f32),
            pltpu.VMEM((slots, rows, width), f32),
            pltpu.VMEM((slots, 16, width), f32),
            pltpu.VMEM((slots, rows, width), f32),
            pltpu.VMEM((owners // 2, fields + 2) + tile, f32),
            pltpu.VMEM((owners, fields + 1) + tile, jnp.int16),
            pltpu.VMEM((owners,) + tile, f32),
            pltpu.VMEM((n // 2 + owners // 2, fields + 1) + tile, jnp.int16),
            pltpu.VMEM((n // 2 + owners // 2,) + tile, f32),
            pltpu.VMEM((owners, fields + 1) + tile, jnp.int16),
            pltpu.SemaphoreType.DMA((2, 3)),
            pltpu.SemaphoreType.DMA((owners,)),
            pltpu.SemaphoreType.DMA((n // 2 + owners // 2,)),
            pltpu.SemaphoreType.DMA((owners,)),
            pltpu.SemaphoreType.DMA((n // 2 + owners // 2,)),
            pltpu.SemaphoreType.DMA((n,)),
            pltpu.SemaphoreType.DMA((owners,)),
            pltpu.SemaphoreType.DMA((owners,)),
            pltpu.SemaphoreType.DMA((9,)),
            pltpu.SemaphoreType.DMA((owners,)),
            pltpu.SemaphoreType.DMA((n,)),
            pltpu.SemaphoreType.DMA((n,)),
            pltpu.SemaphoreType.DMA((owners,)),
        ],
        compiler_params=pltpu.CompilerParams(
            collective_id=0, has_side_effects=True, vmem_limit_bytes=56 * 1024 * 1024
        ),
    )(state, counts, east_wind, north_wind, *obs, relax)


def write_kernel(fresh, mean, out, mean_out, sems):
    copies = [
        pltpu.make_async_copy(fresh, out, sems.at[0]),
        pltpu.make_async_copy(mean, mean_out, sems.at[1]),
    ]
    for copy in copies:
        copy.start()
    for copy in copies:
        copy.wait()


def write_out(fresh, mean):
    hbm = pl.BlockSpec(memory_space=pl.ANY)
    return pl.pallas_call(
        write_kernel,
        out_shape=(
            jax.ShapeDtypeStruct(fresh.shape, fresh.dtype),
            jax.ShapeDtypeStruct(mean.shape, mean.dtype),
        ),
        in_specs=[hbm, hbm],
        out_specs=(hbm, hbm),
        scratch_shapes=[pltpu.SemaphoreType.DMA((2,))],
    )(*(pltpu.with_memory_space_constraint(x, pltpu.VMEM) for x in (fresh, mean)))


def on_device(
    n, state, counts, east_wind, north_wind, obs_cells, obs_mask, obs_values, obs_error, relax
):
    obs = (obs_cells, obs_mask, obs_values, obs_error)
    fresh, mean = cycle(n, state, counts, east_wind, north_wind, obs, relax)
    return write_out(fresh, mean)


def solution(mesh):
    return jax.shard_map(
        functools.partial(on_device, mesh.shape["mem"]),
        mesh=mesh,
        in_specs=(
            P(("groups", "mem"), None, "lat", None),
            P(("groups", "mem")),
            P(("groups", "lat"), None),
            P(("groups", "lat"), None),
            P(("groups", "lat"), None),
            P(("groups", "lat"), None),
            P(("groups", "lat"), None),
            P(("groups", "lat"), None),
            P(),
        ),
        out_specs=(P(("groups", "mem"), None, "lat", None), P("groups", "lat", None)),
        check_vma=False,
    )
```

```python
import functools
import math

import jax
import jax.numpy as jnp
from jax import lax
from jax.experimental import pallas as pl
from jax.experimental.pallas import tpu as pltpu
from jax.sharding import PartitionSpec as P

STEPS = 4
SMOOTH = 16
LOG_TWO_PI = 1.8378770664093453
MESH = pl.DeviceIdType.MESH
TILE_ROWS = 16
TILE_COLS = 128
OBS_BLOCK = 2048
TOGETHER = 4
SHARERS = 4
LEVELS = 32760.0
OCTAVE = 128.0
TINY = 1e-33


def pieces(values):
    high = values.astype(jnp.bfloat16).astype(jnp.float32)
    rest = values - high
    mid = rest.astype(jnp.bfloat16).astype(jnp.float32)
    return high, mid, rest - mid


def partial_grids(rows, width, cells, mask, values, error):
    count = cells.shape[1]
    used = mask.astype(jnp.float32)
    inverse = used / (error * error)
    terms = (
        inverse,
        inverse * values,
        inverse * values * values + used * (2.0 * jnp.log(error) + LOG_TWO_PI),
    )
    row = cells // width
    column = cells - row * width
    row_hit = lax.broadcasted_iota(jnp.int32, (rows, count), 0) == row
    column_hit = jnp.where(
        lax.broadcasted_iota(jnp.int32, (width, count), 0) == column, 1.0, 0.0
    ).astype(jnp.bfloat16)
    left = jnp.concatenate(
        [
            jnp.where(row_hit, piece, 0.0).astype(jnp.bfloat16)
            for piece in pieces(terms[0]) + pieces(terms[1]) + pieces(terms[2])[:2]
        ],
        axis=0,
    )
    return lax.dot_general(
        left, column_hit, (((1,), (1,)), ((), ())), preferred_element_type=jnp.float32
    )


def one_hot(hit):
    return jnp.where(hit, 1.0, 0.0).astype(jnp.bfloat16)


def permute(values, matrix):
    return jnp.dot(values, matrix, preferred_element_type=jnp.float32)


def kernel_values(offset):
    values = jnp.exp(-((2.0 * offset.astype(jnp.float32) / SMOOTH) ** 2))
    return jnp.where(jnp.abs(offset) <= SMOOTH, values, 0.0)


def encode(means):
    top = functools.reduce(jnp.maximum, [jnp.abs(mean) for mean in means])
    code = jnp.ceil(jnp.log(jnp.maximum(top, TINY)) * (OCTAVE / math.log(2.0))) + 1.0
    levels = LEVELS * jnp.exp(code * (-math.log(2.0) / OCTAVE))
    whole = [jnp.floor(mean * levels + 0.5) for mean in means] + [code]
    return [value.astype(jnp.int32).astype(jnp.int16) for value in whole]


def integer(ref):
    return ref.astype(jnp.int32).astype(jnp.float32)


def scale_of(code):
    return jnp.exp(integer(code) * (math.log(2.0) / OCTAVE)) * (1.0 / LEVELS)


def cycle_kernel(
    n,
    state_ref,
    counts_ref,
    east_ref,
    north_ref,
    cells_ref,
    mask_ref,
    values_ref,
    error_ref,
    relax_ref,
    out_ref,
    mean_ref,
    cells,
    mask,
    values,
    error,
    state,
    count,
    factors,
    counted,
    obs_send,
    obs_recv,
    grids,
    halo,
    wind_in,
    wind_halo,
    winds,
    spread_columns,
    gather_columns,
    lines,
    moved,
    advected,
    lon_kernel,
    loglik,
    loglik_halo,
    scores,
    held,
    send,
    send_log,
    recv,
    recv_log,
    merged,
    halo_sems,
    send_sems,
    recv_sems,
    send_log_sems,
    recv_log_sems,
    back_send,
    back_recv,
    relay_send,
    local_sems,
    obs_sems,
    obs_arrived,
    grid_sems,
    grid_arrived,
):
    slots, fields, rows, width = state_ref.shape
    across = width // TILE_COLS
    owners = (rows // TILE_ROWS) * across
    me = lax.axis_index("mem")
    band = lax.axis_index("lat")
    other = 1 - band

    share = cells.shape[1]
    rank = lax.rem(me, SHARERS)
    first_rank = me - rank
    mine = pl.ds(pl.multiple_of(rank * share, 128), share)
    loads = [
        pltpu.make_async_copy(source, target, local_sems.at[k])
        for k, (source, target) in enumerate(
            (
                (cells_ref.at[:, mine], cells),
                (mask_ref.at[:, mine], mask),
                (values_ref.at[:, mine], values),
                (error_ref.at[:, mine], error),
                (state_ref, state),
                (east_ref, wind_in.at[0]),
                (north_ref, wind_in.at[1]),
                (counts_ref, count),
                (relax_ref, factors),
            )
        )
    ]
    for load in loads:
        load.start()

    barrier = pltpu.get_barrier_semaphore()

    def greet(d, carry):
        pl.semaphore_signal(
            barrier, inc=1, device_id={"mem": lax.rem(me + d, n)}, device_id_type=MESH
        )
        return carry

    pl.semaphore_signal(barrier, inc=1, device_id={"lat": other}, device_id_type=MESH)
    lax.fori_loop(1, n, greet, 0)

    for load in loads[5:]:
        load.wait()
    pl.semaphore_wait(barrier, n)

    def to_other(source, target, slot):
        copy = pltpu.make_async_remote_copy(
            src_ref=source,
            dst_ref=target,
            send_sem=halo_sems.at[0, slot],
            recv_sem=halo_sems.at[1, slot],
            device_id={"lat": other},
            device_id_type=MESH,
        )
        copy.start()
        return copy

    edge16 = pl.ds(pl.multiple_of(other * (rows - 16), 16), 16)
    edge8 = pl.ds(pl.multiple_of(other * (rows - 8), 8), 8)
    copy_winds = to_other(wind_in.at[:, edge8, :], wind_halo, 0)
    copy_state = to_other(state_ref.at[:, :, edge16, :], halo, 1)

    def tile(t):
        down = t // across
        return (
            pl.ds(pl.multiple_of(down * TILE_ROWS, TILE_ROWS), TILE_ROWS),
            pl.ds(pl.multiple_of((t - down * across) * TILE_COLS, TILE_COLS), TILE_COLS),
        )

    for load in loads[:4]:
        load.wait()
    block = min(share, OBS_BLOCK)

    def count_block(index, carry):
        at = pl.ds(pl.multiple_of(index * block, 128), block)
        part = partial_grids(rows, width, *(ref[:, at] for ref in (cells, mask, values, error)))
        for term, (base, number) in enumerate(((0, 3), (3, 3), (6, 2))):
            counted[term] += functools.reduce(
                jnp.add, [part[(base + k) * rows : (base + k + 1) * rows] for k in range(number)]
            )
        return carry

    counted[...] = jnp.zeros_like(counted)
    lax.fori_loop(0, share // block, count_block, 0)
    held_tiles = owners // SHARERS

    def near_by(d):
        return lax.rem(rank + d, SHARERS)

    def obs_out(d):
        return pltpu.make_async_remote_copy(
            src_ref=obs_send.at[near_by(d)],
            dst_ref=obs_recv.at[rank],
            send_sem=obs_sems.at[near_by(d)],
            recv_sem=obs_arrived.at[rank],
            device_id={"mem": first_rank + near_by(d)},
            device_id_type=MESH,
        )

    def give(d, carry):
        for k in range(held_tiles):
            down, along = tile(held_tiles * near_by(d) + k)
            for term in range(3):
                obs_send[near_by(d), k, term] = counted[term, down, along]

        @pl.when(d < SHARERS)
        def _():
            obs_out(d).start()

        return carry

    lax.fori_loop(1, SHARERS + 1, give, 0)

    def grid_out(d):
        return pltpu.make_async_remote_copy(
            src_ref=grids.at[rank],
            dst_ref=grids.at[rank],
            send_sem=grid_sems.at[d],
            recv_sem=grid_arrived.at[rank],
            device_id={"mem": first_rank + near_by(d)},
            device_id_type=MESH,
        )

    i0 = lax.broadcasted_iota(jnp.int32, (width, width), 0)
    i1 = lax.broadcasted_iota(jnp.int32, (width, width), 1)
    spread_columns[...] = one_hot(i0 == across * lax.rem(i1, TILE_COLS) + i1 // TILE_COLS)
    gather_columns[...] = one_hot(i1 == across * lax.rem(i0, TILE_COLS) + i0 // TILE_COLS)
    apart = jnp.abs(i0 - i1)
    lon_kernel[...] = kernel_values(jnp.minimum(apart, width - apart))

    near = lax.broadcasted_iota(jnp.int32, (8, width), 0)
    keep = jnp.where(band == 0, near, 7 - near) < STEPS

    layers = (rows + 8) // 8

    def columns(c):
        return slice(c * TILE_COLS, (c + 1) * TILE_COLS)

    def spread(ref, c):
        return jnp.stack([ref[c, pl.ds(k, 8, stride=layers), :] for k in range(layers)])

    copy_winds.wait()
    split = []
    for kind in range(2):
        far = jnp.where(keep, wind_halo[kind], 0.0)
        split += pieces(jnp.concatenate([wind_in[kind], far], axis=0))
    split = permute(
        jnp.concatenate([piece.astype(jnp.bfloat16) for piece in split], axis=0),
        spread_columns[...],
    ).reshape(2, 3, rows + 8, width)
    for kind in range(2):
        whole = (split[kind, 0] + split[kind, 1]) + split[kind, 2]
        for c in range(across):
            lines[0, kind, c] = whole[:, columns(c)]
            wind = spread(lines.at[0, kind], c)
            winds[2 * kind, c] = jnp.abs(wind)
            winds[2 * kind + 1, c] = wind
    loads[4].wait()
    copy_state.wait()

    def lay_out(slot, carry):
        whole = permute(
            jnp.concatenate(
                [state[slot].reshape(fields * rows, width), halo[slot].reshape(fields * 16, width)],
                axis=0,
            ),
            spread_columns[...],
        )
        own = whole[: fields * rows].reshape(fields, rows, width)
        far = whole[fields * rows :].reshape(fields, 16, width)
        far = jnp.where(band == 0, far[:, :8], far[:, 8:])
        for c in range(across):
            lines[slot, :, c, :rows] = own[:, :, columns(c)]
            lines[slot, :, c, rows:] = jnp.where(keep[:, columns(c)], far[:, :, columns(c)], 0.0)
        return carry

    lax.fori_loop(0, slots, lay_out, 0)

    def step(x):
        west = [pltpu.roll(x[across - 1], 1, 2)] + x[:-1]
        east = x[1:] + [pltpu.roll(x[0], TILE_COLS - 1, 2)]
        south = [
            jnp.concatenate([pltpu.roll(v[layers - 1 :], 1, 1), v[: layers - 1]], axis=0) for v in x
        ]
        north = [jnp.concatenate([v[1:], pltpu.roll(v[:1], 7, 1)], axis=0) for v in x]
        return [
            x[c]
            - winds[0, c] * (x[c] - jnp.where(winds[1, c] > 0.0, west[c], east[c]))
            - winds[2, c] * (x[c] - jnp.where(winds[3, c] > 0.0, south[c], north[c]))
            for c in range(across)
        ]

    def move(index, carry):
        kind = index // (slots // TOGETHER)
        first = TOGETHER * lax.rem(index, slots // TOGETHER)
        fields_of = [lines.at[first + k, kind] for k in range(TOGETHER)]
        xs = [[spread(field, c) for c in range(across)] for field in fields_of]
        for _ in range(STEPS):
            xs = [step(x) for x in xs]
        for k, (field, x) in enumerate(zip(fields_of, xs)):
            for c in range(across):
                for layer in range(layers):
                    field[c, pl.ds(layer, 8, stride=layers), :] = x[c][layer]
                moved[kind, first + k, :, columns(c)] = field[c, :rows].astype(jnp.bfloat16)
        return carry

    def collect(first, last):
        whole = moved[first:last].reshape((last - first) * slots * rows, width)
        whole = permute(whole, gather_columns[...]).astype(jnp.bfloat16)
        advected[first:last] = whole.reshape(last - first, slots, rows, width)

    total = fields * (slots // TOGETHER)
    early, late = 3 * total // 8, 6 * total // 8
    lax.fori_loop(0, slots // TOGETHER, move, 0)
    collect(0, 1)
    lax.fori_loop(slots // TOGETHER, early, move, 0)

    def arrive(d, carry):
        source = near_by(SHARERS - d)
        pltpu.make_async_remote_copy(
            src_ref=obs_send.at[0],
            dst_ref=obs_recv.at[source],
            send_sem=obs_sems.at[0],
            recv_sem=obs_arrived.at[source],
            device_id={"mem": first_rank + source},
            device_id_type=MESH,
        ).wait_recv()
        return carry

    lax.fori_loop(1, SHARERS, arrive, 0)
    obs_recv[rank] = obs_send[rank]
    grids[rank] = functools.reduce(jnp.add, [obs_recv[k] for k in range(SHARERS)])
    for d in range(1, SHARERS):
        grid_out(d).start()

    lax.fori_loop(early, late, move, 0)

    def likely(d, carry):
        source = near_by(d)

        @pl.when(d > 0)
        def _():
            pltpu.make_async_remote_copy(
                src_ref=grids.at[source],
                dst_ref=grids.at[source],
                send_sem=grid_sems.at[0],
                recv_sem=grid_arrived.at[source],
                device_id={"mem": first_rank + source},
                device_id_type=MESH,
            ).wait_recv()

        for k in range(held_tiles):
            down, along = tile(held_tiles * source + k)
            inverse, linear, constant = (grids[source, k, term] for term in range(3))
            for slot in range(slots):
                value = advected[0, slot, down, along].astype(jnp.float32)
                loglik[slot, down, along] = -0.5 * (
                    inverse * value * value - 2.0 * linear * value + constant
                )
        return carry

    lax.fori_loop(0, SHARERS, likely, 0)
    copy_loglik = to_other(loglik.at[:, edge16, :], loglik_halo, 2)
    lax.fori_loop(late, total, move, 0)
    collect(1, fields)

    r0 = lax.broadcasted_iota(jnp.int32, (rows, rows), 0)
    r1 = lax.broadcasted_iota(jnp.int32, (rows, rows), 1)
    own_band = kernel_values(r0 - r1)
    h0 = lax.broadcasted_iota(jnp.int32, (rows, 16), 0)
    h1 = lax.broadcasted_iota(jnp.int32, (rows, 16), 1)
    far_band = kernel_values(jnp.where(band == 0, rows + h1 - h0, h0 + 16 - h1))
    dot = functools.partial(
        jnp.dot, precision=lax.Precision.HIGHEST, preferred_element_type=jnp.float32
    )
    copy_loglik.wait()
    smoothed = jnp.concatenate(
        [
            dot(own_band, loglik[slot]) + dot(far_band, loglik_halo[slot])
            for slot in range(slots)
        ],
        axis=0,
    )
    scores[...] = dot(smoothed, lon_kernel[...]).reshape(slots, rows, width)

    partner = me + 1 - 2 * lax.rem(me, 2)
    parity = lax.rem(me, 2)

    half = n // 2

    def copies(t, slot, target):
        return [
            pltpu.make_async_remote_copy(
                src_ref=source.at[t],
                dst_ref=landing.at[slot],
                send_sem=sent_sems.at[t],
                recv_sem=landed_sems.at[slot],
                device_id={"mem": target},
                device_id_type=MESH,
            )
            for source, landing, sent_sems, landed_sems in (
                (send_log, recv_log, send_log_sems, recv_log_sems),
                (send, recv, send_sems, recv_sems),
            )
        ]

    def outgoing(t):
        return copies(t, me // 2, t)

    def across_pair(t):
        return copies(t, half + t // 2, partner)

    def start_all(made):
        for copy in made:
            copy.start()

    def gather(t):
        down, along = tile(t)
        live = [
            jnp.where(slot < count[0], scores[slot, down, along], -jnp.inf)
            for slot in range(slots)
        ]
        peak = functools.reduce(jnp.maximum, live)
        gains = [jnp.exp(score - peak) for score in live]
        weighted = [
            functools.reduce(
                jnp.add,
                [
                    gains[slot] * advected[kind, slot, down, along].astype(jnp.float32)
                    for slot in range(slots)
                ],
            )
            for kind in range(fields)
        ]
        return weighted, functools.reduce(jnp.add, gains), peak

    def put(t, weighted, total, peak):
        send_log[t] = peak + jnp.log(total)
        inverse = 1.0 / total
        for plane, value in enumerate(encode([value * inverse for value in weighted])):
            send[t, plane] = value

    def hold(t, weighted, total, peak):
        for plane, value in enumerate(weighted + [total, peak]):
            held[t // 2, plane] = value

    def turn(j):
        middle = owners // 2
        other_ones = 2 * j + 2 * jnp.where(2 * j >= middle, 1, 0)
        return jnp.where(j == 0, middle, jnp.where(j == middle - 1, 0, other_ones))

    def give_pair(j, carry):
        t = lax.rem(partner + turn(j), owners)
        put(t, *gather(t))
        start_all(across_pair(t))
        return carry

    def keep_own(j, carry):
        t = 2 * j + parity
        hold(t, *gather(t))
        return carry

    def merge(t, slot):
        low, high = held[t // 2, fields + 1], recv_log[slot]
        peak = jnp.maximum(low, high)
        low, high = jnp.exp(low - peak), jnp.exp(high - peak)
        scaled = high * scale_of(recv[slot, fields])
        weighted = [
            low * held[t // 2, kind] + scaled * integer(recv[slot, kind])
            for kind in range(fields)
        ]
        return weighted, low * held[t // 2, fields] + high, peak

    def give_owner(j, carry):
        t = lax.rem(me + turn(j), owners)
        for copy in across_pair(t):
            copy.wait_recv()
        sums = merge(t, half + t // 2)

        @pl.when(t != me)
        def _():
            put(t, *sums)
            start_all(outgoing(t))

        @pl.when(t == me)
        def _():
            hold(t, *sums)

        return carry

    lax.fori_loop(0, owners // 2, give_pair, 0)
    lax.fori_loop(0, owners // 2, keep_own, 0)
    lax.fori_loop(0, owners // 2, give_owner, 0)

    def back(d):
        return pltpu.make_async_remote_copy(
            src_ref=merged.at[me],
            dst_ref=merged.at[me],
            send_sem=back_send.at[d],
            recv_sem=back_recv.at[me],
            device_id={"mem": lax.rem(me + 2 * d, n)},
            device_id_type=MESH,
        )

    def relay(t):
        return pltpu.make_async_remote_copy(
            src_ref=merged.at[t],
            dst_ref=merged.at[t],
            send_sem=relay_send.at[t],
            recv_sem=back_recv.at[t],
            device_id={"mem": partner},
            device_id_type=MESH,
        )

    @pl.when(me < owners)
    def _():
        def arrive(d, carry):
            source = lax.rem(me + 2 * d, n)
            for copy in copies(0, source // 2, source):
                copy.wait_recv()
            return carry

        lax.fori_loop(1, half, arrive, 0)
        own = me // 2
        peak = lax.fori_loop(
            1,
            half,
            lambda d, top: jnp.maximum(top, recv_log[lax.rem(own + d, half)]),
            held[own, fields + 1],
        )

        def add(d, sums):
            slot = lax.rem(own + d, half)
            factor = jnp.exp(recv_log[slot] - peak)
            scaled = factor * scale_of(recv[slot, fields])
            return tuple(
                sums[kind] + scaled * integer(recv[slot, kind]) for kind in range(fields)
            ) + (sums[fields] + factor,)

        factor = jnp.exp(held[own, fields + 1] - peak)
        sums = lax.fori_loop(
            1, half, add, tuple(factor * held[own, plane] for plane in range(fields + 1))
        )
        inverse = 1.0 / sums[fields]
        for plane, value in enumerate(encode([sums[kind] * inverse for kind in range(fields)])):
            merged[me, plane] = value

        def start(d, carry):
            back(d).start()
            return carry

        lax.fori_loop(1, n // 2, start, 0)

    def landed(t):
        @pl.when(t != me)
        def _():
            relay(t).wait_recv()

    def pass_on(j, carry):
        t = lax.rem(me + owners - 2 * j, owners)
        landed(t)
        relay(t).start()
        finish(t)
        return carry

    def accept(j, carry):
        t = lax.rem(partner + owners - 2 * j, owners)
        landed(t)
        finish(t)
        return carry

    def finish(t):
        down, along = tile(t)
        scale = scale_of(merged[t, fields])
        for kind in range(fields):
            mean = scale * integer(merged[t, kind])
            mean_ref[kind, down, along] = mean.astype(jnp.bfloat16)
            for slot in range(slots):
                value = advected[kind, slot, down, along].astype(jnp.float32)
                fresh = value + factors[kind] * (mean - value)
                out_ref[slot, kind, down, along] = jnp.where(
                    slot < count[0], fresh, 0.0
                ).astype(jnp.bfloat16)

    lax.fori_loop(0, owners // 2, pass_on, 0)
    lax.fori_loop(0, owners // 2, accept, 0)

    for d in range(1, SHARERS):
        obs_out(d).wait_send()
        grid_out(d).wait_send()

    def passed(j, carry):
        for copy in across_pair(2 * j + 1 - parity):
            copy.wait_send()

        @pl.when(2 * j + parity != me)
        def _():
            for copy in outgoing(2 * j + parity):
                copy.wait_send()

        relay(2 * j + parity).wait_send()
        return carry

    lax.fori_loop(0, owners // 2, passed, 0)

    @pl.when(me < owners)
    def _():
        def sent_back(d, carry):
            back(d).wait_send()
            return carry

        lax.fori_loop(1, n // 2, sent_back, 0)


def cycle(n, state, counts, east_wind, north_wind, obs, relax):
    slots, fields, rows, width = state.shape
    across = width // TILE_COLS
    owners = (rows // TILE_ROWS) * across
    share = obs[0].shape[1] // SHARERS
    held_tiles = owners // SHARERS
    tile = (TILE_ROWS, TILE_COLS)
    hbm = pl.BlockSpec(memory_space=pl.ANY)
    vmem = pl.BlockSpec(memory_space=pltpu.VMEM)
    f32, bf16 = jnp.float32, jnp.bfloat16
    return pl.pallas_call(
        functools.partial(cycle_kernel, n),
        out_shape=(
            pltpu.VMEM(state.shape, bf16),
            pltpu.VMEM((fields, rows, width), bf16),
        ),
        in_specs=[hbm] * 9,
        out_specs=(vmem, vmem),
        scratch_shapes=[
            pltpu.VMEM((1, share), jnp.int32),
            pltpu.VMEM((1, share), jnp.int32),
            pltpu.VMEM((1, share), f32),
            pltpu.VMEM((1, share), f32),
            pltpu.VMEM(state.shape, bf16),
            pltpu.SMEM(counts.shape, counts.dtype),
            pltpu.SMEM(relax.shape, relax.dtype),
            pltpu.VMEM((3, rows, width), f32),
            pltpu.VMEM((SHARERS, held_tiles, 3) + tile, f32),
            pltpu.VMEM((SHARERS, held_tiles, 3) + tile, f32),
            pltpu.VMEM((SHARERS, held_tiles, 3) + tile, f32),
            pltpu.VMEM((slots, fields, 16, width), bf16),
            pltpu.VMEM((2, rows, width), f32),
            pltpu.VMEM((2, 8, width), f32),
            pltpu.VMEM((4, across, (rows + 8) // 8, 8, TILE_COLS), f32),
            pltpu.VMEM((width, width), bf16),
            pltpu.VMEM((width, width), bf16),
            pltpu.VMEM((slots, fields, across, rows + 8, TILE_COLS), f32),
            pltpu.VMEM((fields, slots, rows, width), bf16),
            pltpu.VMEM((fields, slots, rows, width), bf16),
            pltpu.VMEM((width, width), f32),
            pltpu.VMEM((slots, rows, width), f32),
            pltpu.VMEM((slots, 16, width), f32),
            pltpu.VMEM((slots, rows, width), f32),
            pltpu.VMEM((owners // 2, fields + 2) + tile, f32),
            pltpu.VMEM((owners, fields + 1) + tile, jnp.int16),
            pltpu.VMEM((owners,) + tile, f32),
            pltpu.VMEM((n // 2 + owners // 2, fields + 1) + tile, jnp.int16),
            pltpu.VMEM((n // 2 + owners // 2,) + tile, f32),
            pltpu.VMEM((owners, fields + 1) + tile, jnp.int16),
            pltpu.SemaphoreType.DMA((2, 3)),
            pltpu.SemaphoreType.DMA((owners,)),
            pltpu.SemaphoreType.DMA((n // 2 + owners // 2,)),
            pltpu.SemaphoreType.DMA((owners,)),
            pltpu.SemaphoreType.DMA((n // 2 + owners // 2,)),
            pltpu.SemaphoreType.DMA((n,)),
            pltpu.SemaphoreType.DMA((owners,)),
            pltpu.SemaphoreType.DMA((owners,)),
            pltpu.SemaphoreType.DMA((9,)),
            pltpu.SemaphoreType.DMA((SHARERS,)),
            pltpu.SemaphoreType.DMA((SHARERS,)),
            pltpu.SemaphoreType.DMA((SHARERS,)),
            pltpu.SemaphoreType.DMA((SHARERS,)),
        ],
        compiler_params=pltpu.CompilerParams(
            collective_id=0, has_side_effects=True, vmem_limit_bytes=56 * 1024 * 1024
        ),
    )(state, counts, east_wind, north_wind, *obs, relax)


def write_kernel(fresh, mean, out, mean_out, sems):
    copies = [
        pltpu.make_async_copy(fresh, out, sems.at[0]),
        pltpu.make_async_copy(mean, mean_out, sems.at[1]),
    ]
    for copy in copies:
        copy.start()
    for copy in copies:
        copy.wait()


def write_out(fresh, mean):
    hbm = pl.BlockSpec(memory_space=pl.ANY)
    return pl.pallas_call(
        write_kernel,
        out_shape=(
            jax.ShapeDtypeStruct(fresh.shape, fresh.dtype),
            jax.ShapeDtypeStruct(mean.shape, mean.dtype),
        ),
        in_specs=[hbm, hbm],
        out_specs=(hbm, hbm),
        scratch_shapes=[pltpu.SemaphoreType.DMA((2,))],
    )(*(pltpu.with_memory_space_constraint(x, pltpu.VMEM) for x in (fresh, mean)))


def on_device(
    n, state, counts, east_wind, north_wind, obs_cells, obs_mask, obs_values, obs_error, relax
):
    obs = (obs_cells, obs_mask, obs_values, obs_error)
    fresh, mean = cycle(n, state, counts, east_wind, north_wind, obs, relax)
    return write_out(fresh, mean)


def solution(mesh):
    return jax.shard_map(
        functools.partial(on_device, mesh.shape["mem"]),
        mesh=mesh,
        in_specs=(
            P(("groups", "mem"), None, "lat", None),
            P(("groups", "mem")),
            P(("groups", "lat"), None),
            P(("groups", "lat"), None),
            P(("groups", "lat"), None),
            P(("groups", "lat"), None),
            P(("groups", "lat"), None),
            P(("groups", "lat"), None),
            P(),
        ),
        out_specs=(P(("groups", "mem"), None, "lat", None), P("groups", "lat", None)),
        check_vma=False,
    )
```

```python
import functools
import math

import jax
import jax.numpy as jnp
from jax import lax
from jax.experimental import pallas as pl
from jax.experimental.pallas import tpu as pltpu
from jax.sharding import PartitionSpec as P

STEPS = 4
SMOOTH = 16
LOG_TWO_PI = 1.8378770664093453
MESH = pl.DeviceIdType.MESH
TILE_ROWS = 16
TILE_COLS = 128
OBS_BLOCK = 2048
TOGETHER = 4
SHARERS = 4
LEVELS = 32760.0
OCTAVE = 128.0
TINY = 1e-33


def pieces(values):
    high = values.astype(jnp.bfloat16).astype(jnp.float32)
    rest = values - high
    mid = rest.astype(jnp.bfloat16).astype(jnp.float32)
    return high, mid, rest - mid


def partial_grids(rows, width, cells, mask, values, error):
    count = cells.shape[1]
    used = mask.astype(jnp.float32)
    inverse = used / (error * error)
    terms = (
        inverse,
        inverse * values,
        inverse * values * values + used * (2.0 * jnp.log(error) + LOG_TWO_PI),
    )
    row = cells // width
    column = cells - row * width
    row_hit = lax.broadcasted_iota(jnp.int32, (rows, count), 0) == row
    column_hit = jnp.where(
        lax.broadcasted_iota(jnp.int32, (width, count), 0) == column, 1.0, 0.0
    ).astype(jnp.bfloat16)
    left = jnp.concatenate(
        [
            jnp.where(row_hit, piece, 0.0).astype(jnp.bfloat16)
            for piece in pieces(terms[0]) + pieces(terms[1]) + pieces(terms[2])[:2]
        ],
        axis=0,
    )
    return lax.dot_general(
        left, column_hit, (((1,), (1,)), ((), ())), preferred_element_type=jnp.float32
    )


def one_hot(hit):
    return jnp.where(hit, 1.0, 0.0).astype(jnp.bfloat16)


def permute(values, matrix):
    return jnp.dot(values, matrix, preferred_element_type=jnp.float32)


def kernel_values(offset):
    values = jnp.exp(-((2.0 * offset.astype(jnp.float32) / SMOOTH) ** 2))
    return jnp.where(jnp.abs(offset) <= SMOOTH, values, 0.0)


def encode(means):
    top = functools.reduce(jnp.maximum, [jnp.abs(mean) for mean in means])
    code = jnp.ceil(jnp.log(jnp.maximum(top, TINY)) * (OCTAVE / math.log(2.0))) + 1.0
    levels = LEVELS * jnp.exp(code * (-math.log(2.0) / OCTAVE))
    whole = [jnp.floor(mean * levels + 0.5) for mean in means] + [code]
    return [value.astype(jnp.int32).astype(jnp.int16) for value in whole]


def integer(ref):
    return ref.astype(jnp.int32).astype(jnp.float32)


def scale_of(code):
    return jnp.exp(integer(code) * (math.log(2.0) / OCTAVE)) * (1.0 / LEVELS)


def cycle_kernel(
    n,
    state_ref,
    counts_ref,
    east_ref,
    north_ref,
    cells_ref,
    mask_ref,
    values_ref,
    error_ref,
    relax_ref,
    out_ref,
    mean_ref,
    cells,
    mask,
    values,
    error,
    state,
    count,
    factors,
    counted,
    obs_send,
    obs_recv,
    grids,
    halo,
    wind_in,
    wind_halo,
    winds,
    spread_columns,
    gather_columns,
    lines,
    moved,
    advected,
    lon_kernel,
    loglik,
    loglik_halo,
    scores,
    held,
    send,
    send_log,
    recv,
    recv_log,
    merged,
    halo_sems,
    send_sems,
    recv_sems,
    send_log_sems,
    recv_log_sems,
    back_send,
    back_recv,
    relay_send,
    local_sems,
    obs_sems,
    obs_arrived,
    grid_sems,
    grid_arrived,
):
    slots, fields, rows, width = state_ref.shape
    across = width // TILE_COLS
    owners = (rows // TILE_ROWS) * across
    me = lax.axis_index("mem")
    band = lax.axis_index("lat")
    other = 1 - band

    share = cells.shape[1]
    rank = lax.rem(me, SHARERS)
    first_rank = me - rank
    mine = pl.ds(pl.multiple_of(rank * share, 128), share)
    loads = [
        pltpu.make_async_copy(source, target, local_sems.at[k])
        for k, (source, target) in enumerate(
            (
                (cells_ref.at[:, mine], cells),
                (mask_ref.at[:, mine], mask),
                (values_ref.at[:, mine], values),
                (error_ref.at[:, mine], error),
                (state_ref, state),
                (east_ref, wind_in.at[0]),
                (north_ref, wind_in.at[1]),
                (counts_ref, count),
                (relax_ref, factors),
            )
        )
    ]
    for load in loads:
        load.start()

    barrier = pltpu.get_barrier_semaphore()

    def greet(d, carry):
        pl.semaphore_signal(
            barrier, inc=1, device_id={"mem": lax.rem(me + d, n)}, device_id_type=MESH
        )
        return carry

    pl.semaphore_signal(barrier, inc=1, device_id={"lat": other}, device_id_type=MESH)
    lax.fori_loop(1, n, greet, 0)

    for load in loads[5:]:
        load.wait()
    pl.semaphore_wait(barrier, n)

    def to_other(source, target, slot):
        copy = pltpu.make_async_remote_copy(
            src_ref=source,
            dst_ref=target,
            send_sem=halo_sems.at[0, slot],
            recv_sem=halo_sems.at[1, slot],
            device_id={"lat": other},
            device_id_type=MESH,
        )
        copy.start()
        return copy

    edge16 = pl.ds(pl.multiple_of(other * (rows - 16), 16), 16)
    edge8 = pl.ds(pl.multiple_of(other * (rows - 8), 8), 8)
    copy_winds = to_other(wind_in.at[:, edge8, :], wind_halo, 0)
    copy_state = to_other(state_ref.at[:, :, edge16, :], halo, 1)

    def tile(t):
        down = t // across
        return (
            pl.ds(pl.multiple_of(down * TILE_ROWS, TILE_ROWS), TILE_ROWS),
            pl.ds(pl.multiple_of((t - down * across) * TILE_COLS, TILE_COLS), TILE_COLS),
        )

    for load in loads[:4]:
        load.wait()
    block = min(share, OBS_BLOCK)

    def count_block(index, carry):
        at = pl.ds(pl.multiple_of(index * block, 128), block)
        part = partial_grids(rows, width, *(ref[:, at] for ref in (cells, mask, values, error)))
        for term, (base, number) in enumerate(((0, 3), (3, 3), (6, 2))):
            counted[term] += functools.reduce(
                jnp.add, [part[(base + k) * rows : (base + k + 1) * rows] for k in range(number)]
            )
        return carry

    counted[...] = jnp.zeros_like(counted)
    lax.fori_loop(0, share // block, count_block, 0)
    held_tiles = owners // SHARERS

    def near_by(d):
        return lax.rem(rank + d, SHARERS)

    def obs_out(d):
        return pltpu.make_async_remote_copy(
            src_ref=obs_send.at[near_by(d)],
            dst_ref=obs_recv.at[rank],
            send_sem=obs_sems.at[near_by(d)],
            recv_sem=obs_arrived.at[rank],
            device_id={"mem": first_rank + near_by(d)},
            device_id_type=MESH,
        )

    def give(d, carry):
        for k in range(held_tiles):
            down, along = tile(held_tiles * near_by(d) + k)
            for term in range(3):
                obs_send[near_by(d), k, term] = counted[term, down, along]

        @pl.when(d < SHARERS)
        def _():
            obs_out(d).start()

        return carry

    lax.fori_loop(1, SHARERS + 1, give, 0)

    def grid_out(d):
        return pltpu.make_async_remote_copy(
            src_ref=grids.at[rank],
            dst_ref=grids.at[rank],
            send_sem=grid_sems.at[d],
            recv_sem=grid_arrived.at[rank],
            device_id={"mem": first_rank + near_by(d)},
            device_id_type=MESH,
        )

    i0 = lax.broadcasted_iota(jnp.int32, (width, width), 0)
    i1 = lax.broadcasted_iota(jnp.int32, (width, width), 1)
    spread_columns[...] = one_hot(i0 == across * lax.rem(i1, TILE_COLS) + i1 // TILE_COLS)
    gather_columns[...] = one_hot(i1 == across * lax.rem(i0, TILE_COLS) + i0 // TILE_COLS)
    apart = jnp.abs(i0 - i1)
    lon_kernel[...] = kernel_values(jnp.minimum(apart, width - apart))

    near = lax.broadcasted_iota(jnp.int32, (8, width), 0)
    keep = jnp.where(band == 0, near, 7 - near) < STEPS

    layers = (rows + 8) // 8

    def columns(c):
        return slice(c * TILE_COLS, (c + 1) * TILE_COLS)

    def spread(ref, c):
        return jnp.stack([ref[c, pl.ds(k, 8, stride=layers), :] for k in range(layers)])

    copy_winds.wait()
    split = []
    for kind in range(2):
        far = jnp.where(keep, wind_halo[kind], 0.0)
        split += pieces(jnp.concatenate([wind_in[kind], far], axis=0))
    split = permute(
        jnp.concatenate([piece.astype(jnp.bfloat16) for piece in split], axis=0),
        spread_columns[...],
    ).reshape(2, 3, rows + 8, width)
    for kind in range(2):
        whole = (split[kind, 0] + split[kind, 1]) + split[kind, 2]
        for c in range(across):
            lines[0, kind, c] = whole[:, columns(c)]
            wind = spread(lines.at[0, kind], c)
            winds[2 * kind, c] = jnp.abs(wind)
            winds[2 * kind + 1, c] = wind
    loads[4].wait()
    copy_state.wait()

    def lay_out(slot, carry):
        whole = permute(
            jnp.concatenate(
                [state[slot].reshape(fields * rows, width), halo[slot].reshape(fields * 16, width)],
                axis=0,
            ),
            spread_columns[...],
        )
        own = whole[: fields * rows].reshape(fields, rows, width)
        far = whole[fields * rows :].reshape(fields, 16, width)
        far = jnp.where(band == 0, far[:, :8], far[:, 8:])
        for c in range(across):
            lines[slot, :, c, :rows] = own[:, :, columns(c)]
            lines[slot, :, c, rows:] = jnp.where(keep[:, columns(c)], far[:, :, columns(c)], 0.0)
        return carry

    lax.fori_loop(0, slots, lay_out, 0)

    def step(x):
        west = [pltpu.roll(x[across - 1], 1, 2)] + x[:-1]
        east = x[1:] + [pltpu.roll(x[0], TILE_COLS - 1, 2)]
        south = [
            jnp.concatenate([pltpu.roll(v[layers - 1 :], 1, 1), v[: layers - 1]], axis=0) for v in x
        ]
        north = [jnp.concatenate([v[1:], pltpu.roll(v[:1], 7, 1)], axis=0) for v in x]
        return [
            x[c]
            - winds[0, c] * (x[c] - jnp.where(winds[1, c] > 0.0, west[c], east[c]))
            - winds[2, c] * (x[c] - jnp.where(winds[3, c] > 0.0, south[c], north[c]))
            for c in range(across)
        ]

    def move(index, carry):
        kind = index // (slots // TOGETHER)
        first = TOGETHER * lax.rem(index, slots // TOGETHER)
        fields_of = [lines.at[first + k, kind] for k in range(TOGETHER)]
        xs = [[spread(field, c) for c in range(across)] for field in fields_of]
        for _ in range(STEPS):
            xs = [step(x) for x in xs]
        for k, (field, x) in enumerate(zip(fields_of, xs)):
            for c in range(across):
                for layer in range(layers):
                    field[c, pl.ds(layer, 8, stride=layers), :] = x[c][layer]
                moved[kind, first + k, :, columns(c)] = field[c, :rows].astype(jnp.bfloat16)
        return carry

    def collect(first, last):
        whole = moved[first:last].reshape((last - first) * slots * rows, width)
        whole = permute(whole, gather_columns[...]).astype(jnp.bfloat16)
        advected[first:last] = whole.reshape(last - first, slots, rows, width)

    total = fields * (slots // TOGETHER)
    early, late = total // 8, 7 * total // 8
    lax.fori_loop(0, slots // TOGETHER, move, 0)
    collect(0, 1)
    lax.fori_loop(slots // TOGETHER, early, move, 0)

    def arrive(d, carry):
        source = near_by(SHARERS - d)
        pltpu.make_async_remote_copy(
            src_ref=obs_send.at[0],
            dst_ref=obs_recv.at[source],
            send_sem=obs_sems.at[0],
            recv_sem=obs_arrived.at[source],
            device_id={"mem": first_rank + source},
            device_id_type=MESH,
        ).wait_recv()
        return carry

    lax.fori_loop(1, SHARERS, arrive, 0)
    obs_recv[rank] = obs_send[rank]
    grids[rank] = functools.reduce(jnp.add, [obs_recv[k] for k in range(SHARERS)])
    for d in range(1, SHARERS):
        grid_out(d).start()

    lax.fori_loop(early, late, move, 0)

    def likely(d, carry):
        source = near_by(d)

        @pl.when(d > 0)
        def _():
            pltpu.make_async_remote_copy(
                src_ref=grids.at[source],
                dst_ref=grids.at[source],
                send_sem=grid_sems.at[0],
                recv_sem=grid_arrived.at[source],
                device_id={"mem": first_rank + source},
                device_id_type=MESH,
            ).wait_recv()

        for k in range(held_tiles):
            down, along = tile(held_tiles * source + k)
            inverse, linear, constant = (grids[source, k, term] for term in range(3))
            for slot in range(slots):
                value = advected[0, slot, down, along].astype(jnp.float32)
                loglik[slot, down, along] = -0.5 * (
                    inverse * value * value - 2.0 * linear * value + constant
                )
        return carry

    lax.fori_loop(0, SHARERS, likely, 0)
    copy_loglik = to_other(loglik.at[:, edge16, :], loglik_halo, 2)
    lax.fori_loop(late, total, move, 0)
    collect(1, fields)

    r0 = lax.broadcasted_iota(jnp.int32, (rows, rows), 0)
    r1 = lax.broadcasted_iota(jnp.int32, (rows, rows), 1)
    own_band = kernel_values(r0 - r1)
    h0 = lax.broadcasted_iota(jnp.int32, (rows, 16), 0)
    h1 = lax.broadcasted_iota(jnp.int32, (rows, 16), 1)
    far_band = kernel_values(jnp.where(band == 0, rows + h1 - h0, h0 + 16 - h1))
    dot = functools.partial(
        jnp.dot, precision=lax.Precision.HIGHEST, preferred_element_type=jnp.float32
    )
    copy_loglik.wait()
    smoothed = jnp.concatenate(
        [
            dot(own_band, loglik[slot]) + dot(far_band, loglik_halo[slot])
            for slot in range(slots)
        ],
        axis=0,
    )
    scores[...] = dot(smoothed, lon_kernel[...]).reshape(slots, rows, width)

    partner = me + 1 - 2 * lax.rem(me, 2)
    parity = lax.rem(me, 2)

    half = n // 2

    def copies(t, slot, target):
        return [
            pltpu.make_async_remote_copy(
                src_ref=source.at[t],
                dst_ref=landing.at[slot],
                send_sem=sent_sems.at[t],
                recv_sem=landed_sems.at[slot],
                device_id={"mem": target},
                device_id_type=MESH,
            )
            for source, landing, sent_sems, landed_sems in (
                (send_log, recv_log, send_log_sems, recv_log_sems),
                (send, recv, send_sems, recv_sems),
            )
        ]

    def outgoing(t):
        return copies(t, me // 2, t)

    def across_pair(t):
        return copies(t, half + t // 2, partner)

    def start_all(made):
        for copy in made:
            copy.start()

    def gather(t):
        down, along = tile(t)
        live = [
            jnp.where(slot < count[0], scores[slot, down, along], -jnp.inf)
            for slot in range(slots)
        ]
        peak = functools.reduce(jnp.maximum, live)
        gains = [jnp.exp(score - peak) for score in live]
        weighted = [
            functools.reduce(
                jnp.add,
                [
                    gains[slot] * advected[kind, slot, down, along].astype(jnp.float32)
                    for slot in range(slots)
                ],
            )
            for kind in range(fields)
        ]
        return weighted, functools.reduce(jnp.add, gains), peak

    def put(t, weighted, total, peak):
        send_log[t] = peak + jnp.log(total)
        inverse = 1.0 / total
        for plane, value in enumerate(encode([value * inverse for value in weighted])):
            send[t, plane] = value

    def hold(t, weighted, total, peak):
        for plane, value in enumerate(weighted + [total, peak]):
            held[t // 2, plane] = value

    middle = owners // 2
    place = lax.rem(me // 2, middle)

    def near_to_far(k):
        ups, downs = middle - 1 - place, place
        both = jnp.minimum(ups, downs)
        upward = jnp.where(ups > downs, k - both, 0 - (k - both))
        paired = jnp.where(lax.rem(k, 2) == 1, (k + 1) // 2, 0 - (k // 2))
        return lax.rem(jnp.where(k <= 2 * both, paired, upward) + middle, middle)

    def turn(j):
        return 2 * near_to_far(middle - 1 - j)

    def give_pair(j, carry):
        t = lax.rem(partner + turn(j), owners)
        put(t, *gather(t))
        start_all(across_pair(t))
        return carry

    def keep_own(j, carry):
        t = 2 * j + parity
        hold(t, *gather(t))
        return carry

    def merge(t, slot):
        low, high = held[t // 2, fields + 1], recv_log[slot]
        peak = jnp.maximum(low, high)
        low, high = jnp.exp(low - peak), jnp.exp(high - peak)
        scaled = high * scale_of(recv[slot, fields])
        weighted = [
            low * held[t // 2, kind] + scaled * integer(recv[slot, kind])
            for kind in range(fields)
        ]
        return weighted, low * held[t // 2, fields] + high, peak

    def give_owner(j, carry):
        t = lax.rem(me + turn(j), owners)
        for copy in across_pair(t):
            copy.wait_recv()
        sums = merge(t, half + t // 2)

        @pl.when(t != me)
        def _():
            put(t, *sums)
            start_all(outgoing(t))

        @pl.when(t == me)
        def _():
            hold(t, *sums)

        return carry

    lax.fori_loop(0, owners // 2, give_pair, 0)
    lax.fori_loop(0, owners // 2, keep_own, 0)
    lax.fori_loop(0, owners // 2, give_owner, 0)

    def back(d):
        return pltpu.make_async_remote_copy(
            src_ref=merged.at[me],
            dst_ref=merged.at[me],
            send_sem=back_send.at[d],
            recv_sem=back_recv.at[me],
            device_id={"mem": lax.rem(me + 2 * d, n)},
            device_id_type=MESH,
        )

    def relay(t):
        return pltpu.make_async_remote_copy(
            src_ref=merged.at[t],
            dst_ref=merged.at[t],
            send_sem=relay_send.at[t],
            recv_sem=back_recv.at[t],
            device_id={"mem": partner},
            device_id_type=MESH,
        )

    @pl.when(me < owners)
    def _():
        def arrive(d, carry):
            source = lax.rem(me + 2 * d, n)
            for copy in copies(0, source // 2, source):
                copy.wait_recv()
            return carry

        lax.fori_loop(1, half, arrive, 0)
        own = me // 2
        peak = lax.fori_loop(
            1,
            half,
            lambda d, top: jnp.maximum(top, recv_log[lax.rem(own + d, half)]),
            held[own, fields + 1],
        )

        def add(d, sums):
            slot = lax.rem(own + d, half)
            factor = jnp.exp(recv_log[slot] - peak)
            scaled = factor * scale_of(recv[slot, fields])
            return tuple(
                sums[kind] + scaled * integer(recv[slot, kind]) for kind in range(fields)
            ) + (sums[fields] + factor,)

        factor = jnp.exp(held[own, fields + 1] - peak)
        sums = lax.fori_loop(
            1, half, add, tuple(factor * held[own, plane] for plane in range(fields + 1))
        )
        inverse = 1.0 / sums[fields]
        for plane, value in enumerate(encode([sums[kind] * inverse for kind in range(fields)])):
            merged[me, plane] = value

        def start(d, carry):
            back(d).start()
            return carry

        lax.fori_loop(1, half, start, 0)

    def landed(t):
        @pl.when(t != me)
        def _():
            relay(t).wait_recv()

    def place_of(start, k):
        return lax.rem(start + 2 * near_to_far(k), owners)

    def pass_on(k, carry):
        t = place_of(me, k)
        landed(t)
        relay(t).start()
        return carry

    def finish_passed(k, carry):
        finish(place_of(me, k))
        return carry

    def accept(k, carry):
        t = place_of(partner, k)
        landed(t)
        finish(t)
        return carry

    def finish(t):
        down, along = tile(t)
        scale = scale_of(merged[t, fields])
        for kind in range(fields):
            mean = scale * integer(merged[t, kind])
            mean_ref[kind, down, along] = mean.astype(jnp.bfloat16)
            for slot in range(slots):
                value = advected[kind, slot, down, along].astype(jnp.float32)
                fresh = value + factors[kind] * (mean - value)
                out_ref[slot, kind, down, along] = jnp.where(
                    slot < count[0], fresh, 0.0
                ).astype(jnp.bfloat16)

    for d in range(1, SHARERS):
        obs_out(d).wait_send()
        grid_out(d).wait_send()

    def passed(j, carry):
        for copy in across_pair(2 * j + 1 - parity):
            copy.wait_send()

        @pl.when(2 * j + parity != me)
        def _():
            for copy in outgoing(2 * j + parity):
                copy.wait_send()

        return carry

    lax.fori_loop(0, owners // 2, passed, 0)
    pass_on(0, 0)
    finish(place_of(me, 0))
    lax.fori_loop(1, middle, pass_on, 0)
    lax.fori_loop(1, middle, finish_passed, 0)
    lax.fori_loop(0, middle, accept, 0)

    def relayed(j, carry):
        relay(2 * j + parity).wait_send()
        return carry

    lax.fori_loop(0, middle, relayed, 0)

    @pl.when(me < owners)
    def _():
        def sent_back(d, carry):
            back(d).wait_send()
            return carry

        lax.fori_loop(1, n // 2, sent_back, 0)


def cycle(n, state, counts, east_wind, north_wind, obs, relax):
    slots, fields, rows, width = state.shape
    across = width // TILE_COLS
    owners = (rows // TILE_ROWS) * across
    share = obs[0].shape[1] // SHARERS
    held_tiles = owners // SHARERS
    tile = (TILE_ROWS, TILE_COLS)
    hbm = pl.BlockSpec(memory_space=pl.ANY)
    vmem = pl.BlockSpec(memory_space=pltpu.VMEM)
    f32, bf16 = jnp.float32, jnp.bfloat16
    return pl.pallas_call(
        functools.partial(cycle_kernel, n),
        out_shape=(
            pltpu.VMEM(state.shape, bf16),
            pltpu.VMEM((fields, rows, width), bf16),
        ),
        in_specs=[hbm] * 9,
        out_specs=(vmem, vmem),
        scratch_shapes=[
            pltpu.VMEM((1, share), jnp.int32),
            pltpu.VMEM((1, share), jnp.int32),
            pltpu.VMEM((1, share), f32),
            pltpu.VMEM((1, share), f32),
            pltpu.VMEM(state.shape, bf16),
            pltpu.SMEM(counts.shape, counts.dtype),
            pltpu.SMEM(relax.shape, relax.dtype),
            pltpu.VMEM((3, rows, width), f32),
            pltpu.VMEM((SHARERS, held_tiles, 3) + tile, f32),
            pltpu.VMEM((SHARERS, held_tiles, 3) + tile, f32),
            pltpu.VMEM((SHARERS, held_tiles, 3) + tile, f32),
            pltpu.VMEM((slots, fields, 16, width), bf16),
            pltpu.VMEM((2, rows, width), f32),
            pltpu.VMEM((2, 8, width), f32),
            pltpu.VMEM((4, across, (rows + 8) // 8, 8, TILE_COLS), f32),
            pltpu.VMEM((width, width), bf16),
            pltpu.VMEM((width, width), bf16),
            pltpu.VMEM((slots, fields, across, rows + 8, TILE_COLS), f32),
            pltpu.VMEM((fields, slots, rows, width), bf16),
            pltpu.VMEM((fields, slots, rows, width), bf16),
            pltpu.VMEM((width, width), f32),
            pltpu.VMEM((slots, rows, width), f32),
            pltpu.VMEM((slots, 16, width), f32),
            pltpu.VMEM((slots, rows, width), f32),
            pltpu.VMEM((owners // 2, fields + 2) + tile, f32),
            pltpu.VMEM((owners, fields + 1) + tile, jnp.int16),
            pltpu.VMEM((owners,) + tile, f32),
            pltpu.VMEM((n // 2 + owners // 2, fields + 1) + tile, jnp.int16),
            pltpu.VMEM((n // 2 + owners // 2,) + tile, f32),
            pltpu.VMEM((owners, fields + 1) + tile, jnp.int16),
            pltpu.SemaphoreType.DMA((2, 3)),
            pltpu.SemaphoreType.DMA((owners,)),
            pltpu.SemaphoreType.DMA((n // 2 + owners // 2,)),
            pltpu.SemaphoreType.DMA((owners,)),
            pltpu.SemaphoreType.DMA((n // 2 + owners // 2,)),
            pltpu.SemaphoreType.DMA((n,)),
            pltpu.SemaphoreType.DMA((owners,)),
            pltpu.SemaphoreType.DMA((owners,)),
            pltpu.SemaphoreType.DMA((9,)),
            pltpu.SemaphoreType.DMA((SHARERS,)),
            pltpu.SemaphoreType.DMA((SHARERS,)),
            pltpu.SemaphoreType.DMA((SHARERS,)),
            pltpu.SemaphoreType.DMA((SHARERS,)),
        ],
        compiler_params=pltpu.CompilerParams(
            collective_id=0, has_side_effects=True, vmem_limit_bytes=56 * 1024 * 1024
        ),
    )(state, counts, east_wind, north_wind, *obs, relax)


def write_kernel(fresh, mean, out, mean_out, sems):
    copies = [
        pltpu.make_async_copy(fresh, out, sems.at[0]),
        pltpu.make_async_copy(mean, mean_out, sems.at[1]),
    ]
    for copy in copies:
        copy.start()
    for copy in copies:
        copy.wait()


def write_out(fresh, mean):
    hbm = pl.BlockSpec(memory_space=pl.ANY)
    return pl.pallas_call(
        write_kernel,
        out_shape=(
            jax.ShapeDtypeStruct(fresh.shape, fresh.dtype),
            jax.ShapeDtypeStruct(mean.shape, mean.dtype),
        ),
        in_specs=[hbm, hbm],
        out_specs=(hbm, hbm),
        scratch_shapes=[pltpu.SemaphoreType.DMA((2,))],
    )(*(pltpu.with_memory_space_constraint(x, pltpu.VMEM) for x in (fresh, mean)))


def on_device(
    n, state, counts, east_wind, north_wind, obs_cells, obs_mask, obs_values, obs_error, relax
):
    obs = (obs_cells, obs_mask, obs_values, obs_error)
    fresh, mean = cycle(n, state, counts, east_wind, north_wind, obs, relax)
    return write_out(fresh, mean)


def solution(mesh):
    return jax.shard_map(
        functools.partial(on_device, mesh.shape["mem"]),
        mesh=mesh,
        in_specs=(
            P(("groups", "mem"), None, "lat", None),
            P(("groups", "mem")),
            P(("groups", "lat"), None),
            P(("groups", "lat"), None),
            P(("groups", "lat"), None),
            P(("groups", "lat"), None),
            P(("groups", "lat"), None),
            P(("groups", "lat"), None),
            P(),
        ),
        out_specs=(P(("groups", "mem"), None, "lat", None), P("groups", "lat", None)),
        check_vma=False,
    )
```

```python
import functools
import math

import jax
import jax.numpy as jnp
from jax import lax
from jax.experimental import pallas as pl
from jax.experimental.pallas import tpu as pltpu
from jax.sharding import PartitionSpec as P

STEPS = 4
SMOOTH = 16
LOG_TWO_PI = 1.8378770664093453
MESH = pl.DeviceIdType.MESH
TILE_ROWS = 16
TILE_COLS = 128
OBS_BLOCK = 4096
TOGETHER = 4
SHARERS = 4
LEVELS = 32760.0
OCTAVE = 128.0
TINY = 1e-33


def pieces(values):
    high = values.astype(jnp.bfloat16).astype(jnp.float32)
    rest = values - high
    mid = rest.astype(jnp.bfloat16).astype(jnp.float32)
    return high, mid, rest - mid


def partial_grids(rows, width, cells, mask, values, error):
    count = cells.shape[1]
    used = mask.astype(jnp.float32)
    inverse = used / (error * error)
    terms = (
        inverse,
        inverse * values,
        inverse * values * values + used * (2.0 * jnp.log(error) + LOG_TWO_PI),
    )
    row = cells // width
    column = cells - row * width
    row_hit = lax.broadcasted_iota(jnp.int32, (rows, count), 0) == row
    column_hit = jnp.where(
        lax.broadcasted_iota(jnp.int32, (width, count), 0) == column, 1.0, 0.0
    ).astype(jnp.bfloat16)
    left = jnp.concatenate(
        [
            jnp.where(row_hit, piece, 0.0).astype(jnp.bfloat16)
            for piece in pieces(terms[0]) + pieces(terms[1]) + pieces(terms[2])[:2]
        ],
        axis=0,
    )
    return lax.dot_general(
        left, column_hit, (((1,), (1,)), ((), ())), preferred_element_type=jnp.float32
    )


def one_hot(hit):
    return jnp.where(hit, 1.0, 0.0).astype(jnp.bfloat16)


def permute(values, matrix):
    return jnp.dot(values, matrix, preferred_element_type=jnp.float32)


def kernel_values(offset):
    values = jnp.exp(-((2.0 * offset.astype(jnp.float32) / SMOOTH) ** 2))
    return jnp.where(jnp.abs(offset) <= SMOOTH, values, 0.0)


def encode(means):
    top = functools.reduce(jnp.maximum, [jnp.abs(mean) for mean in means])
    code = jnp.ceil(jnp.log(jnp.maximum(top, TINY)) * (OCTAVE / math.log(2.0))) + 1.0
    levels = LEVELS * jnp.exp(code * (-math.log(2.0) / OCTAVE))
    whole = [jnp.floor(mean * levels + 0.5) for mean in means] + [code]
    return [value.astype(jnp.int32).astype(jnp.int16) for value in whole]


def integer(ref):
    return ref.astype(jnp.int32).astype(jnp.float32)


def scale_of(code):
    return jnp.exp(integer(code) * (math.log(2.0) / OCTAVE)) * (1.0 / LEVELS)


def cycle_kernel(
    n,
    state_ref,
    counts_ref,
    east_ref,
    north_ref,
    cells_ref,
    mask_ref,
    values_ref,
    error_ref,
    relax_ref,
    out_ref,
    mean_ref,
    cells,
    mask,
    values,
    error,
    state,
    count,
    factors,
    counted,
    obs_send,
    obs_recv,
    grids,
    halo,
    wind_in,
    wind_halo,
    winds,
    spread_columns,
    gather_columns,
    lines,
    moved,
    advected,
    lon_kernel,
    loglik,
    loglik_halo,
    scores,
    held,
    send,
    send_log,
    recv,
    recv_log,
    merged,
    halo_sems,
    send_sems,
    recv_sems,
    send_log_sems,
    recv_log_sems,
    back_send,
    back_recv,
    relay_send,
    local_sems,
    obs_sems,
    obs_arrived,
    grid_sems,
    grid_arrived,
):
    slots, fields, rows, width = state_ref.shape
    across = width // TILE_COLS
    owners = (rows // TILE_ROWS) * across
    me = lax.axis_index("mem")
    band = lax.axis_index("lat")
    other = 1 - band

    share = cells.shape[1]
    rank = lax.rem(me, SHARERS)
    first_rank = me - rank
    mine = pl.ds(pl.multiple_of(rank * share, 128), share)
    loads = [
        pltpu.make_async_copy(source, target, local_sems.at[k])
        for k, (source, target) in enumerate(
            (
                (cells_ref.at[:, mine], cells),
                (mask_ref.at[:, mine], mask),
                (values_ref.at[:, mine], values),
                (error_ref.at[:, mine], error),
                (state_ref, state),
                (east_ref, wind_in.at[0]),
                (north_ref, wind_in.at[1]),
                (counts_ref, count),
                (relax_ref, factors),
            )
        )
    ]
    for load in loads:
        load.start()

    barrier = pltpu.get_barrier_semaphore()

    def greet(d, carry):
        pl.semaphore_signal(
            barrier, inc=1, device_id={"mem": lax.rem(me + d, n)}, device_id_type=MESH
        )
        return carry

    pl.semaphore_signal(barrier, inc=1, device_id={"lat": other}, device_id_type=MESH)
    lax.fori_loop(1, n, greet, 0)

    for load in loads[5:]:
        load.wait()
    pl.semaphore_wait(barrier, n)

    def to_other(source, target, slot):
        copy = pltpu.make_async_remote_copy(
            src_ref=source,
            dst_ref=target,
            send_sem=halo_sems.at[0, slot],
            recv_sem=halo_sems.at[1, slot],
            device_id={"lat": other},
            device_id_type=MESH,
        )
        copy.start()
        return copy

    edge16 = pl.ds(pl.multiple_of(other * (rows - 16), 16), 16)
    edge8 = pl.ds(pl.multiple_of(other * (rows - 8), 8), 8)
    copy_winds = to_other(wind_in.at[:, edge8, :], wind_halo, 0)
    copy_state = to_other(state_ref.at[:, :, edge16, :], halo, 1)

    def tile(t):
        down = t // across
        return (
            pl.ds(pl.multiple_of(down * TILE_ROWS, TILE_ROWS), TILE_ROWS),
            pl.ds(pl.multiple_of((t - down * across) * TILE_COLS, TILE_COLS), TILE_COLS),
        )

    for load in loads[:4]:
        load.wait()
    block = min(share, OBS_BLOCK)

    def count_block(index, carry):
        at = pl.ds(pl.multiple_of(index * block, 128), block)
        part = partial_grids(rows, width, *(ref[:, at] for ref in (cells, mask, values, error)))
        for term, (base, number) in enumerate(((0, 3), (3, 3), (6, 2))):
            counted[term] += functools.reduce(
                jnp.add, [part[(base + k) * rows : (base + k + 1) * rows] for k in range(number)]
            )
        return carry

    counted[...] = jnp.zeros_like(counted)
    lax.fori_loop(0, share // block, count_block, 0)
    held_tiles = owners // SHARERS

    def near_by(d):
        one_on = rank + 1 - 2 * lax.rem(rank, 2)
        across_block = lax.rem(rank + SHARERS // 2, SHARERS)
        opposite = SHARERS - 1 - rank
        return jnp.where(
            d == 1, opposite, jnp.where(d == 2, across_block, jnp.where(d == 3, one_on, rank))
        )

    def obs_out(d):
        return pltpu.make_async_remote_copy(
            src_ref=obs_send.at[near_by(d)],
            dst_ref=obs_recv.at[rank],
            send_sem=obs_sems.at[near_by(d)],
            recv_sem=obs_arrived.at[rank],
            device_id={"mem": first_rank + near_by(d)},
            device_id_type=MESH,
        )

    def give(d, carry):
        for k in range(held_tiles):
            down, along = tile(held_tiles * near_by(d) + k)
            for term in range(3):
                obs_send[near_by(d), k, term] = counted[term, down, along]

        @pl.when(d < SHARERS)
        def _():
            obs_out(d).start()

        return carry

    lax.fori_loop(1, SHARERS + 1, give, 0)

    def grid_out(d):
        return pltpu.make_async_remote_copy(
            src_ref=grids.at[rank],
            dst_ref=grids.at[rank],
            send_sem=grid_sems.at[d],
            recv_sem=grid_arrived.at[rank],
            device_id={"mem": first_rank + near_by(d)},
            device_id_type=MESH,
        )

    i0 = lax.broadcasted_iota(jnp.int32, (width, width), 0)
    i1 = lax.broadcasted_iota(jnp.int32, (width, width), 1)
    spread_columns[...] = one_hot(i0 == across * lax.rem(i1, TILE_COLS) + i1 // TILE_COLS)
    gather_columns[...] = one_hot(i1 == across * lax.rem(i0, TILE_COLS) + i0 // TILE_COLS)
    apart = jnp.abs(i0 - i1)
    lon_kernel[...] = kernel_values(jnp.minimum(apart, width - apart))

    near = lax.broadcasted_iota(jnp.int32, (8, width), 0)
    keep = jnp.where(band == 0, near, 7 - near) < STEPS

    layers = (rows + 8) // 8

    def columns(c):
        return slice(c * TILE_COLS, (c + 1) * TILE_COLS)

    def spread(ref, c):
        return jnp.stack([ref[c, pl.ds(k, 8, stride=layers), :] for k in range(layers)])

    copy_winds.wait()
    split = []
    for kind in range(2):
        far = jnp.where(keep, wind_halo[kind], 0.0)
        split += pieces(jnp.concatenate([wind_in[kind], far], axis=0))
    split = permute(
        jnp.concatenate([piece.astype(jnp.bfloat16) for piece in split], axis=0),
        spread_columns[...],
    ).reshape(2, 3, rows + 8, width)
    for kind in range(2):
        whole = (split[kind, 0] + split[kind, 1]) + split[kind, 2]
        for c in range(across):
            lines[0, kind, c] = whole[:, columns(c)]
            wind = spread(lines.at[0, kind], c)
            winds[2 * kind, c] = jnp.abs(wind)
            winds[2 * kind + 1, c] = wind
    loads[4].wait()
    copy_state.wait()

    def lay_out(slot, carry):
        whole = permute(
            jnp.concatenate(
                [state[slot].reshape(fields * rows, width), halo[slot].reshape(fields * 16, width)],
                axis=0,
            ),
            spread_columns[...],
        )
        own = whole[: fields * rows].reshape(fields, rows, width)
        far = whole[fields * rows :].reshape(fields, 16, width)
        far = jnp.where(band == 0, far[:, :8], far[:, 8:])
        for c in range(across):
            lines[slot, :, c, :rows] = own[:, :, columns(c)]
            lines[slot, :, c, rows:] = jnp.where(keep[:, columns(c)], far[:, :, columns(c)], 0.0)
        return carry

    lax.fori_loop(0, slots, lay_out, 0)

    def step(x):
        west = [pltpu.roll(x[across - 1], 1, 2)] + x[:-1]
        east = x[1:] + [pltpu.roll(x[0], TILE_COLS - 1, 2)]
        south = [
            jnp.concatenate([pltpu.roll(v[layers - 1 :], 1, 1), v[: layers - 1]], axis=0) for v in x
        ]
        north = [jnp.concatenate([v[1:], pltpu.roll(v[:1], 7, 1)], axis=0) for v in x]
        return [
            x[c]
            - winds[0, c] * (x[c] - jnp.where(winds[1, c] > 0.0, west[c], east[c]))
            - winds[2, c] * (x[c] - jnp.where(winds[3, c] > 0.0, south[c], north[c]))
            for c in range(across)
        ]

    def move(index, carry):
        kind = index // (slots // TOGETHER)
        first = TOGETHER * lax.rem(index, slots // TOGETHER)
        fields_of = [lines.at[first + k, kind] for k in range(TOGETHER)]
        xs = [[spread(field, c) for c in range(across)] for field in fields_of]
        for _ in range(STEPS):
            xs = [step(x) for x in xs]
        for k, (field, x) in enumerate(zip(fields_of, xs)):
            for c in range(across):
                for layer in range(layers):
                    field[c, pl.ds(layer, 8, stride=layers), :] = x[c][layer]
                moved[kind, first + k, :, columns(c)] = field[c, :rows].astype(jnp.bfloat16)
        return carry

    def collect(first, last):
        whole = moved[first:last].reshape((last - first) * slots * rows, width)
        whole = permute(whole, gather_columns[...]).astype(jnp.bfloat16)
        advected[first:last] = whole.reshape(last - first, slots, rows, width)

    total = fields * (slots // TOGETHER)
    early, late = total // 8, 7 * total // 8
    lax.fori_loop(0, slots // TOGETHER, move, 0)
    collect(0, 1)
    lax.fori_loop(slots // TOGETHER, early, move, 0)

    def arrive(d, carry):
        source = near_by(d)
        pltpu.make_async_remote_copy(
            src_ref=obs_send.at[0],
            dst_ref=obs_recv.at[source],
            send_sem=obs_sems.at[0],
            recv_sem=obs_arrived.at[source],
            device_id={"mem": first_rank + source},
            device_id_type=MESH,
        ).wait_recv()
        return carry

    lax.fori_loop(1, SHARERS, arrive, 0)
    obs_recv[rank] = obs_send[rank]
    grids[rank] = functools.reduce(jnp.add, [obs_recv[k] for k in range(SHARERS)])
    for d in range(1, SHARERS):
        grid_out(d).start()

    lax.fori_loop(early, late, move, 0)

    def likely(d, carry):
        source = near_by(SHARERS - d)

        @pl.when(d > 0)
        def _():
            pltpu.make_async_remote_copy(
                src_ref=grids.at[source],
                dst_ref=grids.at[source],
                send_sem=grid_sems.at[0],
                recv_sem=grid_arrived.at[source],
                device_id={"mem": first_rank + source},
                device_id_type=MESH,
            ).wait_recv()

        for k in range(held_tiles):
            down, along = tile(held_tiles * source + k)
            inverse, linear, constant = (grids[source, k, term] for term in range(3))
            for slot in range(slots):
                value = advected[0, slot, down, along].astype(jnp.float32)
                loglik[slot, down, along] = -0.5 * (
                    inverse * value * value - 2.0 * linear * value + constant
                )
        return carry

    lax.fori_loop(0, SHARERS, likely, 0)
    copy_loglik = to_other(loglik.at[:, edge16, :], loglik_halo, 2)
    lax.fori_loop(late, total, move, 0)
    collect(1, fields)

    r0 = lax.broadcasted_iota(jnp.int32, (rows, rows), 0)
    r1 = lax.broadcasted_iota(jnp.int32, (rows, rows), 1)
    own_band = kernel_values(r0 - r1)
    h0 = lax.broadcasted_iota(jnp.int32, (rows, 16), 0)
    h1 = lax.broadcasted_iota(jnp.int32, (rows, 16), 1)
    far_band = kernel_values(jnp.where(band == 0, rows + h1 - h0, h0 + 16 - h1))
    dot = functools.partial(
        jnp.dot, precision=lax.Precision.HIGHEST, preferred_element_type=jnp.float32
    )
    copy_loglik.wait()
    smoothed = jnp.concatenate(
        [
            dot(own_band, loglik[slot]) + dot(far_band, loglik_halo[slot])
            for slot in range(slots)
        ],
        axis=0,
    )
    scores[...] = dot(smoothed, lon_kernel[...]).reshape(slots, rows, width)

    partner = me + 1 - 2 * lax.rem(me, 2)
    parity = lax.rem(me, 2)

    half = n // 2

    def copies(t, slot, target):
        return [
            pltpu.make_async_remote_copy(
                src_ref=source.at[t],
                dst_ref=landing.at[slot],
                send_sem=sent_sems.at[t],
                recv_sem=landed_sems.at[slot],
                device_id={"mem": target},
                device_id_type=MESH,
            )
            for source, landing, sent_sems, landed_sems in (
                (send_log, recv_log, send_log_sems, recv_log_sems),
                (send, recv, send_sems, recv_sems),
            )
        ]

    def outgoing(t):
        return copies(t, me // 2, t)

    def across_pair(t):
        return copies(t, half + t // 2, partner)

    def start_all(made):
        for copy in made:
            copy.start()

    def gather(t):
        down, along = tile(t)
        live = [
            jnp.where(slot < count[0], scores[slot, down, along], -jnp.inf)
            for slot in range(slots)
        ]
        peak = functools.reduce(jnp.maximum, live)
        gains = [jnp.exp(score - peak) for score in live]
        weighted = [
            functools.reduce(
                jnp.add,
                [
                    gains[slot] * advected[kind, slot, down, along].astype(jnp.float32)
                    for slot in range(slots)
                ],
            )
            for kind in range(fields)
        ]
        return weighted, functools.reduce(jnp.add, gains), peak

    def put(t, weighted, total, peak):
        send_log[t] = peak + jnp.log(total)
        inverse = 1.0 / total
        for plane, value in enumerate(encode([value * inverse for value in weighted])):
            send[t, plane] = value

    def hold(t, weighted, total, peak):
        for plane, value in enumerate(weighted + [total, peak]):
            held[t // 2, plane] = value

    middle = owners // 2
    place = lax.rem(me // 2, middle)

    def near_to_far(k):
        ups, downs = middle - 1 - place, place
        both = jnp.minimum(ups, downs)
        upward = jnp.where(ups > downs, k - both, 0 - (k - both))
        paired = jnp.where(lax.rem(k, 2) == 1, (k + 1) // 2, 0 - (k // 2))
        return lax.rem(jnp.where(k <= 2 * both, paired, upward) + middle, middle)

    def turn(j):
        return 2 * near_to_far(middle - 1 - j)

    def give_pair(j, carry):
        t = lax.rem(partner + turn(j), owners)
        put(t, *gather(t))
        start_all(across_pair(t))
        return carry

    def keep_own(j, carry):
        t = 2 * j + parity
        hold(t, *gather(t))
        return carry

    def merge(t, slot):
        low, high = held[t // 2, fields + 1], recv_log[slot]
        peak = jnp.maximum(low, high)
        low, high = jnp.exp(low - peak), jnp.exp(high - peak)
        scaled = high * scale_of(recv[slot, fields])
        weighted = [
            low * held[t // 2, kind] + scaled * integer(recv[slot, kind])
            for kind in range(fields)
        ]
        return weighted, low * held[t // 2, fields] + high, peak

    def give_owner(j, carry):
        t = lax.rem(me + turn(j), owners)
        for copy in across_pair(t):
            copy.wait_recv()
        sums = merge(t, half + t // 2)

        @pl.when(t != me)
        def _():
            put(t, *sums)
            start_all(outgoing(t))

        @pl.when(t == me)
        def _():
            hold(t, *sums)

        return carry

    lax.fori_loop(0, owners // 2, give_pair, 0)
    lax.fori_loop(0, owners // 2, keep_own, 0)
    lax.fori_loop(0, owners // 2, give_owner, 0)

    def back(d):
        return pltpu.make_async_remote_copy(
            src_ref=merged.at[me],
            dst_ref=merged.at[me],
            send_sem=back_send.at[d],
            recv_sem=back_recv.at[me],
            device_id={"mem": lax.rem(me + 2 * d, n)},
            device_id_type=MESH,
        )

    def relay(t):
        return pltpu.make_async_remote_copy(
            src_ref=merged.at[t],
            dst_ref=merged.at[t],
            send_sem=relay_send.at[t],
            recv_sem=back_recv.at[t],
            device_id={"mem": partner},
            device_id_type=MESH,
        )

    @pl.when(me < owners)
    def _():
        def arrive(d, carry):
            source = lax.rem(me + 2 * d, n)
            for copy in copies(0, source // 2, source):
                copy.wait_recv()
            return carry

        lax.fori_loop(1, half, arrive, 0)
        own = me // 2
        peak = lax.fori_loop(
            1,
            half,
            lambda d, top: jnp.maximum(top, recv_log[lax.rem(own + d, half)]),
            held[own, fields + 1],
        )

        def add(d, sums):
            slot = lax.rem(own + d, half)
            factor = jnp.exp(recv_log[slot] - peak)
            scaled = factor * scale_of(recv[slot, fields])
            return tuple(
                sums[kind] + scaled * integer(recv[slot, kind]) for kind in range(fields)
            ) + (sums[fields] + factor,)

        factor = jnp.exp(held[own, fields + 1] - peak)
        sums = lax.fori_loop(
            1, half, add, tuple(factor * held[own, plane] for plane in range(fields + 1))
        )
        inverse = 1.0 / sums[fields]
        for plane, value in enumerate(encode([sums[kind] * inverse for kind in range(fields)])):
            merged[me, plane] = value

        def start(d, carry):
            back(d).start()
            return carry

        lax.fori_loop(1, half, start, 0)

    def landed(t):
        @pl.when(t != me)
        def _():
            relay(t).wait_recv()

    def place_of(start, k):
        return lax.rem(start + 2 * near_to_far(k), owners)

    def pass_on(k, carry):
        t = place_of(me, k)
        landed(t)
        relay(t).start()
        return carry

    def finish_passed(k, carry):
        finish(place_of(me, k))
        return carry

    def accept(k, carry):
        t = place_of(partner, k)
        landed(t)
        finish(t)
        return carry

    def finish(t):
        down, along = tile(t)
        scale = scale_of(merged[t, fields])
        for kind in range(fields):
            mean = scale * integer(merged[t, kind])
            mean_ref[kind, down, along] = mean.astype(jnp.bfloat16)
            for slot in range(slots):
                value = advected[kind, slot, down, along].astype(jnp.float32)
                fresh = value + factors[kind] * (mean - value)
                out_ref[slot, kind, down, along] = jnp.where(
                    slot < count[0], fresh, 0.0
                ).astype(jnp.bfloat16)

    for d in range(1, SHARERS):
        obs_out(d).wait_send()
        grid_out(d).wait_send()

    def passed(j, carry):
        for copy in across_pair(2 * j + 1 - parity):
            copy.wait_send()

        @pl.when(2 * j + parity != me)
        def _():
            for copy in outgoing(2 * j + parity):
                copy.wait_send()

        return carry

    lax.fori_loop(0, owners // 2, passed, 0)
    pass_on(0, 0)
    finish(place_of(me, 0))
    lax.fori_loop(1, middle, pass_on, 0)
    lax.fori_loop(1, middle, finish_passed, 0)
    lax.fori_loop(0, middle, accept, 0)

    def relayed(j, carry):
        relay(2 * j + parity).wait_send()
        return carry

    lax.fori_loop(0, middle, relayed, 0)

    @pl.when(me < owners)
    def _():
        def sent_back(d, carry):
            back(d).wait_send()
            return carry

        lax.fori_loop(1, n // 2, sent_back, 0)


def cycle(n, state, counts, east_wind, north_wind, obs, relax):
    slots, fields, rows, width = state.shape
    across = width // TILE_COLS
    owners = (rows // TILE_ROWS) * across
    share = obs[0].shape[1] // SHARERS
    held_tiles = owners // SHARERS
    tile = (TILE_ROWS, TILE_COLS)
    hbm = pl.BlockSpec(memory_space=pl.ANY)
    vmem = pl.BlockSpec(memory_space=pltpu.VMEM)
    f32, bf16 = jnp.float32, jnp.bfloat16
    return pl.pallas_call(
        functools.partial(cycle_kernel, n),
        out_shape=(
            pltpu.VMEM(state.shape, bf16),
            pltpu.VMEM((fields, rows, width), bf16),
        ),
        in_specs=[hbm] * 9,
        out_specs=(vmem, vmem),
        scratch_shapes=[
            pltpu.VMEM((1, share), jnp.int32),
            pltpu.VMEM((1, share), jnp.int32),
            pltpu.VMEM((1, share), f32),
            pltpu.VMEM((1, share), f32),
            pltpu.VMEM(state.shape, bf16),
            pltpu.SMEM(counts.shape, counts.dtype),
            pltpu.SMEM(relax.shape, relax.dtype),
            pltpu.VMEM((3, rows, width), f32),
            pltpu.VMEM((SHARERS, held_tiles, 3) + tile, f32),
            pltpu.VMEM((SHARERS, held_tiles, 3) + tile, f32),
            pltpu.VMEM((SHARERS, held_tiles, 3) + tile, f32),
            pltpu.VMEM((slots, fields, 16, width), bf16),
            pltpu.VMEM((2, rows, width), f32),
            pltpu.VMEM((2, 8, width), f32),
            pltpu.VMEM((4, across, (rows + 8) // 8, 8, TILE_COLS), f32),
            pltpu.VMEM((width, width), bf16),
            pltpu.VMEM((width, width), bf16),
            pltpu.VMEM((slots, fields, across, rows + 8, TILE_COLS), f32),
            pltpu.VMEM((fields, slots, rows, width), bf16),
            pltpu.VMEM((fields, slots, rows, width), bf16),
            pltpu.VMEM((width, width), f32),
            pltpu.VMEM((slots, rows, width), f32),
            pltpu.VMEM((slots, 16, width), f32),
            pltpu.VMEM((slots, rows, width), f32),
            pltpu.VMEM((owners // 2, fields + 2) + tile, f32),
            pltpu.VMEM((owners, fields + 1) + tile, jnp.int16),
            pltpu.VMEM((owners,) + tile, f32),
            pltpu.VMEM((n // 2 + owners // 2, fields + 1) + tile, jnp.int16),
            pltpu.VMEM((n // 2 + owners // 2,) + tile, f32),
            pltpu.VMEM((owners, fields + 1) + tile, jnp.int16),
            pltpu.SemaphoreType.DMA((2, 3)),
            pltpu.SemaphoreType.DMA((owners,)),
            pltpu.SemaphoreType.DMA((n // 2 + owners // 2,)),
            pltpu.SemaphoreType.DMA((owners,)),
            pltpu.SemaphoreType.DMA((n // 2 + owners // 2,)),
            pltpu.SemaphoreType.DMA((n,)),
            pltpu.SemaphoreType.DMA((owners,)),
            pltpu.SemaphoreType.DMA((owners,)),
            pltpu.SemaphoreType.DMA((9,)),
            pltpu.SemaphoreType.DMA((SHARERS,)),
            pltpu.SemaphoreType.DMA((SHARERS,)),
            pltpu.SemaphoreType.DMA((SHARERS,)),
            pltpu.SemaphoreType.DMA((SHARERS,)),
        ],
        compiler_params=pltpu.CompilerParams(
            collective_id=0, has_side_effects=True, vmem_limit_bytes=56 * 1024 * 1024
        ),
    )(state, counts, east_wind, north_wind, *obs, relax)


def write_kernel(fresh, mean, out, mean_out, sems):
    copies = [
        pltpu.make_async_copy(fresh, out, sems.at[0]),
        pltpu.make_async_copy(mean, mean_out, sems.at[1]),
    ]
    for copy in copies:
        copy.start()
    for copy in copies:
        copy.wait()


def write_out(fresh, mean):
    hbm = pl.BlockSpec(memory_space=pl.ANY)
    return pl.pallas_call(
        write_kernel,
        out_shape=(
            jax.ShapeDtypeStruct(fresh.shape, fresh.dtype),
            jax.ShapeDtypeStruct(mean.shape, mean.dtype),
        ),
        in_specs=[hbm, hbm],
        out_specs=(hbm, hbm),
        scratch_shapes=[pltpu.SemaphoreType.DMA((2,))],
    )(*(pltpu.with_memory_space_constraint(x, pltpu.VMEM) for x in (fresh, mean)))


def on_device(
    n, state, counts, east_wind, north_wind, obs_cells, obs_mask, obs_values, obs_error, relax
):
    obs = (obs_cells, obs_mask, obs_values, obs_error)
    fresh, mean = cycle(n, state, counts, east_wind, north_wind, obs, relax)
    return write_out(fresh, mean)


def solution(mesh):
    return jax.shard_map(
        functools.partial(on_device, mesh.shape["mem"]),
        mesh=mesh,
        in_specs=(
            P(("groups", "mem"), None, "lat", None),
            P(("groups", "mem")),
            P(("groups", "lat"), None),
            P(("groups", "lat"), None),
            P(("groups", "lat"), None),
            P(("groups", "lat"), None),
            P(("groups", "lat"), None),
            P(("groups", "lat"), None),
            P(),
        ),
        out_specs=(P(("groups", "mem"), None, "lat", None), P("groups", "lat", None)),
        check_vma=False,
    )
```

```python
import functools
import math

import jax
import jax.numpy as jnp
from jax import lax
from jax.experimental import pallas as pl
from jax.experimental.pallas import tpu as pltpu
from jax.sharding import PartitionSpec as P

STEPS = 4
SMOOTH = 16
LOG_TWO_PI = 1.8378770664093453
MESH = pl.DeviceIdType.MESH
TILE_ROWS = 16
TILE_COLS = 128
OBS_BLOCK = 4096
TOGETHER = 4
SHARERS = 4
LEVELS = 32760.0
OCTAVE = 128.0
TINY = 1e-33


def pieces(values):
    high = values.astype(jnp.bfloat16).astype(jnp.float32)
    rest = values - high
    mid = rest.astype(jnp.bfloat16).astype(jnp.float32)
    return high, mid, rest - mid


def partial_grids(rows, width, cells, mask, values, error):
    count = cells.shape[1]
    used = mask.astype(jnp.float32)
    inverse = used / (error * error)
    terms = (
        inverse,
        inverse * values,
        inverse * values * values + used * (2.0 * jnp.log(error) + LOG_TWO_PI),
    )
    row = cells // width
    column = cells - row * width
    row_hit = lax.broadcasted_iota(jnp.int32, (rows, count), 0) == row
    column_hit = jnp.where(
        lax.broadcasted_iota(jnp.int32, (width, count), 0) == column, 1.0, 0.0
    ).astype(jnp.bfloat16)
    left = jnp.concatenate(
        [
            jnp.where(row_hit, piece, 0.0).astype(jnp.bfloat16)
            for piece in pieces(terms[0]) + pieces(terms[1]) + pieces(terms[2])[:2]
        ],
        axis=0,
    )
    return lax.dot_general(
        left, column_hit, (((1,), (1,)), ((), ())), preferred_element_type=jnp.float32
    )


def one_hot(hit):
    return jnp.where(hit, 1.0, 0.0).astype(jnp.bfloat16)


def permute(values, matrix):
    return jnp.dot(values, matrix, preferred_element_type=jnp.float32)


def kernel_values(offset):
    values = jnp.exp(-((2.0 * offset.astype(jnp.float32) / SMOOTH) ** 2))
    return jnp.where(jnp.abs(offset) <= SMOOTH, values, 0.0)


def encode(means):
    top = functools.reduce(jnp.maximum, [jnp.abs(mean) for mean in means])
    code = jnp.ceil(jnp.log(jnp.maximum(top, TINY)) * (OCTAVE / math.log(2.0))) + 1.0
    levels = LEVELS * jnp.exp(code * (-math.log(2.0) / OCTAVE))
    whole = [jnp.floor(mean * levels + 0.5) for mean in means] + [code]
    return [value.astype(jnp.int32).astype(jnp.int16) for value in whole]


def integer(ref):
    return ref.astype(jnp.int32).astype(jnp.float32)


def scale_of(code):
    return jnp.exp(integer(code) * (math.log(2.0) / OCTAVE)) * (1.0 / LEVELS)


def cycle_kernel(
    n,
    state_ref,
    counts_ref,
    east_ref,
    north_ref,
    cells_ref,
    mask_ref,
    values_ref,
    error_ref,
    relax_ref,
    out_ref,
    mean_ref,
    cells,
    mask,
    values,
    error,
    state,
    count,
    factors,
    counted,
    obs_send,
    obs_recv,
    grids,
    halo,
    wind_in,
    wind_halo,
    winds,
    spread_columns,
    gather_columns,
    lines,
    moved,
    advected,
    lon_kernel,
    loglik,
    loglik_halo,
    scores,
    held,
    send,
    send_log,
    recv,
    recv_log,
    merged,
    halo_sems,
    send_sems,
    recv_sems,
    send_log_sems,
    recv_log_sems,
    back_send,
    back_recv,
    relay_send,
    local_sems,
    obs_sems,
    obs_arrived,
    grid_sems,
    grid_arrived,
):
    slots, fields, rows, width = state_ref.shape
    across = width // TILE_COLS
    owners = (rows // TILE_ROWS) * across
    me = lax.axis_index("mem")
    band = lax.axis_index("lat")
    other = 1 - band

    share = cells.shape[1]
    rank = lax.rem(me, SHARERS)
    first_rank = me - rank
    mine = pl.ds(pl.multiple_of(rank * share, 128), share)
    loads = [
        pltpu.make_async_copy(source, target, local_sems.at[k])
        for k, (source, target) in enumerate(
            (
                (cells_ref.at[:, mine], cells),
                (mask_ref.at[:, mine], mask),
                (values_ref.at[:, mine], values),
                (error_ref.at[:, mine], error),
                (state_ref, state),
                (east_ref, wind_in.at[0]),
                (north_ref, wind_in.at[1]),
                (counts_ref, count),
                (relax_ref, factors),
            )
        )
    ]
    for load in loads:
        load.start()

    barrier = pltpu.get_barrier_semaphore()

    def greet(d, carry):
        pl.semaphore_signal(
            barrier, inc=1, device_id={"mem": lax.rem(me + d, n)}, device_id_type=MESH
        )
        return carry

    pl.semaphore_signal(barrier, inc=1, device_id={"lat": other}, device_id_type=MESH)
    lax.fori_loop(1, n, greet, 0)

    for load in loads[5:]:
        load.wait()
    pl.semaphore_wait(barrier, n)

    def to_other(source, target, slot):
        copy = pltpu.make_async_remote_copy(
            src_ref=source,
            dst_ref=target,
            send_sem=halo_sems.at[0, slot],
            recv_sem=halo_sems.at[1, slot],
            device_id={"lat": other},
            device_id_type=MESH,
        )
        copy.start()
        return copy

    edge16 = pl.ds(pl.multiple_of(other * (rows - 16), 16), 16)
    edge8 = pl.ds(pl.multiple_of(other * (rows - 8), 8), 8)
    copy_winds = to_other(wind_in.at[:, edge8, :], wind_halo, 0)
    copy_state = to_other(state_ref.at[:, :, edge16, :], halo, 1)

    def tile(t):
        down = t // across
        return (
            pl.ds(pl.multiple_of(down * TILE_ROWS, TILE_ROWS), TILE_ROWS),
            pl.ds(pl.multiple_of((t - down * across) * TILE_COLS, TILE_COLS), TILE_COLS),
        )

    for load in loads[:4]:
        load.wait()
    block = min(share, OBS_BLOCK)

    def count_block(index, carry):
        at = pl.ds(pl.multiple_of(index * block, 128), block)
        part = partial_grids(rows, width, *(ref[:, at] for ref in (cells, mask, values, error)))
        for term, (base, number) in enumerate(((0, 3), (3, 3), (6, 2))):
            counted[term] += functools.reduce(
                jnp.add, [part[(base + k) * rows : (base + k + 1) * rows] for k in range(number)]
            )
        return carry

    counted[...] = jnp.zeros_like(counted)
    lax.fori_loop(0, share // block, count_block, 0)
    held_tiles = owners // SHARERS

    def near_by(d):
        one_on = rank + 1 - 2 * lax.rem(rank, 2)
        across_block = lax.rem(rank + SHARERS // 2, SHARERS)
        opposite = SHARERS - 1 - rank
        return jnp.where(
            d == 1, opposite, jnp.where(d == 2, across_block, jnp.where(d == 3, one_on, rank))
        )

    def obs_out(d):
        return pltpu.make_async_remote_copy(
            src_ref=obs_send.at[near_by(d)],
            dst_ref=obs_recv.at[rank],
            send_sem=obs_sems.at[near_by(d)],
            recv_sem=obs_arrived.at[rank],
            device_id={"mem": first_rank + near_by(d)},
            device_id_type=MESH,
        )

    def give(d, carry):
        for k in range(held_tiles):
            down, along = tile(held_tiles * near_by(d) + k)
            for term in range(3):
                obs_send[near_by(d), k, term] = counted[term, down, along]

        @pl.when(d < SHARERS)
        def _():
            obs_out(d).start()

        return carry

    lax.fori_loop(1, SHARERS + 1, give, 0)

    def grid_out(d):
        return pltpu.make_async_remote_copy(
            src_ref=grids.at[rank],
            dst_ref=grids.at[rank],
            send_sem=grid_sems.at[d],
            recv_sem=grid_arrived.at[rank],
            device_id={"mem": first_rank + near_by(d)},
            device_id_type=MESH,
        )

    i0 = lax.broadcasted_iota(jnp.int32, (width, width), 0)
    i1 = lax.broadcasted_iota(jnp.int32, (width, width), 1)
    spread_columns[...] = one_hot(i0 == across * lax.rem(i1, TILE_COLS) + i1 // TILE_COLS)
    gather_columns[...] = one_hot(i1 == across * lax.rem(i0, TILE_COLS) + i0 // TILE_COLS)
    apart = jnp.abs(i0 - i1)
    lon_kernel[...] = kernel_values(jnp.minimum(apart, width - apart))

    near = lax.broadcasted_iota(jnp.int32, (8, width), 0)
    keep = jnp.where(band == 0, near, 7 - near) < STEPS

    layers = (rows + 8) // 8

    def columns(c):
        return slice(c * TILE_COLS, (c + 1) * TILE_COLS)

    def spread(ref, c):
        return jnp.stack([ref[c, pl.ds(k, 8, stride=layers), :] for k in range(layers)])

    copy_winds.wait()
    split = []
    for kind in range(2):
        far = jnp.where(keep, wind_halo[kind], 0.0)
        split += pieces(jnp.concatenate([wind_in[kind], far], axis=0))
    split = permute(
        jnp.concatenate([piece.astype(jnp.bfloat16) for piece in split], axis=0),
        spread_columns[...],
    ).reshape(2, 3, rows + 8, width)
    for kind in range(2):
        whole = (split[kind, 0] + split[kind, 1]) + split[kind, 2]
        for c in range(across):
            lines[0, kind, c] = whole[:, columns(c)]
            wind = spread(lines.at[0, kind], c)
            winds[2 * kind, c] = jnp.abs(wind)
            winds[2 * kind + 1, c] = wind
    loads[4].wait()
    copy_state.wait()

    def lay_out(slot, carry):
        whole = permute(
            jnp.concatenate(
                [state[slot].reshape(fields * rows, width), halo[slot].reshape(fields * 16, width)],
                axis=0,
            ),
            spread_columns[...],
        )
        own = whole[: fields * rows].reshape(fields, rows, width)
        far = whole[fields * rows :].reshape(fields, 16, width)
        far = jnp.where(band == 0, far[:, :8], far[:, 8:])
        for c in range(across):
            lines[slot, :, c, :rows] = own[:, :, columns(c)]
            lines[slot, :, c, rows:] = jnp.where(keep[:, columns(c)], far[:, :, columns(c)], 0.0)
        return carry

    lax.fori_loop(0, slots, lay_out, 0)

    def step(x):
        west = [pltpu.roll(x[across - 1], 1, 2)] + x[:-1]
        east = x[1:] + [pltpu.roll(x[0], TILE_COLS - 1, 2)]
        south = [
            jnp.concatenate([pltpu.roll(v[layers - 1 :], 1, 1), v[: layers - 1]], axis=0) for v in x
        ]
        north = [jnp.concatenate([v[1:], pltpu.roll(v[:1], 7, 1)], axis=0) for v in x]
        return [
            x[c]
            - winds[0, c] * (x[c] - jnp.where(winds[1, c] > 0.0, west[c], east[c]))
            - winds[2, c] * (x[c] - jnp.where(winds[3, c] > 0.0, south[c], north[c]))
            for c in range(across)
        ]

    def move(index, carry):
        kind = index // (slots // TOGETHER)
        first = TOGETHER * lax.rem(index, slots // TOGETHER)
        fields_of = [lines.at[first + k, kind] for k in range(TOGETHER)]
        xs = [[spread(field, c) for c in range(across)] for field in fields_of]
        for _ in range(STEPS):
            xs = [step(x) for x in xs]
        for k, (field, x) in enumerate(zip(fields_of, xs)):
            for c in range(across):
                for layer in range(layers):
                    field[c, pl.ds(layer, 8, stride=layers), :] = x[c][layer]
                moved[kind, first + k, :, columns(c)] = field[c, :rows].astype(jnp.bfloat16)
        return carry

    def collect(first, last):
        whole = moved[first:last].reshape((last - first) * slots * rows, width)
        whole = permute(whole, gather_columns[...]).astype(jnp.bfloat16)
        advected[first:last] = whole.reshape(last - first, slots, rows, width)

    total = fields * (slots // TOGETHER)
    early = total // 8
    lax.fori_loop(0, slots // TOGETHER, move, 0)
    collect(0, 1)
    lax.fori_loop(slots // TOGETHER, early, move, 0)

    def arrive(d, carry):
        source = near_by(d)
        pltpu.make_async_remote_copy(
            src_ref=obs_send.at[0],
            dst_ref=obs_recv.at[source],
            send_sem=obs_sems.at[0],
            recv_sem=obs_arrived.at[source],
            device_id={"mem": first_rank + source},
            device_id_type=MESH,
        ).wait_recv()
        return carry

    lax.fori_loop(1, SHARERS, arrive, 0)
    obs_recv[rank] = obs_send[rank]
    grids[rank] = functools.reduce(jnp.add, [obs_recv[k] for k in range(SHARERS)])
    for d in range(1, SHARERS):
        grid_out(d).start()

    lax.fori_loop(early, total, move, 0)

    collect(1, fields)

    def likely(index, carry):
        source = lax.rem(index + (1 - band) * (SHARERS // 2), SHARERS)

        @pl.when(source != rank)
        def _():
            pltpu.make_async_remote_copy(
                src_ref=grids.at[source],
                dst_ref=grids.at[source],
                send_sem=grid_sems.at[0],
                recv_sem=grid_arrived.at[source],
                device_id={"mem": first_rank + source},
                device_id_type=MESH,
            ).wait_recv()

        for k in range(held_tiles):
            down, along = tile(held_tiles * source + k)
            inverse, linear, constant = (grids[source, k, term] for term in range(3))
            for slot in range(slots):
                value = advected[0, slot, down, along].astype(jnp.float32)
                loglik[slot, down, along] = -0.5 * (
                    inverse * value * value - 2.0 * linear * value + constant
                )
        return carry

    lax.fori_loop(0, SHARERS // 2, likely, 0)
    copy_loglik = to_other(loglik.at[:, edge16, :], loglik_halo, 2)
    lax.fori_loop(SHARERS // 2, SHARERS, likely, 0)

    r0 = lax.broadcasted_iota(jnp.int32, (rows, rows), 0)
    r1 = lax.broadcasted_iota(jnp.int32, (rows, rows), 1)
    own_band = kernel_values(r0 - r1)
    h0 = lax.broadcasted_iota(jnp.int32, (rows, 16), 0)
    h1 = lax.broadcasted_iota(jnp.int32, (rows, 16), 1)
    far_band = kernel_values(jnp.where(band == 0, rows + h1 - h0, h0 + 16 - h1))
    dot = functools.partial(
        jnp.dot, precision=lax.Precision.HIGHEST, preferred_element_type=jnp.float32
    )
    own_part = [dot(own_band, loglik[slot]) for slot in range(slots)]
    copy_loglik.wait()
    smoothed = jnp.concatenate(
        [own_part[slot] + dot(far_band, loglik_halo[slot]) for slot in range(slots)], axis=0
    )
    scores[...] = dot(smoothed, lon_kernel[...]).reshape(slots, rows, width)

    partner = me + 1 - 2 * lax.rem(me, 2)
    parity = lax.rem(me, 2)

    half = n // 2

    def copies(t, slot, target):
        return [
            pltpu.make_async_remote_copy(
                src_ref=source.at[t],
                dst_ref=landing.at[slot],
                send_sem=sent_sems.at[t],
                recv_sem=landed_sems.at[slot],
                device_id={"mem": target},
                device_id_type=MESH,
            )
            for source, landing, sent_sems, landed_sems in (
                (send_log, recv_log, send_log_sems, recv_log_sems),
                (send, recv, send_sems, recv_sems),
            )
        ]

    def outgoing(t):
        return copies(t, me // 2, t)

    def across_pair(t):
        return copies(t, half + t // 2, partner)

    def start_all(made):
        for copy in made:
            copy.start()

    def gather(t):
        down, along = tile(t)
        live = [
            jnp.where(slot < count[0], scores[slot, down, along], -jnp.inf)
            for slot in range(slots)
        ]
        peak = functools.reduce(jnp.maximum, live)
        gains = [jnp.exp(score - peak) for score in live]
        weighted = [
            functools.reduce(
                jnp.add,
                [
                    gains[slot] * advected[kind, slot, down, along].astype(jnp.float32)
                    for slot in range(slots)
                ],
            )
            for kind in range(fields)
        ]
        return weighted, functools.reduce(jnp.add, gains), peak

    def put(t, weighted, total, peak):
        send_log[t] = peak + jnp.log(total)
        inverse = 1.0 / total
        for plane, value in enumerate(encode([value * inverse for value in weighted])):
            send[t, plane] = value

    def hold(t, weighted, total, peak):
        for plane, value in enumerate(weighted + [total, peak]):
            held[t // 2, plane] = value

    middle = owners // 2
    place = lax.rem(me // 2, middle)

    def near_to_far(k):
        ups, downs = middle - 1 - place, place
        both = jnp.minimum(ups, downs)
        upward = jnp.where(ups > downs, k - both, 0 - (k - both))
        paired = jnp.where(lax.rem(k, 2) == 1, (k + 1) // 2, 0 - (k // 2))
        return lax.rem(jnp.where(k <= 2 * both, paired, upward) + middle, middle)

    def turn(j):
        return 2 * near_to_far(middle - 1 - j)

    def give_pair(j, carry):
        t = lax.rem(partner + turn(j), owners)
        put(t, *gather(t))
        start_all(across_pair(t))
        return carry

    def keep_own(j, carry):
        t = 2 * j + parity
        hold(t, *gather(t))
        return carry

    def merge(t, slot):
        low, high = held[t // 2, fields + 1], recv_log[slot]
        peak = jnp.maximum(low, high)
        low, high = jnp.exp(low - peak), jnp.exp(high - peak)
        scaled = high * scale_of(recv[slot, fields])
        weighted = [
            low * held[t // 2, kind] + scaled * integer(recv[slot, kind])
            for kind in range(fields)
        ]
        return weighted, low * held[t // 2, fields] + high, peak

    def give_owner(j, carry):
        t = lax.rem(me + turn(j), owners)
        for copy in across_pair(t):
            copy.wait_recv()
        sums = merge(t, half + t // 2)

        @pl.when(t != me)
        def _():
            put(t, *sums)
            start_all(outgoing(t))

        @pl.when(t == me)
        def _():
            hold(t, *sums)

        return carry

    lax.fori_loop(0, owners // 2, give_pair, 0)
    lax.fori_loop(0, owners // 2, keep_own, 0)
    lax.fori_loop(0, owners // 2, give_owner, 0)

    def back(d):
        return pltpu.make_async_remote_copy(
            src_ref=merged.at[me],
            dst_ref=merged.at[me],
            send_sem=back_send.at[d],
            recv_sem=back_recv.at[me],
            device_id={"mem": lax.rem(me + 2 * d, n)},
            device_id_type=MESH,
        )

    def relay(t):
        return pltpu.make_async_remote_copy(
            src_ref=merged.at[t],
            dst_ref=merged.at[t],
            send_sem=relay_send.at[t],
            recv_sem=back_recv.at[t],
            device_id={"mem": partner},
            device_id_type=MESH,
        )

    @pl.when(me < owners)
    def _():
        def arrive(d, carry):
            source = lax.rem(me + 2 * d, n)
            for copy in copies(0, source // 2, source):
                copy.wait_recv()
            return carry

        lax.fori_loop(1, half, arrive, 0)
        own = me // 2
        peak = lax.fori_loop(
            1,
            half,
            lambda d, top: jnp.maximum(top, recv_log[lax.rem(own + d, half)]),
            held[own, fields + 1],
        )

        def add(d, sums):
            slot = lax.rem(own + d, half)
            factor = jnp.exp(recv_log[slot] - peak)
            scaled = factor * scale_of(recv[slot, fields])
            return tuple(
                sums[kind] + scaled * integer(recv[slot, kind]) for kind in range(fields)
            ) + (sums[fields] + factor,)

        factor = jnp.exp(held[own, fields + 1] - peak)
        sums = lax.fori_loop(
            1, half, add, tuple(factor * held[own, plane] for plane in range(fields + 1))
        )
        inverse = 1.0 / sums[fields]
        for plane, value in enumerate(encode([sums[kind] * inverse for kind in range(fields)])):
            merged[me, plane] = value

        def start(d, carry):
            back(d).start()
            return carry

        lax.fori_loop(1, half, start, 0)

    def landed(t):
        @pl.when(t != me)
        def _():
            relay(t).wait_recv()

    def place_of(start, k):
        return lax.rem(start + 2 * near_to_far(k), owners)

    def pass_on(k, carry):
        t = place_of(me, k)
        landed(t)
        relay(t).start()
        return carry

    def finish_passed(k, carry):
        finish(place_of(me, k))
        return carry

    def accept(k, carry):
        t = place_of(partner, k)
        landed(t)
        finish(t)
        return carry

    def finish(t):
        down, along = tile(t)
        scale = scale_of(merged[t, fields])
        for kind in range(fields):
            mean = scale * integer(merged[t, kind])
            mean_ref[kind, down, along] = mean.astype(jnp.bfloat16)
            for slot in range(slots):
                value = advected[kind, slot, down, along].astype(jnp.float32)
                fresh = value + factors[kind] * (mean - value)
                out_ref[slot, kind, down, along] = jnp.where(
                    slot < count[0], fresh, 0.0
                ).astype(jnp.bfloat16)

    for d in range(1, SHARERS):
        obs_out(d).wait_send()
        grid_out(d).wait_send()

    def passed(j, carry):
        for copy in across_pair(2 * j + 1 - parity):
            copy.wait_send()

        @pl.when(2 * j + parity != me)
        def _():
            for copy in outgoing(2 * j + parity):
                copy.wait_send()

        return carry

    lax.fori_loop(0, owners // 2, passed, 0)
    pass_on(0, 0)
    finish(place_of(me, 0))
    lax.fori_loop(1, middle, pass_on, 0)
    lax.fori_loop(1, middle, finish_passed, 0)
    lax.fori_loop(0, middle, accept, 0)

    def relayed(j, carry):
        relay(2 * j + parity).wait_send()
        return carry

    lax.fori_loop(0, middle, relayed, 0)

    @pl.when(me < owners)
    def _():
        def sent_back(d, carry):
            back(d).wait_send()
            return carry

        lax.fori_loop(1, n // 2, sent_back, 0)


def cycle(n, state, counts, east_wind, north_wind, obs, relax):
    slots, fields, rows, width = state.shape
    across = width // TILE_COLS
    owners = (rows // TILE_ROWS) * across
    share = obs[0].shape[1] // SHARERS
    held_tiles = owners // SHARERS
    tile = (TILE_ROWS, TILE_COLS)
    hbm = pl.BlockSpec(memory_space=pl.ANY)
    vmem = pl.BlockSpec(memory_space=pltpu.VMEM)
    f32, bf16 = jnp.float32, jnp.bfloat16
    return pl.pallas_call(
        functools.partial(cycle_kernel, n),
        out_shape=(
            pltpu.VMEM(state.shape, bf16),
            pltpu.VMEM((fields, rows, width), bf16),
        ),
        in_specs=[hbm] * 9,
        out_specs=(vmem, vmem),
        scratch_shapes=[
            pltpu.VMEM((1, share), jnp.int32),
            pltpu.VMEM((1, share), jnp.int32),
            pltpu.VMEM((1, share), f32),
            pltpu.VMEM((1, share), f32),
            pltpu.VMEM(state.shape, bf16),
            pltpu.SMEM(counts.shape, counts.dtype),
            pltpu.SMEM(relax.shape, relax.dtype),
            pltpu.VMEM((3, rows, width), f32),
            pltpu.VMEM((SHARERS, held_tiles, 3) + tile, f32),
            pltpu.VMEM((SHARERS, held_tiles, 3) + tile, f32),
            pltpu.VMEM((SHARERS, held_tiles, 3) + tile, f32),
            pltpu.VMEM((slots, fields, 16, width), bf16),
            pltpu.VMEM((2, rows, width), f32),
            pltpu.VMEM((2, 8, width), f32),
            pltpu.VMEM((4, across, (rows + 8) // 8, 8, TILE_COLS), f32),
            pltpu.VMEM((width, width), bf16),
            pltpu.VMEM((width, width), bf16),
            pltpu.VMEM((slots, fields, across, rows + 8, TILE_COLS), f32),
            pltpu.VMEM((fields, slots, rows, width), bf16),
            pltpu.VMEM((fields, slots, rows, width), bf16),
            pltpu.VMEM((width, width), f32),
            pltpu.VMEM((slots, rows, width), f32),
            pltpu.VMEM((slots, 16, width), f32),
            pltpu.VMEM((slots, rows, width), f32),
            pltpu.VMEM((owners // 2, fields + 2) + tile, f32),
            pltpu.VMEM((owners, fields + 1) + tile, jnp.int16),
            pltpu.VMEM((owners,) + tile, f32),
            pltpu.VMEM((n // 2 + owners // 2, fields + 1) + tile, jnp.int16),
            pltpu.VMEM((n // 2 + owners // 2,) + tile, f32),
            pltpu.VMEM((owners, fields + 1) + tile, jnp.int16),
            pltpu.SemaphoreType.DMA((2, 3)),
            pltpu.SemaphoreType.DMA((owners,)),
            pltpu.SemaphoreType.DMA((n // 2 + owners // 2,)),
            pltpu.SemaphoreType.DMA((owners,)),
            pltpu.SemaphoreType.DMA((n // 2 + owners // 2,)),
            pltpu.SemaphoreType.DMA((n,)),
            pltpu.SemaphoreType.DMA((owners,)),
            pltpu.SemaphoreType.DMA((owners,)),
            pltpu.SemaphoreType.DMA((9,)),
            pltpu.SemaphoreType.DMA((SHARERS,)),
            pltpu.SemaphoreType.DMA((SHARERS,)),
            pltpu.SemaphoreType.DMA((SHARERS,)),
            pltpu.SemaphoreType.DMA((SHARERS,)),
        ],
        compiler_params=pltpu.CompilerParams(
            collective_id=0, has_side_effects=True, vmem_limit_bytes=56 * 1024 * 1024
        ),
    )(state, counts, east_wind, north_wind, *obs, relax)


def write_kernel(fresh, mean, out, mean_out, sems):
    copies = [
        pltpu.make_async_copy(fresh, out, sems.at[0]),
        pltpu.make_async_copy(mean, mean_out, sems.at[1]),
    ]
    for copy in copies:
        copy.start()
    for copy in copies:
        copy.wait()


def write_out(fresh, mean):
    hbm = pl.BlockSpec(memory_space=pl.ANY)
    return pl.pallas_call(
        write_kernel,
        out_shape=(
            jax.ShapeDtypeStruct(fresh.shape, fresh.dtype),
            jax.ShapeDtypeStruct(mean.shape, mean.dtype),
        ),
        in_specs=[hbm, hbm],
        out_specs=(hbm, hbm),
        scratch_shapes=[pltpu.SemaphoreType.DMA((2,))],
    )(*(pltpu.with_memory_space_constraint(x, pltpu.VMEM) for x in (fresh, mean)))


def on_device(
    n, state, counts, east_wind, north_wind, obs_cells, obs_mask, obs_values, obs_error, relax
):
    obs = (obs_cells, obs_mask, obs_values, obs_error)
    fresh, mean = cycle(n, state, counts, east_wind, north_wind, obs, relax)
    return write_out(fresh, mean)


def solution(mesh):
    return jax.shard_map(
        functools.partial(on_device, mesh.shape["mem"]),
        mesh=mesh,
        in_specs=(
            P(("groups", "mem"), None, "lat", None),
            P(("groups", "mem")),
            P(("groups", "lat"), None),
            P(("groups", "lat"), None),
            P(("groups", "lat"), None),
            P(("groups", "lat"), None),
            P(("groups", "lat"), None),
            P(("groups", "lat"), None),
            P(),
        ),
        out_specs=(P(("groups", "mem"), None, "lat", None), P("groups", "lat", None)),
        check_vma=False,
    )
```

```python
import functools
import math

import jax
import jax.numpy as jnp
from jax import lax
from jax.experimental import pallas as pl
from jax.experimental.pallas import tpu as pltpu
from jax.sharding import PartitionSpec as P

STEPS = 4
SMOOTH = 16
LOG_TWO_PI = 1.8378770664093453
MESH = pl.DeviceIdType.MESH
TILE_ROWS = 16
TILE_COLS = 128
OBS_BLOCK = 8192
TOGETHER = 4
SHARERS = 4
LEVELS = 32760.0
OCTAVE = 128.0
TINY = 1e-33


def pieces(values):
    high = values.astype(jnp.bfloat16).astype(jnp.float32)
    rest = values - high
    mid = rest.astype(jnp.bfloat16).astype(jnp.float32)
    return high, mid, rest - mid


def partial_grids(rows, width, cells, mask, values, error):
    count = cells.shape[1]
    used = mask.astype(jnp.float32)
    inverse = used / (error * error)
    terms = (
        inverse,
        inverse * values,
        inverse * values * values + used * (2.0 * jnp.log(error) + LOG_TWO_PI),
    )
    row = cells // width
    column = cells - row * width
    short = jnp.int16
    row_hit = lax.broadcasted_iota(short, (rows, count), 0) == row.astype(short)
    column_hit = lax.broadcasted_iota(short, (width, count), 0) == column.astype(short)
    one, none = jnp.ones((), jnp.bfloat16), jnp.zeros((), jnp.bfloat16)
    column_hit = jnp.where(column_hit, one, none)
    left = jnp.concatenate(
        [
            jnp.where(row_hit, piece.astype(jnp.bfloat16), none)
            for piece in pieces(terms[0]) + pieces(terms[1]) + pieces(terms[2])[:2]
        ],
        axis=0,
    )
    return lax.dot_general(
        left, column_hit, (((1,), (1,)), ((), ())), preferred_element_type=jnp.float32
    )


def cut(values):
    return [piece.astype(jnp.bfloat16) for piece in pieces(values)]


def one_hot(hit):
    return jnp.where(hit, 1.0, 0.0).astype(jnp.bfloat16)


def permute(values, matrix):
    return jnp.dot(values, matrix, preferred_element_type=jnp.float32)


def kernel_values(offset):
    values = jnp.exp(-((2.0 * offset.astype(jnp.float32) / SMOOTH) ** 2))
    return jnp.where(jnp.abs(offset) <= SMOOTH, values, 0.0)


def encode(means):
    top = functools.reduce(jnp.maximum, [jnp.abs(mean) for mean in means])
    code = jnp.ceil(jnp.log(jnp.maximum(top, TINY)) * (OCTAVE / math.log(2.0))) + 1.0
    levels = LEVELS * jnp.exp(code * (-math.log(2.0) / OCTAVE))
    whole = [jnp.floor(mean * levels + 0.5) for mean in means] + [code]
    return [value.astype(jnp.int32).astype(jnp.int16) for value in whole]


def integer(ref):
    return ref.astype(jnp.int32).astype(jnp.float32)


def scale_of(code):
    return jnp.exp(integer(code) * (math.log(2.0) / OCTAVE)) * (1.0 / LEVELS)


def cycle_kernel(
    n,
    state_ref,
    counts_ref,
    east_ref,
    north_ref,
    cells_ref,
    mask_ref,
    values_ref,
    error_ref,
    relax_ref,
    out_ref,
    mean_ref,
    cells,
    mask,
    values,
    error,
    state,
    count,
    factors,
    counted,
    obs_send,
    obs_recv,
    grids,
    halo,
    wind_in,
    wind_halo,
    winds,
    spread_columns,
    gather_columns,
    lines,
    moved,
    advected,
    lon_kernel,
    loglik,
    loglik_halo,
    scores,
    held,
    send,
    send_log,
    recv,
    recv_log,
    merged,
    halo_sems,
    send_sems,
    recv_sems,
    send_log_sems,
    recv_log_sems,
    back_send,
    back_recv,
    relay_send,
    local_sems,
    obs_sems,
    obs_arrived,
    grid_sems,
    grid_arrived,
):
    slots, fields, rows, width = state_ref.shape
    across = width // TILE_COLS
    owners = (rows // TILE_ROWS) * across
    me = lax.axis_index("mem")
    band = lax.axis_index("lat")
    other = 1 - band

    share = cells.shape[1]
    rank = lax.rem(me, SHARERS)
    first_rank = me - rank
    mine = pl.ds(pl.multiple_of(rank * share, 128), share)
    loads = [
        pltpu.make_async_copy(source, target, local_sems.at[k])
        for k, (source, target) in enumerate(
            (
                (cells_ref.at[:, mine], cells),
                (mask_ref.at[:, mine], mask),
                (values_ref.at[:, mine], values),
                (error_ref.at[:, mine], error),
                (state_ref, state),
                (east_ref, wind_in.at[0]),
                (north_ref, wind_in.at[1]),
                (counts_ref, count),
                (relax_ref, factors),
            )
        )
    ]
    for load in loads:
        load.start()

    barrier = pltpu.get_barrier_semaphore()

    def greet(d, carry):
        pl.semaphore_signal(
            barrier, inc=1, device_id={"mem": lax.rem(me + d, n)}, device_id_type=MESH
        )
        return carry

    pl.semaphore_signal(barrier, inc=1, device_id={"lat": other}, device_id_type=MESH)
    lax.fori_loop(1, n, greet, 0)

    i0 = lax.broadcasted_iota(jnp.int32, (width, width), 0)
    i1 = lax.broadcasted_iota(jnp.int32, (width, width), 1)
    spread_columns[...] = one_hot(i0 == (width // TILE_COLS) * lax.rem(i1, TILE_COLS) + i1 // TILE_COLS)
    gather_columns[...] = one_hot(i1 == (width // TILE_COLS) * lax.rem(i0, TILE_COLS) + i0 // TILE_COLS)
    near0 = lax.broadcasted_iota(jnp.int32, (2 * TILE_COLS, TILE_COLS), 0)
    near1 = lax.broadcasted_iota(jnp.int32, (2 * TILE_COLS, TILE_COLS), 1)
    for k, piece in enumerate(cut(kernel_values(near0 - TILE_COLS // 2 - near1))):
        lon_kernel[:, k * TILE_COLS : (k + 1) * TILE_COLS] = piece

    for load in loads[5:]:
        load.wait()
    pl.semaphore_wait(barrier, n)

    def to_other(source, target, slot):
        copy = pltpu.make_async_remote_copy(
            src_ref=source,
            dst_ref=target,
            send_sem=halo_sems.at[0, slot],
            recv_sem=halo_sems.at[1, slot],
            device_id={"lat": other},
            device_id_type=MESH,
        )
        copy.start()
        return copy

    edge16 = pl.ds(pl.multiple_of(other * (rows - 16), 16), 16)
    edge8 = pl.ds(pl.multiple_of(other * (rows - 8), 8), 8)
    copy_winds = to_other(wind_in.at[:, edge8, :], wind_halo, 0)
    copy_state = to_other(state_ref.at[:, :, edge16, :], halo, 1)

    def tile(t):
        down = t // across
        return (
            pl.ds(pl.multiple_of(down * TILE_ROWS, TILE_ROWS), TILE_ROWS),
            pl.ds(pl.multiple_of((t - down * across) * TILE_COLS, TILE_COLS), TILE_COLS),
        )

    for load in loads[:4]:
        load.wait()
    block = min(share, OBS_BLOCK)

    def count_block(index, carry):
        at = pl.ds(pl.multiple_of(index * block, 128), block)
        part = partial_grids(rows, width, *(ref[:, at] for ref in (cells, mask, values, error)))
        for term, (base, number) in enumerate(((0, 3), (3, 3), (6, 2))):
            counted[term] += functools.reduce(
                jnp.add, [part[(base + k) * rows : (base + k + 1) * rows] for k in range(number)]
            )
        return carry

    counted[...] = jnp.zeros_like(counted)
    lax.fori_loop(0, share // block, count_block, 0)
    held_tiles = owners // SHARERS

    def near_by(d):
        one_on = rank + 1 - 2 * lax.rem(rank, 2)
        across_block = lax.rem(rank + SHARERS // 2, SHARERS)
        opposite = SHARERS - 1 - rank
        return jnp.where(
            d == 1, opposite, jnp.where(d == 2, across_block, jnp.where(d == 3, one_on, rank))
        )

    def obs_out(d):
        return pltpu.make_async_remote_copy(
            src_ref=obs_send.at[near_by(d)],
            dst_ref=obs_recv.at[rank],
            send_sem=obs_sems.at[near_by(d)],
            recv_sem=obs_arrived.at[rank],
            device_id={"mem": first_rank + near_by(d)},
            device_id_type=MESH,
        )

    def give(d, carry):
        for k in range(held_tiles):
            down, along = tile(held_tiles * near_by(d) + k)
            for term in range(3):
                obs_send[near_by(d), k, term] = counted[term, down, along]

        @pl.when(d < SHARERS)
        def _():
            obs_out(d).start()

        return carry

    lax.fori_loop(1, SHARERS + 1, give, 0)

    def grid_out(d):
        return pltpu.make_async_remote_copy(
            src_ref=grids.at[rank],
            dst_ref=grids.at[rank],
            send_sem=grid_sems.at[d],
            recv_sem=grid_arrived.at[rank],
            device_id={"mem": first_rank + near_by(d)},
            device_id_type=MESH,
        )

    near = lax.broadcasted_iota(jnp.int32, (8, width), 0)
    keep = jnp.where(band == 0, near, 7 - near) < STEPS

    layers = (rows + 8) // 8

    def columns(c):
        return slice(c * TILE_COLS, (c + 1) * TILE_COLS)

    def spread(ref, c):
        return jnp.stack([ref[c, pl.ds(k, 8, stride=layers), :] for k in range(layers)])

    copy_winds.wait()
    split = []
    for kind in range(2):
        far = jnp.where(keep, wind_halo[kind], 0.0)
        split += pieces(jnp.concatenate([wind_in[kind], far], axis=0))
    split = permute(
        jnp.concatenate([piece.astype(jnp.bfloat16) for piece in split], axis=0),
        spread_columns[...],
    ).reshape(2, 3, rows + 8, width)
    for kind in range(2):
        whole = (split[kind, 0] + split[kind, 1]) + split[kind, 2]
        for c in range(across):
            lines[0, kind, c] = whole[:, columns(c)]
            wind = spread(lines.at[0, kind], c)
            winds[2 * kind, c] = jnp.abs(wind)
            winds[2 * kind + 1, c] = wind
    loads[4].wait()
    copy_state.wait()

    def lay_out(slot, carry):
        whole = permute(
            jnp.concatenate(
                [state[slot].reshape(fields * rows, width), halo[slot].reshape(fields * 16, width)],
                axis=0,
            ),
            spread_columns[...],
        )
        own = whole[: fields * rows].reshape(fields, rows, width)
        far = whole[fields * rows :].reshape(fields, 16, width)
        far = jnp.where(band == 0, far[:, :8], far[:, 8:])
        for c in range(across):
            lines[slot, :, c, :rows] = own[:, :, columns(c)]
            lines[slot, :, c, rows:] = jnp.where(keep[:, columns(c)], far[:, :, columns(c)], 0.0)
        return carry

    lax.fori_loop(0, slots, lay_out, 0)

    def step(x):
        west = [pltpu.roll(x[across - 1], 1, 2)] + x[:-1]
        east = x[1:] + [pltpu.roll(x[0], TILE_COLS - 1, 2)]
        south = [
            jnp.concatenate([pltpu.roll(v[layers - 1 :], 1, 1), v[: layers - 1]], axis=0) for v in x
        ]
        north = [jnp.concatenate([v[1:], pltpu.roll(v[:1], 7, 1)], axis=0) for v in x]
        return [
            x[c]
            - winds[0, c] * (x[c] - jnp.where(winds[1, c] > 0.0, west[c], east[c]))
            - winds[2, c] * (x[c] - jnp.where(winds[3, c] > 0.0, south[c], north[c]))
            for c in range(across)
        ]

    def move(index, carry):
        kind = index // (slots // TOGETHER)
        first = TOGETHER * lax.rem(index, slots // TOGETHER)
        fields_of = [lines.at[first + k, kind] for k in range(TOGETHER)]
        xs = [[spread(field, c) for c in range(across)] for field in fields_of]
        for _ in range(STEPS):
            xs = [step(x) for x in xs]
        for k, (field, x) in enumerate(zip(fields_of, xs)):
            for c in range(across):
                for layer in range(layers):
                    field[c, pl.ds(layer, 8, stride=layers), :] = x[c][layer]
                moved[kind, first + k, :, columns(c)] = field[c, :rows].astype(jnp.bfloat16)
        return carry

    def collect(first, last):
        whole = moved[first:last].reshape((last - first) * slots * rows, width)
        whole = permute(whole, gather_columns[...]).astype(jnp.bfloat16)
        advected[first:last] = whole.reshape(last - first, slots, rows, width)

    total = fields * (slots // TOGETHER)
    early = total // 8
    lax.fori_loop(0, slots // TOGETHER, move, 0)
    collect(0, 1)
    lax.fori_loop(slots // TOGETHER, early, move, 0)

    def arrive(d, carry):
        source = near_by(d)
        pltpu.make_async_remote_copy(
            src_ref=obs_send.at[0],
            dst_ref=obs_recv.at[source],
            send_sem=obs_sems.at[0],
            recv_sem=obs_arrived.at[source],
            device_id={"mem": first_rank + source},
            device_id_type=MESH,
        ).wait_recv()
        return carry

    lax.fori_loop(1, SHARERS, arrive, 0)
    obs_recv[rank] = obs_send[rank]
    grids[rank] = functools.reduce(jnp.add, [obs_recv[k] for k in range(SHARERS)])
    for d in range(1, SHARERS):
        grid_out(d).start()

    lax.fori_loop(early, total, move, 0)

    collect(1, fields)

    def likely(index, carry):
        source = lax.rem(index + (1 - band) * (SHARERS // 2), SHARERS)

        @pl.when(source != rank)
        def _():
            pltpu.make_async_remote_copy(
                src_ref=grids.at[source],
                dst_ref=grids.at[source],
                send_sem=grid_sems.at[0],
                recv_sem=grid_arrived.at[source],
                device_id={"mem": first_rank + source},
                device_id_type=MESH,
            ).wait_recv()

        for k in range(held_tiles):
            down, along = tile(held_tiles * source + k)
            inverse, linear, constant = (grids[source, k, term] for term in range(3))
            for slot in range(slots):
                value = advected[0, slot, down, along].astype(jnp.float32)
                loglik[slot, down, along] = -0.5 * (
                    inverse * value * value - 2.0 * linear * value + constant
                )
        return carry

    lax.fori_loop(0, SHARERS // 2, likely, 0)
    copy_loglik = to_other(loglik.at[:, edge16, :], loglik_halo, 2)
    lax.fori_loop(SHARERS // 2, SHARERS, likely, 0)

    r0 = lax.broadcasted_iota(jnp.int32, (rows, rows), 0)
    r1 = lax.broadcasted_iota(jnp.int32, (rows, rows), 1)
    own_band = kernel_values(r0 - r1)
    h0 = lax.broadcasted_iota(jnp.int32, (rows, 16), 0)
    h1 = lax.broadcasted_iota(jnp.int32, (rows, 16), 1)
    far_band = kernel_values(jnp.where(band == 0, rows + h1 - h0, h0 + 16 - h1))
    dot = functools.partial(
        jnp.dot, precision=lax.Precision.HIGHEST, preferred_element_type=jnp.float32
    )
    own_part = [dot(own_band, loglik[slot]) for slot in range(slots)]
    copy_loglik.wait()
    smoothed = jnp.concatenate(
        [own_part[slot] + dot(far_band, loglik_halo[slot]) for slot in range(slots)], axis=0
    )
    tall = slots * rows
    smoothed = pltpu.roll(smoothed, TILE_COLS // 2, 1)
    parts = []
    for piece in cut(smoothed):
        around = jnp.concatenate([piece, piece[:, :TILE_COLS]], axis=1)
        parts += [
            around[:, c * TILE_COLS : (c + 2) * TILE_COLS] for c in range(across)
        ]
    one = permute(jnp.concatenate(parts, axis=0), lon_kernel[:, : 2 * TILE_COLS])
    three = permute(jnp.concatenate(parts[:across], axis=0), lon_kernel[:, 2 * TILE_COLS :])
    high, mid, low = (one[k * across * tall : (k + 1) * across * tall] for k in range(3))
    result = high[:, :TILE_COLS] + (
        (high[:, TILE_COLS:] + mid[:, :TILE_COLS])
        + ((mid[:, TILE_COLS:] + low[:, :TILE_COLS]) + three)
    )
    for c in range(across):
        scores[:, :, columns(c)] = result[c * tall : (c + 1) * tall].reshape(slots, rows, TILE_COLS)


    partner = me + 1 - 2 * lax.rem(me, 2)
    parity = lax.rem(me, 2)

    half = n // 2

    def copies(t, slot, target):
        return [
            pltpu.make_async_remote_copy(
                src_ref=source.at[t],
                dst_ref=landing.at[slot],
                send_sem=sent_sems.at[t],
                recv_sem=landed_sems.at[slot],
                device_id={"mem": target},
                device_id_type=MESH,
            )
            for source, landing, sent_sems, landed_sems in (
                (send, recv, send_sems, recv_sems),
                (send_log, recv_log, send_log_sems, recv_log_sems),
            )
        ]

    def outgoing(t):
        return copies(t, me // 2, t)

    def across_pair(t):
        return copies(t, half + t // 2, partner)

    def start_all(made):
        for copy in made:
            copy.start()

    def gather(t):
        down, along = tile(t)
        live = [
            jnp.where(slot < count[0], scores[slot, down, along], -jnp.inf)
            for slot in range(slots)
        ]
        peak = functools.reduce(jnp.maximum, live)
        gains = [jnp.exp(score - peak) for score in live]
        weighted = [
            functools.reduce(
                jnp.add,
                [
                    gains[slot] * advected[kind, slot, down, along].astype(jnp.float32)
                    for slot in range(slots)
                ],
            )
            for kind in range(fields)
        ]
        return weighted, functools.reduce(jnp.add, gains), peak

    def put(t, weighted, total, peak):
        send_log[t] = peak + jnp.log(total)
        inverse = 1.0 / total
        for plane, value in enumerate(encode([value * inverse for value in weighted])):
            send[t, plane] = value

    def hold(t, weighted, total, peak):
        for plane, value in enumerate(weighted + [total, peak]):
            held[t // 2, plane] = value

    middle = owners // 2
    place = lax.rem(me // 2, middle)

    def near_to_far(k):
        ups, downs = middle - 1 - place, place
        both = jnp.minimum(ups, downs)
        upward = jnp.where(ups > downs, k - both, 0 - (k - both))
        paired = jnp.where(lax.rem(k, 2) == 1, (k + 1) // 2, 0 - (k // 2))
        return lax.rem(jnp.where(k <= 2 * both, paired, upward) + middle, middle)

    def turn(j):
        return 2 * near_to_far(middle - 1 - j)

    def give_pair(j, carry):
        t = lax.rem(partner + turn(j), owners)
        put(t, *gather(t))
        start_all(across_pair(t))
        return carry

    def keep_own(j, carry):
        t = 2 * j + parity
        hold(t, *gather(t))
        return carry

    def merge(t, slot):
        low, high = held[t // 2, fields + 1], recv_log[slot]
        peak = jnp.maximum(low, high)
        low, high = jnp.exp(low - peak), jnp.exp(high - peak)
        scaled = high * scale_of(recv[slot, fields])
        weighted = [
            low * held[t // 2, kind] + scaled * integer(recv[slot, kind])
            for kind in range(fields)
        ]
        return weighted, low * held[t // 2, fields] + high, peak

    def give_owner(j, carry):
        t = lax.rem(me + turn(j), owners)
        for copy in across_pair(t):
            copy.wait_recv()
        sums = merge(t, half + t // 2)

        @pl.when(t != me)
        def _():
            put(t, *sums)
            start_all(outgoing(t))

        @pl.when(t == me)
        def _():
            hold(t, *sums)

        return carry

    for j in range(middle):
        give_pair(j, 0)
    for j in range(middle):
        keep_own(j, 0)
    lax.fori_loop(0, owners // 2, give_owner, 0)

    def back(d):
        return pltpu.make_async_remote_copy(
            src_ref=merged.at[me],
            dst_ref=merged.at[me],
            send_sem=back_send.at[d],
            recv_sem=back_recv.at[me],
            device_id={"mem": lax.rem(me + 2 * d, n)},
            device_id_type=MESH,
        )

    def relay(t):
        return pltpu.make_async_remote_copy(
            src_ref=merged.at[t],
            dst_ref=merged.at[t],
            send_sem=relay_send.at[t],
            recv_sem=back_recv.at[t],
            device_id={"mem": partner},
            device_id_type=MESH,
        )

    @pl.when(me < owners)
    def _():
        def arrive(d, carry):
            source = lax.rem(me + 2 * d, n)
            for copy in copies(0, source // 2, source):
                copy.wait_recv()
            return carry

        lax.fori_loop(1, half, arrive, 0)
        own = me // 2
        peak = lax.fori_loop(
            1,
            half,
            lambda d, top: jnp.maximum(top, recv_log[lax.rem(own + d, half)]),
            held[own, fields + 1],
        )

        def add(d, sums):
            slot = lax.rem(own + d, half)
            factor = jnp.exp(recv_log[slot] - peak)
            scaled = factor * scale_of(recv[slot, fields])
            return tuple(
                sums[kind] + scaled * integer(recv[slot, kind]) for kind in range(fields)
            ) + (sums[fields] + factor,)

        factor = jnp.exp(held[own, fields + 1] - peak)
        sums = lax.fori_loop(
            1, half, add, tuple(factor * held[own, plane] for plane in range(fields + 1))
        )
        inverse = 1.0 / sums[fields]
        for plane, value in enumerate(encode([sums[kind] * inverse for kind in range(fields)])):
            merged[me, plane] = value

        def start(d, carry):
            back(jnp.where(2 * place < middle, half - d, d)).start()
            return carry

        lax.fori_loop(1, half, start, 0)

    def landed(t):
        @pl.when(t != me)
        def _():
            relay(t).wait_recv()

    def place_of(start, k):
        return lax.rem(start + 2 * near_to_far(k), owners)

    def pass_on(k, carry):
        t = place_of(me, k)
        landed(t)
        relay(t).start()
        return carry

    def finish_passed(k, carry):
        finish(place_of(me, k))
        return carry

    def accept(k, carry):
        t = place_of(partner, k)
        landed(t)
        finish(t)
        return carry

    def finish(t):
        down, along = tile(t)
        scale = scale_of(merged[t, fields])
        for kind in range(fields):
            mean = scale * integer(merged[t, kind])
            mean_ref[kind, down, along] = mean.astype(jnp.bfloat16)
            for slot in range(slots):
                value = advected[kind, slot, down, along].astype(jnp.float32)
                fresh = value + factors[kind] * (mean - value)
                out_ref[slot, kind, down, along] = jnp.where(
                    slot < count[0], fresh, 0.0
                ).astype(jnp.bfloat16)

    for d in range(1, SHARERS):
        obs_out(d).wait_send()
        grid_out(d).wait_send()

    def passed(j, carry):
        for copy in across_pair(2 * j + 1 - parity):
            copy.wait_send()

        @pl.when(2 * j + parity != me)
        def _():
            for copy in outgoing(2 * j + parity):
                copy.wait_send()

        return carry

    lax.fori_loop(0, owners // 2, passed, 0)
    pass_on(0, 0)
    finish(place_of(me, 0))
    lax.fori_loop(1, middle, pass_on, 0)
    lax.fori_loop(1, middle, finish_passed, 0)
    lax.fori_loop(0, middle, accept, 0)

    def relayed(j, carry):
        relay(2 * j + parity).wait_send()
        return carry

    lax.fori_loop(0, middle, relayed, 0)

    @pl.when(me < owners)
    def _():
        def sent_back(d, carry):
            back(d).wait_send()
            return carry

        lax.fori_loop(1, n // 2, sent_back, 0)


def cycle(n, state, counts, east_wind, north_wind, obs, relax):
    slots, fields, rows, width = state.shape
    across = width // TILE_COLS
    owners = (rows // TILE_ROWS) * across
    share = obs[0].shape[1] // SHARERS
    held_tiles = owners // SHARERS
    tile = (TILE_ROWS, TILE_COLS)
    hbm = pl.BlockSpec(memory_space=pl.ANY)
    vmem = pl.BlockSpec(memory_space=pltpu.VMEM)
    f32, bf16 = jnp.float32, jnp.bfloat16
    return pl.pallas_call(
        functools.partial(cycle_kernel, n),
        out_shape=(
            pltpu.VMEM(state.shape, bf16),
            pltpu.VMEM((fields, rows, width), bf16),
        ),
        in_specs=[hbm] * 9,
        out_specs=(vmem, vmem),
        scratch_shapes=[
            pltpu.VMEM((1, share), jnp.int32),
            pltpu.VMEM((1, share), jnp.int32),
            pltpu.VMEM((1, share), f32),
            pltpu.VMEM((1, share), f32),
            pltpu.VMEM(state.shape, bf16),
            pltpu.SMEM(counts.shape, counts.dtype),
            pltpu.SMEM(relax.shape, relax.dtype),
            pltpu.VMEM((3, rows, width), f32),
            pltpu.VMEM((SHARERS, held_tiles, 3) + tile, f32),
            pltpu.VMEM((SHARERS, held_tiles, 3) + tile, f32),
            pltpu.VMEM((SHARERS, held_tiles, 3) + tile, f32),
            pltpu.VMEM((slots, fields, 16, width), bf16),
            pltpu.VMEM((2, rows, width), f32),
            pltpu.VMEM((2, 8, width), f32),
            pltpu.VMEM((4, across, (rows + 8) // 8, 8, TILE_COLS), f32),
            pltpu.VMEM((width, width), bf16),
            pltpu.VMEM((width, width), bf16),
            pltpu.VMEM((slots, fields, across, rows + 8, TILE_COLS), f32),
            pltpu.VMEM((fields, slots, rows, width), bf16),
            pltpu.VMEM((fields, slots, rows, width), bf16),
            pltpu.VMEM((2 * TILE_COLS, 3 * TILE_COLS), bf16),
            pltpu.VMEM((slots, rows, width), f32),
            pltpu.VMEM((slots, 16, width), f32),
            pltpu.VMEM((slots, rows, width), f32),
            pltpu.VMEM((owners // 2, fields + 2) + tile, f32),
            pltpu.VMEM((owners, fields + 1) + tile, jnp.int16),
            pltpu.VMEM((owners,) + tile, f32),
            pltpu.VMEM((n // 2 + owners // 2, fields + 1) + tile, jnp.int16),
            pltpu.VMEM((n // 2 + owners // 2,) + tile, f32),
            pltpu.VMEM((owners, fields + 1) + tile, jnp.int16),
            pltpu.SemaphoreType.DMA((2, 3)),
            pltpu.SemaphoreType.DMA((owners,)),
            pltpu.SemaphoreType.DMA((n // 2 + owners // 2,)),
            pltpu.SemaphoreType.DMA((owners,)),
            pltpu.SemaphoreType.DMA((n // 2 + owners // 2,)),
            pltpu.SemaphoreType.DMA((n,)),
            pltpu.SemaphoreType.DMA((owners,)),
            pltpu.SemaphoreType.DMA((owners,)),
            pltpu.SemaphoreType.DMA((9,)),
            pltpu.SemaphoreType.DMA((SHARERS,)),
            pltpu.SemaphoreType.DMA((SHARERS,)),
            pltpu.SemaphoreType.DMA((SHARERS,)),
            pltpu.SemaphoreType.DMA((SHARERS,)),
        ],
        compiler_params=pltpu.CompilerParams(
            collective_id=0, has_side_effects=True, vmem_limit_bytes=56 * 1024 * 1024
        ),
    )(state, counts, east_wind, north_wind, *obs, relax)


def write_kernel(fresh, mean, out, mean_out, sems):
    copies = [
        pltpu.make_async_copy(fresh, out, sems.at[0]),
        pltpu.make_async_copy(mean, mean_out, sems.at[1]),
    ]
    for copy in copies:
        copy.start()
    for copy in copies:
        copy.wait()


def write_out(fresh, mean):
    hbm = pl.BlockSpec(memory_space=pl.ANY)
    return pl.pallas_call(
        write_kernel,
        out_shape=(
            jax.ShapeDtypeStruct(fresh.shape, fresh.dtype),
            jax.ShapeDtypeStruct(mean.shape, mean.dtype),
        ),
        in_specs=[hbm, hbm],
        out_specs=(hbm, hbm),
        scratch_shapes=[pltpu.SemaphoreType.DMA((2,))],
    )(*(pltpu.with_memory_space_constraint(x, pltpu.VMEM) for x in (fresh, mean)))


def on_device(
    n, state, counts, east_wind, north_wind, obs_cells, obs_mask, obs_values, obs_error, relax
):
    obs = (obs_cells, obs_mask, obs_values, obs_error)
    fresh, mean = cycle(n, state, counts, east_wind, north_wind, obs, relax)
    return write_out(fresh, mean)


def solution(mesh):
    return jax.shard_map(
        functools.partial(on_device, mesh.shape["mem"]),
        mesh=mesh,
        in_specs=(
            P(("groups", "mem"), None, "lat", None),
            P(("groups", "mem")),
            P(("groups", "lat"), None),
            P(("groups", "lat"), None),
            P(("groups", "lat"), None),
            P(("groups", "lat"), None),
            P(("groups", "lat"), None),
            P(("groups", "lat"), None),
            P(),
        ),
        out_specs=(P(("groups", "mem"), None, "lat", None), P("groups", "lat", None)),
        check_vma=False,
    )
```

```python
import functools
import math

import jax
import jax.numpy as jnp
from jax import lax
from jax.experimental import pallas as pl
from jax.experimental.pallas import tpu as pltpu
from jax.sharding import PartitionSpec as P

STEPS = 4
SMOOTH = 16
LOG_TWO_PI = 1.8378770664093453
MESH = pl.DeviceIdType.MESH
TILE_ROWS = 16
TILE_COLS = 128
OBS_BLOCK = 8192
TOGETHER = 4
SHARERS = 4
LEVELS = 32760.0
OCTAVE = 128.0
TINY = 1e-33


def pieces(values):
    high = values.astype(jnp.bfloat16).astype(jnp.float32)
    rest = values - high
    mid = rest.astype(jnp.bfloat16).astype(jnp.float32)
    return high, mid, rest - mid


def partial_grids(rows, width, cells, mask, values, error):
    count = cells.shape[1]
    used = mask.astype(jnp.float32)
    inverse = used / (error * error)
    terms = (
        inverse,
        inverse * values,
        inverse * values * values + used * (2.0 * jnp.log(error) + LOG_TWO_PI),
    )
    row = cells // width
    column = cells - row * width
    row_hit = lax.broadcasted_iota(jnp.int32, (rows, count), 0) == row
    column_hit = jnp.where(
        lax.broadcasted_iota(jnp.int32, (width, count), 0) == column, 1.0, 0.0
    ).astype(jnp.bfloat16)
    left = jnp.concatenate(
        [
            jnp.where(row_hit, piece, 0.0).astype(jnp.bfloat16)
            for piece in pieces(terms[0]) + pieces(terms[1]) + pieces(terms[2])[:2]
        ],
        axis=0,
    )
    return lax.dot_general(
        left, column_hit, (((1,), (1,)), ((), ())), preferred_element_type=jnp.float32
    )


def one_hot(hit):
    return jnp.where(hit, 1.0, 0.0).astype(jnp.bfloat16)


def permute(values, matrix):
    return jnp.dot(values, matrix, preferred_element_type=jnp.float32)


def kernel_values(offset):
    values = jnp.exp(-((2.0 * offset.astype(jnp.float32) / SMOOTH) ** 2))
    return jnp.where(jnp.abs(offset) <= SMOOTH, values, 0.0)


def encode(means):
    top = functools.reduce(jnp.maximum, [jnp.abs(mean) for mean in means])
    code = jnp.ceil(jnp.log(jnp.maximum(top, TINY)) * (OCTAVE / math.log(2.0))) + 1.0
    levels = LEVELS * jnp.exp(code * (-math.log(2.0) / OCTAVE))
    whole = [jnp.floor(mean * levels + 0.5) for mean in means] + [code]
    return [value.astype(jnp.int32).astype(jnp.int16) for value in whole]


def integer(ref):
    return ref.astype(jnp.int32).astype(jnp.float32)


def scale_of(code):
    return jnp.exp(integer(code) * (math.log(2.0) / OCTAVE)) * (1.0 / LEVELS)


def cycle_kernel(
    n,
    state_ref,
    counts_ref,
    east_ref,
    north_ref,
    cells_ref,
    mask_ref,
    values_ref,
    error_ref,
    relax_ref,
    out_ref,
    mean_ref,
    cells,
    mask,
    values,
    error,
    state,
    count,
    factors,
    counted,
    obs_send,
    obs_recv,
    grids,
    halo,
    wind_in,
    wind_halo,
    winds,
    spread_columns,
    gather_columns,
    lines,
    moved,
    advected,
    lon_kernel,
    loglik,
    loglik_halo,
    scores,
    held,
    send,
    send_log,
    recv,
    recv_log,
    merged,
    halo_sems,
    send_sems,
    recv_sems,
    send_log_sems,
    recv_log_sems,
    back_send,
    back_recv,
    relay_send,
    local_sems,
    obs_sems,
    obs_arrived,
    grid_sems,
    grid_arrived,
):
    slots, fields, rows, width = state_ref.shape
    across = width // TILE_COLS
    owners = (rows // TILE_ROWS) * across
    me = lax.axis_index("mem")
    band = lax.axis_index("lat")
    other = 1 - band

    share = cells.shape[1]
    rank = lax.rem(me, SHARERS)
    first_rank = me - rank
    mine = pl.ds(pl.multiple_of(rank * share, 128), share)
    loads = [
        pltpu.make_async_copy(source, target, local_sems.at[k])
        for k, (source, target) in enumerate(
            (
                (cells_ref.at[:, mine], cells),
                (mask_ref.at[:, mine], mask),
                (values_ref.at[:, mine], values),
                (error_ref.at[:, mine], error),
                (state_ref, state),
                (east_ref, wind_in.at[0]),
                (north_ref, wind_in.at[1]),
                (counts_ref, count),
                (relax_ref, factors),
            )
        )
    ]
    for load in loads:
        load.start()

    barrier = pltpu.get_barrier_semaphore()

    def greet(d, carry):
        pl.semaphore_signal(
            barrier, inc=1, device_id={"mem": lax.rem(me + d, n)}, device_id_type=MESH
        )
        return carry

    pl.semaphore_signal(barrier, inc=1, device_id={"lat": other}, device_id_type=MESH)
    lax.fori_loop(1, n, greet, 0)

    for load in loads[5:]:
        load.wait()
    pl.semaphore_wait(barrier, n)

    def to_other(source, target, slot):
        copy = pltpu.make_async_remote_copy(
            src_ref=source,
            dst_ref=target,
            send_sem=halo_sems.at[0, slot],
            recv_sem=halo_sems.at[1, slot],
            device_id={"lat": other},
            device_id_type=MESH,
        )
        copy.start()
        return copy

    edge16 = pl.ds(pl.multiple_of(other * (rows - 16), 16), 16)
    edge8 = pl.ds(pl.multiple_of(other * (rows - 8), 8), 8)
    copy_winds = to_other(wind_in.at[:, edge8, :], wind_halo, 0)
    copy_state = to_other(state_ref.at[:, :, edge16, :], halo, 1)

    def tile(t):
        down = t // across
        return (
            pl.ds(pl.multiple_of(down * TILE_ROWS, TILE_ROWS), TILE_ROWS),
            pl.ds(pl.multiple_of((t - down * across) * TILE_COLS, TILE_COLS), TILE_COLS),
        )

    for load in loads[:4]:
        load.wait()
    block = min(share, OBS_BLOCK)

    def count_block(index, carry):
        at = pl.ds(pl.multiple_of(index * block, 128), block)
        part = partial_grids(rows, width, *(ref[:, at] for ref in (cells, mask, values, error)))
        for term, (base, number) in enumerate(((0, 3), (3, 3), (6, 2))):
            counted[term] += functools.reduce(
                jnp.add, [part[(base + k) * rows : (base + k + 1) * rows] for k in range(number)]
            )
        return carry

    counted[...] = jnp.zeros_like(counted)
    lax.fori_loop(0, share // block, count_block, 0)
    held_tiles = owners // SHARERS

    def near_by(d):
        one_on = rank + 1 - 2 * lax.rem(rank, 2)
        across_block = lax.rem(rank + SHARERS // 2, SHARERS)
        opposite = SHARERS - 1 - rank
        return jnp.where(
            d == 1, opposite, jnp.where(d == 2, across_block, jnp.where(d == 3, one_on, rank))
        )

    def obs_out(d):
        return pltpu.make_async_remote_copy(
            src_ref=obs_send.at[near_by(d)],
            dst_ref=obs_recv.at[rank],
            send_sem=obs_sems.at[near_by(d)],
            recv_sem=obs_arrived.at[rank],
            device_id={"mem": first_rank + near_by(d)},
            device_id_type=MESH,
        )

    def give(d, carry):
        for k in range(held_tiles):
            down, along = tile(held_tiles * near_by(d) + k)
            for term in range(3):
                obs_send[near_by(d), k, term] = counted[term, down, along]

        @pl.when(d < SHARERS)
        def _():
            obs_out(d).start()

        return carry

    lax.fori_loop(1, SHARERS + 1, give, 0)

    def grid_out(d):
        return pltpu.make_async_remote_copy(
            src_ref=grids.at[rank],
            dst_ref=grids.at[rank],
            send_sem=grid_sems.at[d],
            recv_sem=grid_arrived.at[rank],
            device_id={"mem": first_rank + near_by(d)},
            device_id_type=MESH,
        )

    i0 = lax.broadcasted_iota(jnp.int32, (width, width), 0)
    i1 = lax.broadcasted_iota(jnp.int32, (width, width), 1)
    spread_columns[...] = one_hot(i0 == across * lax.rem(i1, TILE_COLS) + i1 // TILE_COLS)
    gather_columns[...] = one_hot(i1 == across * lax.rem(i0, TILE_COLS) + i0 // TILE_COLS)
    apart = jnp.abs(i0 - i1)
    lon_kernel[...] = kernel_values(jnp.minimum(apart, width - apart))

    near = lax.broadcasted_iota(jnp.int32, (8, width), 0)
    keep = jnp.where(band == 0, near, 7 - near) < STEPS

    layers = (rows + 8) // 8

    def columns(c):
        return slice(c * TILE_COLS, (c + 1) * TILE_COLS)

    def spread(ref, c):
        return jnp.stack([ref[c, pl.ds(k, 8, stride=layers), :] for k in range(layers)])

    copy_winds.wait()
    split = []
    for kind in range(2):
        far = jnp.where(keep, wind_halo[kind], 0.0)
        split += pieces(jnp.concatenate([wind_in[kind], far], axis=0))
    split = permute(
        jnp.concatenate([piece.astype(jnp.bfloat16) for piece in split], axis=0),
        spread_columns[...],
    ).reshape(2, 3, rows + 8, width)
    for kind in range(2):
        whole = (split[kind, 0] + split[kind, 1]) + split[kind, 2]
        for c in range(across):
            lines[0, kind, c] = whole[:, columns(c)]
            wind = spread(lines.at[0, kind], c)
            winds[2 * kind, c] = jnp.abs(wind)
            winds[2 * kind + 1, c] = wind
    loads[4].wait()
    copy_state.wait()

    def lay_out(slot, carry):
        whole = permute(
            jnp.concatenate(
                [state[slot].reshape(fields * rows, width), halo[slot].reshape(fields * 16, width)],
                axis=0,
            ),
            spread_columns[...],
        )
        own = whole[: fields * rows].reshape(fields, rows, width)
        far = whole[fields * rows :].reshape(fields, 16, width)
        far = jnp.where(band == 0, far[:, :8], far[:, 8:])
        for c in range(across):
            lines[slot, :, c, :rows] = own[:, :, columns(c)]
            lines[slot, :, c, rows:] = jnp.where(keep[:, columns(c)], far[:, :, columns(c)], 0.0)
        return carry

    lax.fori_loop(0, slots, lay_out, 0)

    def step(x):
        west = [pltpu.roll(x[across - 1], 1, 2)] + x[:-1]
        east = x[1:] + [pltpu.roll(x[0], TILE_COLS - 1, 2)]
        south = [
            jnp.concatenate([pltpu.roll(v[layers - 1 :], 1, 1), v[: layers - 1]], axis=0) for v in x
        ]
        north = [jnp.concatenate([v[1:], pltpu.roll(v[:1], 7, 1)], axis=0) for v in x]
        return [
            x[c]
            - winds[0, c] * (x[c] - jnp.where(winds[1, c] > 0.0, west[c], east[c]))
            - winds[2, c] * (x[c] - jnp.where(winds[3, c] > 0.0, south[c], north[c]))
            for c in range(across)
        ]

    def move(index, carry):
        kind = index // (slots // TOGETHER)
        first = TOGETHER * lax.rem(index, slots // TOGETHER)
        fields_of = [lines.at[first + k, kind] for k in range(TOGETHER)]
        xs = [[spread(field, c) for c in range(across)] for field in fields_of]
        for _ in range(STEPS):
            xs = [step(x) for x in xs]
        for k, (field, x) in enumerate(zip(fields_of, xs)):
            for c in range(across):
                for layer in range(layers):
                    field[c, pl.ds(layer, 8, stride=layers), :] = x[c][layer]
                moved[kind, first + k, :, columns(c)] = field[c, :rows].astype(jnp.bfloat16)
        return carry

    def collect(first, last):
        whole = moved[first:last].reshape((last - first) * slots * rows, width)
        whole = permute(whole, gather_columns[...]).astype(jnp.bfloat16)
        advected[first:last] = whole.reshape(last - first, slots, rows, width)

    total = fields * (slots // TOGETHER)
    early = total // 8
    lax.fori_loop(0, slots // TOGETHER, move, 0)
    collect(0, 1)
    lax.fori_loop(slots // TOGETHER, early, move, 0)

    def arrive(d, carry):
        source = near_by(d)
        pltpu.make_async_remote_copy(
            src_ref=obs_send.at[0],
            dst_ref=obs_recv.at[source],
            send_sem=obs_sems.at[0],
            recv_sem=obs_arrived.at[source],
            device_id={"mem": first_rank + source},
            device_id_type=MESH,
        ).wait_recv()
        return carry

    lax.fori_loop(1, SHARERS, arrive, 0)
    obs_recv[rank] = obs_send[rank]
    grids[rank] = functools.reduce(jnp.add, [obs_recv[k] for k in range(SHARERS)])
    for d in range(1, SHARERS):
        grid_out(d).start()

    lax.fori_loop(early, total, move, 0)

    collect(1, fields)

    def likely(index, carry):
        source = lax.rem(index + (1 - band) * (SHARERS // 2), SHARERS)

        @pl.when(source != rank)
        def _():
            pltpu.make_async_remote_copy(
                src_ref=grids.at[source],
                dst_ref=grids.at[source],
                send_sem=grid_sems.at[0],
                recv_sem=grid_arrived.at[source],
                device_id={"mem": first_rank + source},
                device_id_type=MESH,
            ).wait_recv()

        for k in range(held_tiles):
            down, along = tile(held_tiles * source + k)
            inverse, linear, constant = (grids[source, k, term] for term in range(3))
            for slot in range(slots):
                value = advected[0, slot, down, along].astype(jnp.float32)
                loglik[slot, down, along] = -0.5 * (
                    inverse * value * value - 2.0 * linear * value + constant
                )
        return carry

    lax.fori_loop(0, SHARERS // 2, likely, 0)
    copy_loglik = to_other(loglik.at[:, edge16, :], loglik_halo, 2)
    lax.fori_loop(SHARERS // 2, SHARERS, likely, 0)

    r0 = lax.broadcasted_iota(jnp.int32, (rows, rows), 0)
    r1 = lax.broadcasted_iota(jnp.int32, (rows, rows), 1)
    own_band = kernel_values(r0 - r1)
    h0 = lax.broadcasted_iota(jnp.int32, (rows, 16), 0)
    h1 = lax.broadcasted_iota(jnp.int32, (rows, 16), 1)
    far_band = kernel_values(jnp.where(band == 0, rows + h1 - h0, h0 + 16 - h1))
    dot = functools.partial(
        jnp.dot, precision=lax.Precision.HIGHEST, preferred_element_type=jnp.float32
    )
    own_part = [dot(own_band, loglik[slot]) for slot in range(slots)]
    copy_loglik.wait()
    smoothed = jnp.concatenate(
        [own_part[slot] + dot(far_band, loglik_halo[slot]) for slot in range(slots)], axis=0
    )
    scores[...] = dot(smoothed, lon_kernel[...]).reshape(slots, rows, width)

    partner = me + 1 - 2 * lax.rem(me, 2)
    parity = lax.rem(me, 2)

    half = n // 2

    def copies(t, slot, target):
        return [
            pltpu.make_async_remote_copy(
                src_ref=source.at[t],
                dst_ref=landing.at[slot],
                send_sem=sent_sems.at[t],
                recv_sem=landed_sems.at[slot],
                device_id={"mem": target},
                device_id_type=MESH,
            )
            for source, landing, sent_sems, landed_sems in (
                (send_log, recv_log, send_log_sems, recv_log_sems),
                (send, recv, send_sems, recv_sems),
            )
        ]

    def outgoing(t):
        return copies(t, me // 2, t)

    def across_pair(t):
        return copies(t, half + t // 2, partner)

    def start_all(made):
        for copy in made:
            copy.start()

    def gather(t):
        down, along = tile(t)
        live = [
            jnp.where(slot < count[0], scores[slot, down, along], -jnp.inf)
            for slot in range(slots)
        ]
        peak = functools.reduce(jnp.maximum, live)
        gains = [jnp.exp(score - peak) for score in live]
        weighted = [
            functools.reduce(
                jnp.add,
                [
                    gains[slot] * advected[kind, slot, down, along].astype(jnp.float32)
                    for slot in range(slots)
                ],
            )
            for kind in range(fields)
        ]
        return weighted, functools.reduce(jnp.add, gains), peak

    def put(t, weighted, total, peak):
        send_log[t] = peak + jnp.log(total)
        inverse = 1.0 / total
        for plane, value in enumerate(encode([value * inverse for value in weighted])):
            send[t, plane] = value

    def hold(t, weighted, total, peak):
        for plane, value in enumerate(weighted + [total, peak]):
            held[t // 2, plane] = value

    middle = owners // 2
    place = lax.rem(me // 2, middle)

    def near_to_far(k):
        ups, downs = middle - 1 - place, place
        both = jnp.minimum(ups, downs)
        upward = jnp.where(ups > downs, k - both, 0 - (k - both))
        paired = jnp.where(lax.rem(k, 2) == 1, (k + 1) // 2, 0 - (k // 2))
        return lax.rem(jnp.where(k <= 2 * both, paired, upward) + middle, middle)

    def turn(j):
        return 2 * near_to_far(middle - 1 - j)

    def give_pair(j, carry):
        t = lax.rem(partner + turn(j), owners)
        put(t, *gather(t))
        start_all(across_pair(t))
        return carry

    def keep_own(j, carry):
        t = 2 * j + parity
        hold(t, *gather(t))
        return carry

    def merge(t, slot):
        low, high = held[t // 2, fields + 1], recv_log[slot]
        peak = jnp.maximum(low, high)
        low, high = jnp.exp(low - peak), jnp.exp(high - peak)
        scaled = high * scale_of(recv[slot, fields])
        weighted = [
            low * held[t // 2, kind] + scaled * integer(recv[slot, kind])
            for kind in range(fields)
        ]
        return weighted, low * held[t // 2, fields] + high, peak

    def give_owner(j, carry):
        t = lax.rem(me + turn(j), owners)
        for copy in across_pair(t):
            copy.wait_recv()
        sums = merge(t, half + t // 2)

        @pl.when(t != me)
        def _():
            put(t, *sums)
            start_all(outgoing(t))

        @pl.when(t == me)
        def _():
            hold(t, *sums)

        return carry

    lax.fori_loop(0, owners // 2, give_pair, 0)
    lax.fori_loop(0, owners // 2, keep_own, 0)
    lax.fori_loop(0, owners // 2, give_owner, 0)

    def back(d):
        return pltpu.make_async_remote_copy(
            src_ref=merged.at[me],
            dst_ref=merged.at[me],
            send_sem=back_send.at[d],
            recv_sem=back_recv.at[me],
            device_id={"mem": lax.rem(me + 2 * d, n)},
            device_id_type=MESH,
        )

    def relay(t):
        return pltpu.make_async_remote_copy(
            src_ref=merged.at[t],
            dst_ref=merged.at[t],
            send_sem=relay_send.at[t],
            recv_sem=back_recv.at[t],
            device_id={"mem": partner},
            device_id_type=MESH,
        )

    @pl.when(me < owners)
    def _():
        def arrive(d, carry):
            source = lax.rem(me + 2 * d, n)
            for copy in copies(0, source // 2, source):
                copy.wait_recv()
            return carry

        lax.fori_loop(1, half, arrive, 0)
        own = me // 2
        peak = lax.fori_loop(
            1,
            half,
            lambda d, top: jnp.maximum(top, recv_log[lax.rem(own + d, half)]),
            held[own, fields + 1],
        )

        def add(d, sums):
            slot = lax.rem(own + d, half)
            factor = jnp.exp(recv_log[slot] - peak)
            scaled = factor * scale_of(recv[slot, fields])
            return tuple(
                sums[kind] + scaled * integer(recv[slot, kind]) for kind in range(fields)
            ) + (sums[fields] + factor,)

        factor = jnp.exp(held[own, fields + 1] - peak)
        sums = lax.fori_loop(
            1, half, add, tuple(factor * held[own, plane] for plane in range(fields + 1))
        )
        inverse = 1.0 / sums[fields]
        for plane, value in enumerate(encode([sums[kind] * inverse for kind in range(fields)])):
            merged[me, plane] = value

        def start(d, carry):
            back(d).start()
            return carry

        lax.fori_loop(1, half, start, 0)

    def landed(t):
        @pl.when(t != me)
        def _():
            relay(t).wait_recv()

    def place_of(start, k):
        return lax.rem(start + 2 * near_to_far(k), owners)

    def pass_on(k, carry):
        t = place_of(me, k)
        landed(t)
        relay(t).start()
        return carry

    def finish_passed(k, carry):
        finish(place_of(me, k))
        return carry

    def accept(k, carry):
        t = place_of(partner, k)
        landed(t)
        finish(t)
        return carry

    def finish(t):
        down, along = tile(t)
        scale = scale_of(merged[t, fields])
        for kind in range(fields):
            mean = scale * integer(merged[t, kind])
            mean_ref[kind, down, along] = mean.astype(jnp.bfloat16)
            for slot in range(slots):
                value = advected[kind, slot, down, along].astype(jnp.float32)
                fresh = value + factors[kind] * (mean - value)
                out_ref[slot, kind, down, along] = jnp.where(
                    slot < count[0], fresh, 0.0
                ).astype(jnp.bfloat16)

    for d in range(1, SHARERS):
        obs_out(d).wait_send()
        grid_out(d).wait_send()

    def passed(j, carry):
        for copy in across_pair(2 * j + 1 - parity):
            copy.wait_send()

        @pl.when(2 * j + parity != me)
        def _():
            for copy in outgoing(2 * j + parity):
                copy.wait_send()

        return carry

    lax.fori_loop(0, owners // 2, passed, 0)
    pass_on(0, 0)
    finish(place_of(me, 0))
    lax.fori_loop(1, middle, pass_on, 0)
    lax.fori_loop(1, middle, finish_passed, 0)
    lax.fori_loop(0, middle, accept, 0)

    def relayed(j, carry):
        relay(2 * j + parity).wait_send()
        return carry

    lax.fori_loop(0, middle, relayed, 0)

    @pl.when(me < owners)
    def _():
        def sent_back(d, carry):
            back(d).wait_send()
            return carry

        lax.fori_loop(1, n // 2, sent_back, 0)


def cycle(n, state, counts, east_wind, north_wind, obs, relax):
    slots, fields, rows, width = state.shape
    across = width // TILE_COLS
    owners = (rows // TILE_ROWS) * across
    share = obs[0].shape[1] // SHARERS
    held_tiles = owners // SHARERS
    tile = (TILE_ROWS, TILE_COLS)
    hbm = pl.BlockSpec(memory_space=pl.ANY)
    vmem = pl.BlockSpec(memory_space=pltpu.VMEM)
    f32, bf16 = jnp.float32, jnp.bfloat16
    return pl.pallas_call(
        functools.partial(cycle_kernel, n),
        out_shape=(
            pltpu.VMEM(state.shape, bf16),
            pltpu.VMEM((fields, rows, width), bf16),
        ),
        in_specs=[hbm] * 9,
        out_specs=(vmem, vmem),
        scratch_shapes=[
            pltpu.VMEM((1, share), jnp.int32),
            pltpu.VMEM((1, share), jnp.int32),
            pltpu.VMEM((1, share), f32),
            pltpu.VMEM((1, share), f32),
            pltpu.VMEM(state.shape, bf16),
            pltpu.SMEM(counts.shape, counts.dtype),
            pltpu.SMEM(relax.shape, relax.dtype),
            pltpu.VMEM((3, rows, width), f32),
            pltpu.VMEM((SHARERS, held_tiles, 3) + tile, f32),
            pltpu.VMEM((SHARERS, held_tiles, 3) + tile, f32),
            pltpu.VMEM((SHARERS, held_tiles, 3) + tile, f32),
            pltpu.VMEM((slots, fields, 16, width), bf16),
            pltpu.VMEM((2, rows, width), f32),
            pltpu.VMEM((2, 8, width), f32),
            pltpu.VMEM((4, across, (rows + 8) // 8, 8, TILE_COLS), f32),
            pltpu.VMEM((width, width), bf16),
            pltpu.VMEM((width, width), bf16),
            pltpu.VMEM((slots, fields, across, rows + 8, TILE_COLS), f32),
            pltpu.VMEM((fields, slots, rows, width), bf16),
            pltpu.VMEM((fields, slots, rows, width), bf16),
            pltpu.VMEM((width, width), f32),
            pltpu.VMEM((slots, rows, width), f32),
            pltpu.VMEM((slots, 16, width), f32),
            pltpu.VMEM((slots, rows, width), f32),
            pltpu.VMEM((owners // 2, fields + 2) + tile, f32),
            pltpu.VMEM((owners, fields + 1) + tile, jnp.int16),
            pltpu.VMEM((owners,) + tile, f32),
            pltpu.VMEM((n // 2 + owners // 2, fields + 1) + tile, jnp.int16),
            pltpu.VMEM((n // 2 + owners // 2,) + tile, f32),
            pltpu.VMEM((owners, fields + 1) + tile, jnp.int16),
            pltpu.SemaphoreType.DMA((2, 3)),
            pltpu.SemaphoreType.DMA((owners,)),
            pltpu.SemaphoreType.DMA((n // 2 + owners // 2,)),
            pltpu.SemaphoreType.DMA((owners,)),
            pltpu.SemaphoreType.DMA((n // 2 + owners // 2,)),
            pltpu.SemaphoreType.DMA((n,)),
            pltpu.SemaphoreType.DMA((owners,)),
            pltpu.SemaphoreType.DMA((owners,)),
            pltpu.SemaphoreType.DMA((9,)),
            pltpu.SemaphoreType.DMA((SHARERS,)),
            pltpu.SemaphoreType.DMA((SHARERS,)),
            pltpu.SemaphoreType.DMA((SHARERS,)),
            pltpu.SemaphoreType.DMA((SHARERS,)),
        ],
        compiler_params=pltpu.CompilerParams(
            collective_id=0, has_side_effects=True, vmem_limit_bytes=56 * 1024 * 1024
        ),
    )(state, counts, east_wind, north_wind, *obs, relax)


def write_kernel(fresh, mean, out, mean_out, sems):
    copies = [
        pltpu.make_async_copy(fresh, out, sems.at[0]),
        pltpu.make_async_copy(mean, mean_out, sems.at[1]),
    ]
    for copy in copies:
        copy.start()
    for copy in copies:
        copy.wait()


def write_out(fresh, mean):
    hbm = pl.BlockSpec(memory_space=pl.ANY)
    return pl.pallas_call(
        write_kernel,
        out_shape=(
            jax.ShapeDtypeStruct(fresh.shape, fresh.dtype),
            jax.ShapeDtypeStruct(mean.shape, mean.dtype),
        ),
        in_specs=[hbm, hbm],
        out_specs=(hbm, hbm),
        scratch_shapes=[pltpu.SemaphoreType.DMA((2,))],
    )(*(pltpu.with_memory_space_constraint(x, pltpu.VMEM) for x in (fresh, mean)))


def on_device(
    n, state, counts, east_wind, north_wind, obs_cells, obs_mask, obs_values, obs_error, relax
):
    obs = (obs_cells, obs_mask, obs_values, obs_error)
    fresh, mean = cycle(n, state, counts, east_wind, north_wind, obs, relax)
    return write_out(fresh, mean)


def solution(mesh):
    return jax.shard_map(
        functools.partial(on_device, mesh.shape["mem"]),
        mesh=mesh,
        in_specs=(
            P(("groups", "mem"), None, "lat", None),
            P(("groups", "mem")),
            P(("groups", "lat"), None),
            P(("groups", "lat"), None),
            P(("groups", "lat"), None),
            P(("groups", "lat"), None),
            P(("groups", "lat"), None),
            P(("groups", "lat"), None),
            P(),
        ),
        out_specs=(P(("groups", "mem"), None, "lat", None), P("groups", "lat", None)),
        check_vma=False,
    )
```
